256 devices in a mesh: rows: 32 (over y, z), cols: 8 (over x, core).
Axes of the slice: x: 4, y: 4, z: 8, core: 2. Of those that a mesh axis runs over, the one named last changes fastest.
Arguments:
- features: bfloat16 [4, 256, 1280, 128], P(None, 'rows', 'cols'), may hold values from -60 to 60
- conv_first: bfloat16 [3, 3, 3, 128, 128], replicated, may hold values from -0.109375 to 0.109375
- first_reduce_kernel: bfloat16 [3, 3, 128, 256], replicated, may hold values from -0.1875 to 0.1875
- conv_second: bfloat16 [3, 3, 3, 256, 256], replicated, may hold values from -0.078125 to 0.078125
- second_reduce_kernel: bfloat16 [3, 3, 256, 512], replicated, may hold values from -0.125 to 0.125
- conv_last: bfloat16 [3, 3, 3, 512, 32], replicated, may hold values from -0.0546875 to 0.0546875
- gain_first: float32 [128], replicated, may hold values from 0.5 to 1.5
- shift_first: float32 [128], replicated, may hold values from -0.5 to 0.5
- gain_second: float32 [256], replicated, may hold values from 0.5 to 1.5
- shift_second: float32 [256], replicated, may hold values from -0.5 to 0.5
- gain_third: float32 [512], replicated, may hold values from 0.5 to 1.5
- shift_third: float32 [512], replicated, may hold values from -0.5 to 0.5
Outputs:
- moments: bfloat16 [4, 64, 320, 32], P(None, 'rows', 'cols')
The draws below stay inside these ranges and needn't reach their ends.
All inputs are finite; a program needn't handle non-finite values.
Results may differ from the reference program's by a relative error of at most 0.01.
Values may be sent and summed in bfloat16 or wider, within the bound.
No kernel may reach another device: no remote copies, remote signals or barrier semaphores. Data moves between devices by JAX's collectives and lax.ppermute only.
A program may use at most 64 MiB of HBM per device.

```python
import jax
import jax.numpy as jnp
from jax import lax

C1 = 128
C2 = 256
C3 = 512
LATENT = 16
GROUPS = 32
FRAMES = 4
HEIGHT = 256
WIDTH = 1280


def draw_features(key, part):
    key_base = jax.random.fold_in(key, 11)
    key_cols = jax.random.fold_in(key, 12)
    extent = (FRAMES, HEIGHT, WIDTH, C1)
    row_pos = jnp.arange(HEIGHT, dtype=jnp.float32)
    row_scale = 10.0 ** (row_pos / HEIGHT - 0.5)
    col_scale = 10.0 ** (jax.random.uniform(key_cols, (WIDTH,), jnp.float32) - 0.5)
    base = jax.random.truncated_normal(key_base, -6.0, 6.0, extent, jnp.float32)
    return (base * row_scale[None, :, None, None] * col_scale[None, None, :, None]).astype(jnp.bfloat16)


def gaussian(stream_key, shape, deviation, bound, held_as=jnp.bfloat16):
    return jnp.clip(deviation * jax.random.normal(stream_key, shape, jnp.float32), -bound, bound).astype(held_as)


def setup_inputs(seed: int = 0) -> dict:
    arg_keys = jax.random.split(jax.random.key(seed), 13)
    features = draw_features(jax.random.fold_in(arg_keys[12], 71), 0)
    conv_first = gaussian(arg_keys[1], (3, 3, 3, C1, C1), (27 * C1) ** -0.5, 0.109375)
    first_reduce_kernel = gaussian(arg_keys[2], (3, 3, C1, C2), (9 * C1) ** -0.5, 0.1875)
    conv_second = gaussian(arg_keys[3], (3, 3, 3, C2, C2), (27 * C2) ** -0.5, 0.078125)
    second_reduce_kernel = gaussian(arg_keys[4], (3, 3, C2, C3), (9 * C2) ** -0.5, 0.125)
    conv_last = gaussian(arg_keys[5], (3, 3, 3, C3, 2 * LATENT), (27 * C3) ** -0.5, 0.0546875)
    gain_first = jnp.clip(1.0 + 0.1 * jax.random.normal(arg_keys[6], (C1,), jnp.float32), 0.5, 1.5)
    shift_first = jnp.clip(jax.random.uniform(arg_keys[7], (C1,), jnp.float32, -0.5, 0.5), -0.5, 0.5)
    gain_second = jnp.clip(1.0 + 0.1 * jax.random.normal(arg_keys[8], (C2,), jnp.float32), 0.5, 1.5)
    shift_second = jnp.clip(jax.random.uniform(arg_keys[9], (C2,), jnp.float32, -0.5, 0.5), -0.5, 0.5)
    gain_third = jnp.clip(1.0 + 0.1 * jax.random.normal(arg_keys[10], (C3,), jnp.float32), 0.5, 1.5)
    shift_third = jnp.clip(jax.random.uniform(arg_keys[11], (C3,), jnp.float32, -0.5, 0.5), -0.5, 0.5)
    return {"features": features, "conv_first": conv_first, "first_reduce_kernel": first_reduce_kernel, "conv_second": conv_second, "second_reduce_kernel": second_reduce_kernel, "conv_last": conv_last, "gain_first": gain_first, "shift_first": shift_first, "gain_second": gain_second, "shift_second": shift_second, "gain_third": gain_third, "shift_third": shift_third}


epsilon = 1e-06

def convolve(input_video, weight_tables, strides):
    return lax.conv_general_dilated(input_video[None], weight_tables, strides, 'VALID', dimension_numbers=('NDHWC', 'DHWIO', 'NDHWC'), preferred_element_type=jnp.float32)[0]

def causal_conv(input_video, weight_tables):
    padding = jnp.pad(input_video, ((0, 0), (1, 1), (1, 1), (0, 0)))
    widened = jnp.concatenate([padding[:1], padding[:1], padding], axis=0)
    return convolve(widened, weight_tables, (1, 1, 1))

def norm_silu(values, norm_gain, norm_shift):
    extent = values.shape
    grouped = values.reshape(extent[:3] + (GROUPS, extent[3] // GROUPS))
    mean_value = lax.optimization_barrier(jnp.mean(grouped, axis=(0, 1, 2, 4), keepdims=True))
    variance = lax.optimization_barrier(jnp.mean(jnp.square(grouped - mean_value), axis=(0, 1, 2, 4), keepdims=True))
    result = ((grouped - mean_value) / jnp.sqrt(variance + epsilon)).reshape(extent) * norm_gain + norm_shift
    return jax.nn.silu(result).astype(jnp.bfloat16)

def reduce_resolution(input_video, weight_tables):
    padding = jnp.pad(input_video, ((0, 0), (0, 1), (0, 1), (0, 0)))
    return convolve(padding, weight_tables[None], (1, 2, 2)).astype(jnp.bfloat16)

def reference(features, conv_first, first_reduce_kernel, conv_second, second_reduce_kernel, conv_last, gain_first, shift_first, gain_second, shift_second, gain_third, shift_third):
    hidden_one = causal_conv(features, conv_first)
    first_activation_map = norm_silu(hidden_one, gain_first, shift_first)
    middle_level_features = reduce_resolution(first_activation_map, first_reduce_kernel)
    hidden_two = causal_conv(middle_level_features, conv_second)
    second_activation_map = norm_silu(hidden_two, gain_second, shift_second)
    coarsest_level_features = reduce_resolution(second_activation_map, second_reduce_kernel)
    active_three = norm_silu(coarsest_level_features.astype(jnp.float32), gain_third, shift_third)
    return causal_conv(active_three, conv_last).astype(jnp.bfloat16)
```

```python
import functools

import jax
import jax.numpy as jnp
from jax import lax
from jax.experimental import pallas as pl
from jax.experimental.pallas import tpu as pltpu
from jax.sharding import PartitionSpec as P

GROUPS = 32
EPSILON = 1e-6
FRAMES = 4
ROWS = 8
COLS = 160
C1, C2, C3, OUT = 128, 256, 512, 32
Q = 48
PAD = 2
OWN = COLS // 4
LEFT, RIGHT = 8, 16
LINE = 208
AXES = ("rows", "cols")
F32, BF16 = jnp.float32, jnp.bfloat16
VMEM = pl.BlockSpec(memory_space=pltpu.VMEM)
SMEM = pl.BlockSpec(memory_space=pltpu.SMEM)
ANY = pl.BlockSpec(memory_space=pl.ANY)


def params(mib):
    return pltpu.CompilerParams(vmem_limit_bytes=mib * 1024 * 1024)


def cost(flops, read):
    return pl.CostEstimate(flops=int(flops), bytes_accessed=int(read), transcendentals=0)


def shape(dims, dtype):
    return jax.ShapeDtypeStruct(dims, dtype)


def mm(left, right):
    return jnp.dot(left, right, preferred_element_type=F32)


def exact(left, right):
    return jnp.dot(left, right, preferred_element_type=F32, precision=lax.Precision.HIGHEST)


def weights_kernel(first, second, last, one, two, three):
    zero = jnp.zeros((C1, C1), BF16)
    for b in range(3):
        for e in range(3):
            taps = [first[((a * 3 + b) * 3 + e) * C1 : ((a * 3 + b) * 3 + e + 1) * C1, :] for a in range(3)]
            wide = [k.astype(F32) for k in taps]
            pair = wide[0] + wide[1]
            for s, k in enumerate(taps + [pair.astype(BF16), (pair + wide[2]).astype(BF16)]):
                base = s * 12 * C1 + b * 4 * C1
                one[base + e * C1 : base + (e + 1) * C1, 0:C1] = k
                one[base + (e + 1) * C1 : base + (e + 2) * C1, C1 : 2 * C1] = k
        for s in range(5):
            base = s * 12 * C1 + b * 4 * C1
            one[base + 3 * C1 : base + 4 * C1, 0:C1] = zero
            one[base : base + C1, C1 : 2 * C1] = zero

    def add(i, carry):
        at = pl.ds(pl.multiple_of(i * C2, C2), C2)
        pair = second[0, at, :].astype(F32) + second[1, at, :].astype(F32)
        two[0, at, :] = pair.astype(BF16)
        two[1, at, :] = (pair + second[2, at, :].astype(F32)).astype(BF16)
        return carry

    lax.fori_loop(0, 9, add, 0)

    def pack(i, carry):
        at = pl.ds(pl.multiple_of(i * C3, C3), C3)
        zeros = jnp.zeros((C3, OUT), BF16)
        three[at, :] = jnp.concatenate([last[0, at, :], last[1, at, :], last[2, at, :], zeros], axis=1)
        return carry

    lax.fori_loop(0, 9, pack, 0)


def weights(first, second, last):
    return pl.pallas_call(
        weights_kernel,
        out_shape=(
            shape((5 * 12 * C1, 2 * C1), BF16),
            shape((2, 9 * C2, C2), BF16),
            shape((9 * C3, 4 * OUT), BF16),
        ),
        in_specs=[VMEM] * 3,
        out_specs=(VMEM,) * 3,
        compiler_params=params(40),
        cost_estimate=cost(0, 12e6),
        name="weights",
    )(first.reshape(27 * C1, C1), second.reshape(3, 9 * C2, C2), last.reshape(3, 9 * C3, OUT))


def planes_kernel(left, own, right, planes, top, bottom, line):
    def step(i, carry):
        line[i, 0:8, :] = jnp.zeros((8, C1), F32)
        line[i, 8:16, :] = left[i].astype(F32)
        line[i, 16 : 16 + COLS, :] = own[i].astype(F32)
        line[i, 16 + COLS : 32 + COLS, :] = right[i].astype(F32)
        line[i, 32 + COLS : LINE, :] = jnp.zeros((LINE - 32 - COLS, C1), F32)
        for k in range(6):
            planes[i, :, k * C1 : (k + 1) * C1] = line[i, pl.ds(7 + k, Q, stride=4), :].astype(BF16)
        return carry

    lax.fori_loop(0, FRAMES * ROWS, step, 0)
    for t in range(FRAMES):
        top[t] = planes[t * ROWS, :, C1 : 5 * C1]
        bottom[t] = planes[t * ROWS + ROWS - 1, :, C1 : 5 * C1]


def planes_of(left, own, right):
    lines = FRAMES * ROWS
    return pl.pallas_call(
        planes_kernel,
        out_shape=(
            shape((lines, Q, 6 * C1), BF16),
            shape((FRAMES, Q, 4 * C1), BF16),
            shape((FRAMES, Q, 4 * C1), BF16),
        ),
        in_specs=[VMEM] * 3,
        out_specs=(VMEM,) * 3,
        scratch_shapes=[pltpu.VMEM((lines, LINE, C1), F32)],
        compiler_params=params(24),
        cost_estimate=cost(0, 4e6),
        name="planes",
    )(
        left.reshape(lines, LEFT, C1),
        own.reshape(lines, COLS, C1),
        right.reshape(lines, RIGHT, C1),
    )


def own_entries(rows, lanes):
    at = lax.rem(lax.broadcasted_iota(jnp.int32, (rows, lanes), 0), Q)
    return (at >= PAD) & (at < PAD + OWN)


def sums(values, mask):
    kept = jnp.where(mask, values, 0.0)
    return jnp.sum(kept, axis=0, keepdims=True), jnp.sum(kept * kept, axis=0, keepdims=True)


def frames_conv(frame, weight, size, store):
    cat = lambda parts: jnp.concatenate(parts, axis=1)
    store(0, mm(frame(0), weight(4)))
    store(1, mm(frame(0), weight(3)) + mm(frame(1), weight(2)))
    for t in range(2, FRAMES):
        store(t, mm(frame(t - 2), weight(0)) + mm(frame(t - 1), weight(1)) + mm(frame(t), weight(2)))


def middle_kernel(planes, table, hidden, stats):
    count = ROWS - 2
    rows = count * Q
    mask = own_entries(2 * rows, 2 * C1)
    stats[...] = jnp.zeros(stats.shape, F32)

    def frame(t):
        parts = []
        for b in range(3):
            block = planes[t * ROWS + b : t * ROWS + b + count].reshape(rows, 6 * C1)
            parts.append(jnp.concatenate([block[:, : 4 * C1], block[:, 2 * C1 :]], axis=0))
        return jnp.concatenate(parts, axis=1)

    def store(t, value):
        hidden[t, :, 0:Q, :] = value[:rows].reshape(count, Q, 2 * C1)
        hidden[t, :, Q : 2 * Q, :] = value[rows:].reshape(count, Q, 2 * C1)
        one, two = sums(value, mask)
        stats[0:1, :] += one
        stats[1:2, :] += two

    def weight(s):
        return table[s * 12 * C1 : (s + 1) * 12 * C1, :]

    frames_conv(frame, weight, 0, store)


def middle(planes, table):
    return pl.pallas_call(
        middle_kernel,
        out_shape=(
            shape((FRAMES, ROWS - 2, 2 * Q, 2 * C1), F32),
            shape((8, 2 * C1), F32),
        ),
        in_specs=[VMEM] * 2,
        out_specs=(VMEM,) * 2,
        compiler_params=params(48),
        cost_estimate=cost(6e9, 10e6),
        name="middle",
    )(planes, table)


def group_matrix(channels, shift):
    per = channels // GROUPS
    c = lax.broadcasted_iota(jnp.int32, (channels, 128), 0)
    g = lax.broadcasted_iota(jnp.int32, (channels, 128), 1)
    low = (g - shift) * per
    return jnp.where((c >= low) & (c < low + per), 1.0, 0.0).astype(F32)


def spread_matrix(channels, shift):
    per = channels // GROUPS
    g = lax.broadcasted_iota(jnp.int32, (128, channels), 0)
    c = lax.broadcasted_iota(jnp.int32, (128, channels), 1)
    low = (g - shift) * per
    return jnp.where((c >= low) & (c < low + per), 1.0, 0.0).astype(F32)


def grouped(one, two):
    channels = one.shape[1]
    wide = lambda v: jnp.broadcast_to(v, (8, channels))
    row = exact(wide(one), group_matrix(channels, 0)) + exact(wide(two), group_matrix(channels, GROUPS))
    return row[0:1]


def norm_terms(gathered, gain, shift, members):
    channels = gain.shape[1]
    total = jnp.broadcast_to(jnp.sum(gathered[...], axis=0, keepdims=True), (8, 128))
    mean = exact(total, spread_matrix(channels, 0))[0:1] / members
    square = exact(total, spread_matrix(channels, GROUPS))[0:1] / members
    variance = jnp.maximum(square - mean * mean, 0.0)
    return mean, gain[...] / jnp.sqrt(variance + EPSILON), shift[...]


def edges_kernel(planes, above, below, table, inner, stats, hidden, share, up, down, halo):
    rows = 2 * Q
    lane = 4 * C1
    for t in range(FRAMES):
        for side, ref in enumerate((above, below)):
            whole = ref[t]
            first = pltpu.roll(whole[:, 3 * C1 :].astype(F32), 1, 0).astype(BF16)
            last = pltpu.roll(whole[:, :C1].astype(F32), Q - 1, 0).astype(BF16)
            halo[side, t, :, 0:C1] = first
            halo[side, t, :, C1 : 5 * C1] = whole
            halo[side, t, :, 5 * C1 :] = last

    def frame(t):
        at = t * ROWS
        lines = [
            [halo[0, t], planes[at], planes[at + 1]],
            [planes[at + ROWS - 2], planes[at + ROWS - 1], halo[1, t]],
        ]
        out = []
        for side in range(2):
            for low in (0, 2 * C1):
                out.append(jnp.concatenate([v[:, low : low + lane] for v in lines[side]], axis=1))
        return jnp.concatenate(out, axis=0)

    mask = own_entries(2 * rows, 2 * C1)
    total = [stats[0:1, :], stats[1:2, :]]

    def store(t, value):
        hidden[t, 0] = value[:rows]
        hidden[t, 1] = value[rows:]
        up[t, 0] = value[:rows].astype(BF16)
        down[t, 1] = value[rows:].astype(BF16)
        one, two = sums(value, mask)
        total[0] += one
        total[1] += two

    frames_conv(frame, lambda s: table[s * 12 * C1 : (s + 1) * 12 * C1, :], 0, store)
    for t in range(FRAMES):
        up[t, 1] = inner[t, 0].astype(BF16)
        up[t, 2] = inner[t, 1].astype(BF16)
        down[t, 0] = inner[t, ROWS - 3].astype(BF16)
    one, two = (v[:, :C1] + v[:, C1:] for v in total)
    share[...] = jnp.broadcast_to(grouped(one, two), share.shape)


def edges(planes, above, below, table, inner, stats, devices):
    return pl.pallas_call(
        edges_kernel,
        out_shape=(
            shape((FRAMES, 2, 2 * Q, 2 * C1), F32),
            shape((devices, 128), F32),
            shape((FRAMES, 3, 2 * Q, 2 * C1), BF16),
            shape((FRAMES, 2, 2 * Q, 2 * C1), BF16),
        ),
        in_specs=[VMEM] * 6,
        out_specs=(VMEM,) * 4,
        scratch_shapes=[pltpu.VMEM((2, FRAMES, Q, 6 * C1), BF16)],
        compiler_params=params(48),
        cost_estimate=cost(2e9, 10e6),
        name="edges",
    )(planes, above, below, table, inner, stats)


def silu(values):
    half = 0.5 * values
    return half + half * jnp.tanh(half)


def activate(values, terms):
    mean, scale, shift = terms
    return silu((values - mean) * scale + shift)


def twice(terms):
    return tuple(jnp.concatenate([v, v], axis=1) for v in terms)


def raised(values):
    return pltpu.roll(values, Q - 1, 0)


def lowered(values):
    return pltpu.roll(values, 1, 0)


def second_kernel(
    flags, inner, outer, above, below, gathered, gain, shift, reduce, second, sums2,
    hidden, share, up, down, act, lev, raw, kernels, sem, *, members,
):
    copies = [
        pltpu.make_async_copy(second, kernels.at[pl.ds(0, 3)], sem.at[0]),
        pltpu.make_async_copy(sums2, kernels.at[pl.ds(3, 2)], sem.at[1]),
    ]
    for c in copies:
        c.start()
    first_row, last_row, first_col, last_col = (flags[i] for i in range(4))
    terms = twice(norm_terms(gathered, gain, shift, members))
    entry = lax.broadcasted_iota(jnp.int32, (Q, 1), 0)
    right = jnp.where((entry >= PAD + OWN) & (last_col == 1), 0.0, 1.0)
    outside = jnp.where((entry < PAD) & (first_col == 1), 0.0, right)
    below_in = 1.0 - last_row.astype(F32)
    above_in = 1.0 - first_row.astype(F32)

    def line(t, k, value):
        keep = right * below_in if k >= 10 else right
        a = activate(value[:Q].astype(F32), terms) * keep
        b = activate(value[Q:].astype(F32), terms) * keep
        act[t, k, 0:Q, 0 : 2 * C1] = a.astype(BF16)
        act[t, k, 0:Q, 2 * C1 :] = b[:, :C1].astype(BF16)
        act[t, k, Q:, 0 : 2 * C1] = b.astype(BF16)
        act[t, k, Q:, 2 * C1 :] = raised(a[:, :C1]).astype(BF16)

    def lines(t, carry):
        line(t, 0, above[t, 0])
        line(t, 1, above[t, 1])
        line(t, 2, outer[t, 0])
        for r in range(ROWS - 2):
            line(t, 3 + r, inner[t, r])
        line(t, 9, outer[t, 1])
        for r in range(3):
            line(t, 10 + r, below[t, r])
        value = None
        for b in range(3):
            left = jnp.concatenate([act[t, 2 * i + b] for i in range(6)], axis=0)
            part = mm(left, reduce[b * 3 * C1 : (b + 1) * 3 * C1, :])
            value = part if value is None else value + part
        for i in range(6):
            keep = outside
            if i == 0:
                keep = keep * above_in
            if i == 5:
                keep = keep * below_in
            even = value[i * 2 * Q : i * 2 * Q + Q] * keep
            odd = value[i * 2 * Q + Q : (i + 1) * 2 * Q] * keep
            e, o = even.astype(BF16), odd.astype(BF16)
            lev[t, i, 0:Q, 0:C2] = lowered(odd).astype(BF16)
            lev[t, i, 0:Q, C2 : 2 * C2] = e
            lev[t, i, 0:Q, 2 * C2 :] = o
            lev[t, i, Q:, 0:C2] = e
            lev[t, i, Q:, C2 : 2 * C2] = o
            lev[t, i, Q:, 2 * C2 :] = raised(even).astype(BF16)
        return carry

    lax.fori_loop(0, FRAMES, lines, 0)
    for c in copies:
        c.wait()
    rows = 4 * 2 * Q
    mask = own_entries(rows, C2)
    total = [jnp.zeros((1, C2), F32), jnp.zeros((1, C2), F32)]

    def frame(t):
        return jnp.concatenate([lev[t, b : b + 4].reshape(rows, 3 * C2) for b in range(3)], axis=1)

    def store(t, value):
        full = value.reshape(4, 2 * Q, C2)
        hidden[t] = full
        up[t] = full[0:3].astype(BF16)
        down[t] = full[2:4].astype(BF16)
        one, two = sums(value, mask)
        total[0] += one
        total[1] += two

    frames_conv(frame, lambda s: kernels[s], 0, store)
    share[...] = jnp.broadcast_to(grouped(*total), share.shape)


def second_level(flags, inner, outer, above, below, gathered, gain, shift, reduce, second, sums2, devices):
    return pl.pallas_call(
        functools.partial(second_kernel, members=float(devices * FRAMES * ROWS * COLS * (C1 // GROUPS))),
        out_shape=(
            shape((FRAMES, 4, 2 * Q, C2), F32),
            shape((devices, 128), F32),
            shape((FRAMES, 3, 2 * Q, C2), BF16),
            shape((FRAMES, 2, 2 * Q, C2), BF16),
        ),
        in_specs=[SMEM] + [VMEM] * 8 + [ANY] * 2,
        out_specs=(VMEM,) * 4,
        scratch_shapes=[
            pltpu.VMEM((FRAMES, 14, 2 * Q, 3 * C1), BF16),
            pltpu.VMEM((FRAMES, 6, 2 * Q, 3 * C2), BF16),
            pltpu.VMEM((8, 128), F32),
            pltpu.VMEM((5, 9 * C2, C2), BF16),
            pltpu.SemaphoreType.DMA((2,)),
        ],
        compiler_params=params(48),
        cost_estimate=cost(6e9, 12e6),
        name="second",
    )(
        flags, inner, outer, above, below, gathered,
        gain.reshape(1, C1), shift.reshape(1, C1),
        reduce.reshape(9 * C1, C2), second.reshape(3, 9 * C2, C2), sums2,
    )


def third_kernel(flags, inner, above, below, gathered, gain, shift, reduce, level, share, act, *, members):
    last_row, last_col = flags[1], flags[3]
    terms = norm_terms(gathered, gain, shift, members)
    entry = lax.broadcasted_iota(jnp.int32, (Q, 1), 0)
    right = jnp.where((entry >= PAD + OWN) & (last_col == 1), 0.0, 1.0)
    below_in = 1.0 - last_row.astype(F32)

    def line(t, k, value):
        keep = right * below_in if k >= 6 else right
        even = activate(value[:Q].astype(F32), terms) * keep
        odd = activate(value[Q:].astype(F32), terms) * keep
        act[t, k, :, 0:C2] = even.astype(BF16)
        act[t, k, :, C2 : 2 * C2] = odd.astype(BF16)
        act[t, k, :, 2 * C2 :] = raised(even).astype(BF16)

    def lines(t, carry):
        for r in range(2):
            line(t, r, above[t, r])
        for r in range(4):
            line(t, 2 + r, inner[t, r])
        for r in range(3):
            line(t, 6 + r, below[t, r])
        return carry

    lax.fori_loop(0, FRAMES, lines, 0)
    mask = own_entries(2 * Q, C3)
    total = [jnp.zeros((1, C3), F32), jnp.zeros((1, C3), F32)]
    value = None
    for b in range(3):
        left = jnp.concatenate([act[t, 2 * i + b] for t in range(FRAMES) for i in range(4)], axis=0)
        part = mm(left, reduce[b * 3 * C2 : (b + 1) * 3 * C2, :])
        value = part if value is None else value + part
    rounded = value.astype(BF16)
    level[...] = rounded.reshape(FRAMES, 4, Q, C3)
    wide = rounded.astype(F32)
    for t in range(FRAMES):
        one, two = sums(wide[(4 * t + 1) * Q : (4 * t + 3) * Q], mask)
        total[0] += one
        total[1] += two
    share[...] = jnp.broadcast_to(grouped(*total), share.shape)


def third_level(flags, inner, above, below, gathered, gain, shift, reduce, devices):
    return pl.pallas_call(
        functools.partial(third_kernel, members=float(devices * FRAMES * 4 * 2 * OWN * (C2 // GROUPS))),
        out_shape=(shape((FRAMES, 4, Q, C3), BF16), shape((devices, 128), F32)),
        in_specs=[SMEM] + [VMEM] * 7,
        out_specs=(VMEM,) * 2,
        scratch_shapes=[pltpu.VMEM((FRAMES, 10, Q, 3 * C2), BF16)],
        compiler_params=params(40),
        cost_estimate=cost(2e9, 8e6),
        name="third",
    )(flags, inner, above, below, gathered, gain.reshape(1, C2), shift.reshape(1, C2), reduce.reshape(9 * C2, C3))


def last_kernel(flags, level, gathered, gain, shift, table, result, act, *, members):
    first_row, last_row, first_col, last_col = (flags[i] for i in range(4))
    terms = norm_terms(gathered, gain, shift, members)
    entry = lax.broadcasted_iota(jnp.int32, (Q, 1), 0)
    keep_col = jnp.where((entry >= PAD + OWN) & (last_col == 1), 0.0, 1.0)
    keep_col = jnp.where((entry < PAD) & (first_col == 1), 0.0, keep_col)
    below_in = 1.0 - last_row.astype(F32)
    above_in = 1.0 - first_row.astype(F32)
    for t in range(FRAMES):
        for i in range(4):
            keep = keep_col
            if i == 0:
                keep = keep * above_in
            if i == 3:
                keep = keep * below_in
            v = activate(level[t, i].astype(F32), terms) * keep
            act[t, i, :, 0:C3] = lowered(v).astype(BF16)
            act[t, i, :, C3 : 2 * C3] = v.astype(BF16)
            act[t, i, :, 2 * C3 :] = raised(v).astype(BF16)
    value = None
    for b in range(3):
        left = jnp.concatenate([act[t, i + b] for t in range(FRAMES) for i in range(2)], axis=0)
        part = mm(left, table[b * 3 * C3 : (b + 1) * 3 * C3, :])
        value = part if value is None else value + part
    tap = lambda t, a: value[2 * Q * max(t, 0) : 2 * Q * (max(t, 0) + 1), a * OUT : (a + 1) * OUT]
    for t in range(FRAMES):
        out = tap(t - 2, 0) + tap(t - 1, 1) + tap(t, 2)
        for i in range(2):
            result[t, i] = out[i * Q + PAD : i * Q + PAD + OWN].astype(BF16)


def last_level(flags, level, gathered, gain, shift, table, devices):
    return pl.pallas_call(
        functools.partial(last_kernel, members=float(devices * FRAMES * 2 * OWN * (C3 // GROUPS))),
        out_shape=shape((FRAMES, 2, OWN, OUT), BF16),
        in_specs=[SMEM] + [VMEM] * 5,
        out_specs=VMEM,
        scratch_shapes=[pltpu.VMEM((FRAMES, 4, Q, 3 * C3), BF16)],
        compiler_params=params(32),
        cost_estimate=cost(1e9, 4e6),
        name="last",
    )(flags, level, gathered, gain.reshape(1, C3), shift.reshape(1, C3), table)


def forward(axis):
    return [(i, i + 1) for i in range(lax.axis_size(axis) - 1)]


def backward(axis):
    return [(i + 1, i) for i in range(lax.axis_size(axis) - 1)]


def from_both(last, first, axis):
    return lax.ppermute(last, axis, forward(axis)), lax.ppermute(first, axis, backward(axis))


def everywhere(share):
    return lax.all_to_all(share, AXES, 0, 0, tiled=True)


def shards(
    features, conv_first, first_reduce_kernel, conv_second, second_reduce_kernel, conv_last,
    gain_first, shift_first, gain_second, shift_second, gain_third, shift_third,
):
    rows, cols = lax.axis_size("rows"), lax.axis_size("cols")
    devices = rows * cols
    row, col = lax.axis_index("rows"), lax.axis_index("cols")
    flags = jnp.stack([row == 0, row == rows - 1, col == 0, col == cols - 1]).astype(jnp.int32)

    left, right = from_both(features[:, :, COLS - LEFT :], features[:, :, :RIGHT], "cols")
    table_one, table_two, table_three = weights(conv_first, conv_second, conv_last)
    planes, top, bottom = planes_of(left, features, right)
    above, below = from_both(bottom, top, "rows")
    inner, stats = middle(planes, table_one)
    outer, share, up, down = edges(planes, above, below, table_one, inner, stats, devices)
    above, below = from_both(down, up, "rows")
    hidden, share, up, down = second_level(
        flags, inner, outer, above, below, everywhere(share), gain_first, shift_first,
        first_reduce_kernel, conv_second, table_two, devices,
    )
    above, below = from_both(down, up, "rows")
    level, share = third_level(
        flags, hidden, above, below, everywhere(share), gain_second, shift_second,
        second_reduce_kernel, devices,
    )
    return last_level(flags, level, everywhere(share), gain_third, shift_third, table_three, devices)


def solution(mesh):
    return jax.shard_map(
        shards,
        mesh=mesh,
        in_specs=(P(None, "rows", "cols", None),) + (P(),) * 11,
        out_specs=P(None, "rows", "cols", None),
        check_vma=False,
    )
```

```python
import functools

import jax
import jax.numpy as jnp
from jax import lax
from jax.experimental import pallas as pl
from jax.experimental.pallas import tpu as pltpu
from jax.sharding import PartitionSpec as P

GROUPS = 32
EPSILON = 1e-6
FRAMES = 4
ROWS = 8
COLS = 160
C1, C2, C3, OUT = 128, 256, 512, 32
Q = 48
PAD = 2
OWN = COLS // 4
EDGE = 16
LINE = 208
AXES = ("rows", "cols")
F32, BF16 = jnp.float32, jnp.bfloat16
VMEM = pl.BlockSpec(memory_space=pltpu.VMEM)
HBM = pl.BlockSpec(memory_space=pltpu.HBM)


def params(mib):
    return pltpu.CompilerParams(vmem_limit_bytes=mib * 1024 * 1024)


def cost(flops, read):
    return pl.CostEstimate(flops=int(flops), bytes_accessed=int(read), transcendentals=0)


def shape(dims, dtype):
    return jax.ShapeDtypeStruct(dims, dtype)


def mm(left, right):
    return jnp.dot(left, right, preferred_element_type=F32)


def exact(left, right):
    return jnp.dot(left, right, preferred_element_type=F32, precision=lax.Precision.HIGHEST)


def weights_kernel(first, one):
    zero = jnp.zeros((C1, C1), BF16)
    for b in range(3):
        for e in range(3):
            taps = [first[((a * 3 + b) * 3 + e) * C1 : ((a * 3 + b) * 3 + e + 1) * C1, :] for a in range(3)]
            wide = [k.astype(F32) for k in taps]
            pair = wide[0] + wide[1]
            for s, k in enumerate(taps + [pair.astype(BF16), (pair + wide[2]).astype(BF16)]):
                base = s * 12 * C1 + b * 4 * C1
                one[base + e * C1 : base + (e + 1) * C1, 0:C1] = k
                one[base + (e + 1) * C1 : base + (e + 2) * C1, C1 : 2 * C1] = k
        for s in range(5):
            base = s * 12 * C1 + b * 4 * C1
            one[base + 3 * C1 : base + 4 * C1, 0:C1] = zero
            one[base : base + C1, C1 : 2 * C1] = zero


def weights(first):
    return pl.pallas_call(
        weights_kernel,
        out_shape=shape((5 * 12 * C1, 2 * C1), BF16),
        in_specs=[VMEM],
        out_specs=VMEM,
        compiler_params=params(8),
        cost_estimate=cost(0, 5e6),
        name="weights",
    )(first.reshape(27 * C1, C1))


def cut_kernel(features, last, first, sem):
    copies = [
        pltpu.make_async_copy(features.at[:, pl.ds(COLS - EDGE, EDGE)], last, sem.at[0]),
        pltpu.make_async_copy(features.at[:, pl.ds(0, EDGE)], first, sem.at[1]),
    ]
    for c in copies:
        c.start()
    for c in copies:
        c.wait()


def cut(features):
    edge = shape((FRAMES * ROWS, EDGE, C1), BF16)
    return pl.pallas_call(
        cut_kernel,
        out_shape=(edge, edge),
        in_specs=[HBM],
        out_specs=(VMEM,) * 2,
        scratch_shapes=[pltpu.SemaphoreType.DMA((2,))],
        compiler_params=params(4),
        cost_estimate=cost(0, 4e5),
        name="cut",
    )(features.reshape(FRAMES * ROWS, COLS, C1))


def planes_kernel(left, own, right, planes, top, bottom, line):
    for t in range(FRAMES):
        planes[t, 0] = jnp.zeros((Q, 6 * C1), BF16)
        planes[t, ROWS + 1] = jnp.zeros((Q, 6 * C1), BF16)

        def step(r, carry, t=t):
            i = t * ROWS + r
            line[i, 0:EDGE, :] = left[i].astype(F32)
            line[i, EDGE : EDGE + COLS, :] = own[i].astype(F32)
            line[i, EDGE + COLS : 2 * EDGE + COLS, :] = right[i].astype(F32)
            line[i, 2 * EDGE + COLS : LINE, :] = jnp.zeros((LINE - 2 * EDGE - COLS, C1), F32)
            for k in range(6):
                planes[t, 1 + r, :, k * C1 : (k + 1) * C1] = line[i, pl.ds(7 + k, Q, stride=4), :].astype(BF16)
            return carry

        lax.fori_loop(0, ROWS, step, 0, unroll=True)
        top[t] = planes[t, 1, :, C1 : 5 * C1]
        bottom[t] = planes[t, ROWS, :, C1 : 5 * C1]


def planes_of(left, own, right):
    lines = FRAMES * ROWS
    return pl.pallas_call(
        planes_kernel,
        out_shape=(
            shape((FRAMES, ROWS + 2, Q, 6 * C1), BF16),
            shape((FRAMES, Q, 4 * C1), BF16),
            shape((FRAMES, Q, 4 * C1), BF16),
        ),
        in_specs=[VMEM] * 3,
        out_specs=(VMEM,) * 3,
        scratch_shapes=[pltpu.VMEM((lines, LINE, C1), F32)],
        compiler_params=params(12),
        cost_estimate=cost(0, 4e6),
        name="planes",
    )(left, own.reshape(lines, COLS, C1), right)


def own_entries(rows, lanes):
    at = lax.rem(lax.broadcasted_iota(jnp.int32, (rows, lanes), 0), Q)
    return (at >= PAD) & (at < PAD + OWN)


def sums(values, mask):
    kept = jnp.where(mask, values, 0.0)
    return jnp.sum(kept, axis=0, keepdims=True), jnp.sum(kept * kept, axis=0, keepdims=True)


def frames_conv(frame, weight, store):
    store(0, mm(frame(0), weight(4)))
    store(1, mm(frame(0), weight(3)) + mm(frame(1), weight(2)))
    for t in range(2, FRAMES):
        store(t, mm(frame(t - 2), weight(0)) + mm(frame(t - 1), weight(1)) + mm(frame(t), weight(2)))


def table_of(ref, rows):
    return lambda s: ref[s * rows : (s + 1) * rows, :]


def middle_kernel(planes, table, hidden, stats):
    rows = ROWS * Q
    mask = own_entries(2 * (rows - 2 * Q), 2 * C1)
    stats[...] = jnp.zeros(stats.shape, F32)

    def frame(t):
        parts = []
        for b in range(3):
            block = planes[t, b : b + ROWS].reshape(rows, 6 * C1)
            parts.append(jnp.concatenate([block[:, : 4 * C1], block[:, 2 * C1 :]], axis=0))
        return jnp.concatenate(parts, axis=1)

    def store(t, value):
        hidden[t, :, 0:Q, :] = value[:rows].reshape(ROWS, Q, 2 * C1)
        hidden[t, :, Q : 2 * Q, :] = value[rows:].reshape(ROWS, Q, 2 * C1)
        inside = jnp.concatenate([value[Q : rows - Q], value[rows + Q : 2 * rows - Q]], axis=0)
        one, two = sums(inside, mask)
        stats[0:1, :] += one
        stats[1:2, :] += two

    frames_conv(frame, table_of(table, 12 * C1), store)


def middle(planes, table):
    return pl.pallas_call(
        middle_kernel,
        out_shape=(
            shape((FRAMES, ROWS, 2 * Q, 2 * C1), F32),
            shape((8, 2 * C1), F32),
        ),
        in_specs=[VMEM] * 2,
        out_specs=(VMEM,) * 2,
        compiler_params=params(12),
        cost_estimate=cost(6e9, 10e6),
        name="middle",
    )(planes, table)


def group_matrix(channels, shift):
    per = channels // GROUPS
    c = lax.broadcasted_iota(jnp.int32, (channels, 128), 0)
    g = lax.broadcasted_iota(jnp.int32, (channels, 128), 1)
    low = (g - shift) * per
    return jnp.where((c >= low) & (c < low + per), 1.0, 0.0).astype(F32)


def spread_matrix(channels, shift):
    per = channels // GROUPS
    g = lax.broadcasted_iota(jnp.int32, (128, channels), 0)
    c = lax.broadcasted_iota(jnp.int32, (128, channels), 1)
    low = (g - shift) * per
    return jnp.where((c >= low) & (c < low + per), 1.0, 0.0).astype(F32)


def grouped(one, two):
    channels = one.shape[1]
    wide = lambda v: jnp.broadcast_to(v, (8, channels))
    row = exact(wide(one), group_matrix(channels, 0)) + exact(wide(two), group_matrix(channels, GROUPS))
    return row[0:1]


def norm_terms(gathered, gain, shift, members):
    channels = gain.shape[1]
    total = jnp.broadcast_to(jnp.sum(gathered[...], axis=0, keepdims=True), (8, 128))
    mean = exact(total, spread_matrix(channels, 0))[0:1] / members
    square = exact(total, spread_matrix(channels, GROUPS))[0:1] / members
    variance = jnp.maximum(square - mean * mean, 0.0)
    factor = gain[...] / jnp.sqrt(variance + EPSILON)
    return 0.5 * factor, 0.5 * (shift[...] - mean * factor)


def edges_kernel(above, below, table, inner, stats, hidden, share, up, down):
    mask = own_entries(2 * Q, 2 * C1)
    total = [stats[0:1, :], stats[1:2, :]]
    for side, (ref, b) in enumerate(((above, 0), (below, 2))):
        lines = []
        for t in range(FRAMES):
            whole = ref[t]
            first = pltpu.roll(whole[:, 3 * C1 :].astype(F32), 1, 0).astype(BF16)
            last = pltpu.roll(whole[:, :C1].astype(F32), Q - 1, 0).astype(BF16)
            even = jnp.concatenate([first, whole[:, : 3 * C1]], axis=1)
            odd = jnp.concatenate([whole[:, C1:], last], axis=1)
            lines.append(jnp.concatenate([even, odd], axis=0))

        def part(s, frames):
            base = s * 12 * C1 + b * 4 * C1
            value = mm(jnp.concatenate([lines[t] for t in frames], axis=0), table[base : base + 4 * C1, :])
            return [value[i * 2 * Q : (i + 1) * 2 * Q] for i in range(len(frames))]

        zero, one, two = part(0, (0, 1)), part(1, (1, 2)), part(2, (1, 2, 3))
        pair, all_three = part(3, (0,)), part(4, (0,))
        extra = [all_three[0], pair[0] + two[0], zero[0] + one[0] + two[1], zero[1] + one[1] + two[2]]
        for t in range(FRAMES):
            value = inner[t, side * (ROWS - 1)] + extra[t]
            hidden[t, side] = value
            if side == 0:
                up[t, 0] = value.astype(BF16)
            else:
                down[t, 1] = value.astype(BF16)
            first, second = sums(value, mask)
            total[0] += first
            total[1] += second
    for t in range(FRAMES):
        up[t, 1] = inner[t, 1].astype(BF16)
        up[t, 2] = inner[t, 2].astype(BF16)
        down[t, 0] = inner[t, ROWS - 2].astype(BF16)
    one, two = (v[:, :C1] + v[:, C1:] for v in total)
    share[...] = jnp.broadcast_to(grouped(one, two), share.shape)


def edges(above, below, table, inner, stats, devices):
    return pl.pallas_call(
        edges_kernel,
        out_shape=(
            shape((FRAMES, 2, 2 * Q, 2 * C1), F32),
            shape((devices, 128), F32),
            shape((FRAMES, 3, 2 * Q, 2 * C1), BF16),
            shape((FRAMES, 2, 2 * Q, 2 * C1), BF16),
        ),
        in_specs=[VMEM] * 5,
        out_specs=(VMEM,) * 4,
        compiler_params=params(12),
        cost_estimate=cost(2e9, 10e6),
        name="edges",
    )(above, below, table, inner, stats)


def position():
    row, col = lax.axis_index("rows"), lax.axis_index("cols")
    return row == 0, row == lax.axis_size("rows") - 1, col == 0, col == lax.axis_size("cols") - 1


def kept(entry_out, edge):
    return 1.0 - jnp.where(entry_out, edge.astype(F32), 0.0)


def activate(values, terms):
    half = values * terms[0] + terms[1]
    return half + half * jnp.tanh(half)


def twice(terms):
    return tuple(jnp.concatenate([v, v], axis=1) for v in terms)


def raised(values):
    return pltpu.roll(values, Q - 1, 0)


def lowered(values):
    return pltpu.roll(values, 1, 0)


def second_kernel(
    inner, outer, above, below, gathered, gain, shift, reduce, second,
    hidden, share, up, down, act, lev, summed, *, members,
):
    first_row, last_row, first_col, last_col = position()
    terms = twice(norm_terms(gathered, gain, shift, members))
    entry = lax.broadcasted_iota(jnp.int32, (Q, 1), 0)
    right = kept(entry >= PAD + OWN, last_col)
    outside = right * kept(entry < PAD, first_col)
    below_in = 1.0 - last_row.astype(F32)
    above_in = 1.0 - first_row.astype(F32)

    def line(t, k, value):
        keep = right * below_in if k >= 10 else right
        a = activate(value[:Q].astype(F32), terms) * keep
        b = activate(value[Q:].astype(F32), terms) * keep
        act[t, k, 0:Q, 0 : 2 * C1] = a.astype(BF16)
        act[t, k, 0:Q, 2 * C1 :] = b[:, :C1].astype(BF16)
        act[t, k, Q:, 0 : 2 * C1] = b.astype(BF16)
        act[t, k, Q:, 2 * C1 :] = raised(a[:, :C1]).astype(BF16)

    def lines(t, carry):
        line(t, 0, above[t, 0])
        line(t, 1, above[t, 1])
        line(t, 2, outer[t, 0])
        for r in range(1, ROWS - 1):
            line(t, 2 + r, inner[t, r])
        line(t, 9, outer[t, 1])
        for r in range(3):
            line(t, 10 + r, below[t, r])
        value = None
        for b in range(3):
            left = jnp.concatenate([act[t, 2 * i + b] for i in range(6)], axis=0)
            part = mm(left, reduce[b * 3 * C1 : (b + 1) * 3 * C1, :])
            value = part if value is None else value + part
        for i in range(6):
            keep = outside
            if i == 0:
                keep = keep * above_in
            if i == 5:
                keep = keep * below_in
            even = value[i * 2 * Q : i * 2 * Q + Q] * keep
            odd = value[i * 2 * Q + Q : (i + 1) * 2 * Q] * keep
            e, o = even.astype(BF16), odd.astype(BF16)
            lev[t, i, 0:Q, 0:C2] = lowered(odd).astype(BF16)
            lev[t, i, 0:Q, C2 : 2 * C2] = e
            lev[t, i, 0:Q, 2 * C2 :] = o
            lev[t, i, Q:, 0:C2] = e
            lev[t, i, Q:, C2 : 2 * C2] = o
            lev[t, i, Q:, 2 * C2 :] = raised(even).astype(BF16)
        return carry

    lax.fori_loop(0, FRAMES, lines, 0)

    def add(i, carry):
        at = pl.ds(pl.multiple_of(i * C2, C2), C2)
        pair = second[0, at, :].astype(F32) + second[1, at, :].astype(F32)
        summed[0, at, :] = pair.astype(BF16)
        summed[1, at, :] = (pair + second[2, at, :].astype(F32)).astype(BF16)
        return carry

    lax.fori_loop(0, 9, add, 0)
    rows = 4 * 2 * Q
    mask = own_entries(rows, C2)
    total = [jnp.zeros((1, C2), F32), jnp.zeros((1, C2), F32)]

    def frame(t):
        return jnp.concatenate([lev[t, b : b + 4].reshape(rows, 3 * C2) for b in range(3)], axis=1)

    def store(t, value):
        full = value.reshape(4, 2 * Q, C2)
        hidden[t] = full
        up[t] = full[0:3].astype(BF16)
        down[t] = full[2:4].astype(BF16)
        one, two = sums(value, mask)
        total[0] += one
        total[1] += two

    frames_conv(frame, lambda s: second[s] if s < 3 else summed[s - 3], store)
    share[...] = jnp.broadcast_to(grouped(*total), share.shape)


def second_level(inner, outer, above, below, gathered, gain, shift, reduce, second, devices):
    return pl.pallas_call(
        functools.partial(second_kernel, members=float(devices * FRAMES * ROWS * COLS * (C1 // GROUPS))),
        out_shape=(
            shape((FRAMES, 4, 2 * Q, C2), F32),
            shape((devices, 128), F32),
            shape((FRAMES, 3, 2 * Q, C2), BF16),
            shape((FRAMES, 2, 2 * Q, C2), BF16),
        ),
        in_specs=[VMEM] * 9,
        out_specs=(VMEM,) * 4,
        scratch_shapes=[
            pltpu.VMEM((FRAMES, 14, 2 * Q, 3 * C1), BF16),
            pltpu.VMEM((FRAMES, 6, 2 * Q, 3 * C2), BF16),
            pltpu.VMEM((2, 9 * C2, C2), BF16),
        ],
        compiler_params=params(20),
        cost_estimate=cost(6e9, 12e6),
        name="second",
    )(
        inner, outer, above, below, gathered,
        gain.reshape(1, C1), shift.reshape(1, C1),
        reduce.reshape(9 * C1, C2), second.reshape(3, 9 * C2, C2),
    )


def third_kernel(inner, above, below, gathered, gain, shift, reduce, level, share, act, *, members):
    _, last_row, _, last_col = position()
    terms = norm_terms(gathered, gain, shift, members)
    entry = lax.broadcasted_iota(jnp.int32, (Q, 1), 0)
    right = kept(entry >= PAD + OWN, last_col)
    below_in = 1.0 - last_row.astype(F32)

    def line(t, k, value):
        keep = right * below_in if k >= 6 else right
        even = activate(value[:Q].astype(F32), terms) * keep
        odd = activate(value[Q:].astype(F32), terms) * keep
        act[t, k, :, 0:C2] = even.astype(BF16)
        act[t, k, :, C2 : 2 * C2] = odd.astype(BF16)
        act[t, k, :, 2 * C2 :] = raised(even).astype(BF16)

    def lines(t, carry):
        for r in range(2):
            line(t, r, above[t, r])
        for r in range(4):
            line(t, 2 + r, inner[t, r])
        for r in range(3):
            line(t, 6 + r, below[t, r])
        return carry

    lax.fori_loop(0, FRAMES, lines, 0)
    mask = own_entries(2 * Q, C3)
    total = [jnp.zeros((1, C3), F32), jnp.zeros((1, C3), F32)]
    value = None
    for b in range(3):
        left = jnp.concatenate([act[t, 2 * i + b] for t in range(FRAMES) for i in range(4)], axis=0)
        part = mm(left, reduce[b * 3 * C2 : (b + 1) * 3 * C2, :])
        value = part if value is None else value + part
    rounded = value.astype(BF16)
    level[...] = rounded.reshape(FRAMES, 4, Q, C3)
    wide = rounded.astype(F32)
    for t in range(FRAMES):
        one, two = sums(wide[(4 * t + 1) * Q : (4 * t + 3) * Q], mask)
        total[0] += one
        total[1] += two
    share[...] = jnp.broadcast_to(grouped(*total), share.shape)


def third_level(inner, above, below, gathered, gain, shift, reduce, devices):
    return pl.pallas_call(
        functools.partial(third_kernel, members=float(devices * FRAMES * 4 * 2 * OWN * (C2 // GROUPS))),
        out_shape=(shape((FRAMES, 4, Q, C3), BF16), shape((devices, 128), F32)),
        in_specs=[VMEM] * 7,
        out_specs=(VMEM,) * 2,
        scratch_shapes=[pltpu.VMEM((FRAMES, 10, Q, 3 * C2), BF16)],
        compiler_params=params(12),
        cost_estimate=cost(2e9, 8e6),
        name="third",
    )(inner, above, below, gathered, gain.reshape(1, C2), shift.reshape(1, C2), reduce.reshape(9 * C2, C3))


def last_kernel(level, gathered, gain, shift, table, result, act, *, members):
    first_row, last_row, first_col, last_col = position()
    terms = norm_terms(gathered, gain, shift, members)
    entry = lax.broadcasted_iota(jnp.int32, (Q, 1), 0)
    outside = kept(entry >= PAD + OWN, last_col) * kept(entry < PAD, first_col)
    below_in = 1.0 - last_row.astype(F32)
    above_in = 1.0 - first_row.astype(F32)
    for t in range(FRAMES):
        for i in range(4):
            keep = outside
            if i == 0:
                keep = keep * above_in
            if i == 3:
                keep = keep * below_in
            v = activate(level[t, i].astype(F32), terms) * keep
            act[t, i, :, 0:C3] = lowered(v).astype(BF16)
            act[t, i, :, C3 : 2 * C3] = v.astype(BF16)
            act[t, i, :, 2 * C3 :] = raised(v).astype(BF16)
    value = None
    for b in range(3):
        for e in range(3):
            lanes = slice(e * C3, (e + 1) * C3)
            left = jnp.concatenate([act[t, i + b, :, lanes] for t in range(FRAMES) for i in range(2)], axis=0)
            right = jnp.concatenate([table[a, 3 * b + e] for a in range(3)], axis=0)
            part = lax.dot_general(left, right, (((1,), (1,)), ((), ())), preferred_element_type=F32)
            value = part if value is None else value + part

    def tap(t, a):
        at = 2 * Q * max(t, 0)
        return value[at : at + 2 * Q, a * OUT : (a + 1) * OUT]

    side = jnp.concatenate([tap(t - 2, 0) + tap(t - 1, 1) + tap(t, 2) for t in range(FRAMES)], axis=1).T
    for t in range(FRAMES):
        for i in range(2):
            at = i * Q + PAD
            result[t, i] = side[t * OUT : (t + 1) * OUT, at : at + OWN].astype(BF16)


def last_level(level, gathered, gain, shift, table, devices):
    swapped = jnp.swapaxes(table, 3, 4).reshape(3, 9, OUT, C3)
    out = pl.pallas_call(
        functools.partial(last_kernel, members=float(devices * FRAMES * 2 * OWN * (C3 // GROUPS))),
        out_shape=shape((FRAMES, 2, OUT, OWN), BF16),
        in_specs=[VMEM] * 5,
        out_specs=VMEM,
        scratch_shapes=[pltpu.VMEM((FRAMES, 4, Q, 3 * C3), BF16)],
        compiler_params=params(10),
        cost_estimate=cost(1e9, 4e6),
        name="last",
    )(level, gathered, gain.reshape(1, C3), shift.reshape(1, C3), swapped)
    return jnp.swapaxes(out, 2, 3)


def forward(axis):
    return [(i, i + 1) for i in range(lax.axis_size(axis) - 1)]


def backward(axis):
    return [(i + 1, i) for i in range(lax.axis_size(axis) - 1)]


def from_both(last, first, axis):
    return lax.ppermute(last, axis, forward(axis)), lax.ppermute(first, axis, backward(axis))


def everywhere(share):
    return lax.all_to_all(share, AXES, 0, 0, tiled=True)


def shards(
    features, conv_first, first_reduce_kernel, conv_second, second_reduce_kernel, conv_last,
    gain_first, shift_first, gain_second, shift_second, gain_third, shift_third,
):
    devices = lax.axis_size("rows") * lax.axis_size("cols")
    left, right = from_both(*cut(features), "cols")
    table = weights(conv_first)
    planes, top, bottom = planes_of(left, features, right)
    above, below = from_both(bottom, top, "rows")
    inner, stats = middle(planes, table)
    outer, share, up, down = edges(above, below, table, inner, stats, devices)
    above, below = from_both(down, up, "rows")
    hidden, share, up, down = second_level(
        inner, outer, above, below, everywhere(share), gain_first, shift_first,
        first_reduce_kernel, conv_second, devices,
    )
    above, below = from_both(down, up, "rows")
    level, share = third_level(
        hidden, above, below, everywhere(share), gain_second, shift_second,
        second_reduce_kernel, devices,
    )
    return last_level(level, everywhere(share), gain_third, shift_third, conv_last, devices)


def solution(mesh):
    return jax.shard_map(
        shards,
        mesh=mesh,
        in_specs=(P(None, "rows", "cols", None),) + (P(),) * 11,
        out_specs=P(None, "rows", "cols", None),
        check_vma=False,
    )
```

```python
import functools

import jax
import jax.numpy as jnp
from jax import lax
from jax.experimental import pallas as pl
from jax.experimental.pallas import tpu as pltpu
from jax.sharding import PartitionSpec as P

GROUPS = 32
EPSILON = 1e-6
FRAMES = 4
ROWS = 8
COLS = 160
C1, C2, C3, OUT = 128, 256, 512, 32
Q = 48
PAD = 2
OWN = COLS // 4
EDGE = 16
LINE = 208
AXES = ("rows", "cols")
F32, BF16 = jnp.float32, jnp.bfloat16
VMEM = pl.BlockSpec(memory_space=pltpu.VMEM)
HBM = pl.BlockSpec(memory_space=pltpu.HBM)


def params(mib):
    return pltpu.CompilerParams(vmem_limit_bytes=mib * 1024 * 1024)


def cost(flops, read):
    return pl.CostEstimate(flops=int(flops), bytes_accessed=int(read), transcendentals=0)


def shape(dims, dtype):
    return jax.ShapeDtypeStruct(dims, dtype)


def mm(left, right):
    return jnp.dot(left, right, preferred_element_type=F32)


def position():
    row, col = lax.axis_index("rows"), lax.axis_index("cols")
    return row == 0, row == lax.axis_size("rows") - 1, col == 0, col == lax.axis_size("cols") - 1


def weights_kernel(first, one):
    zero = jnp.zeros((C1, C1), BF16)
    for b in range(3):
        for e in range(3):
            taps = [first[((a * 3 + b) * 3 + e) * C1 : ((a * 3 + b) * 3 + e + 1) * C1, :] for a in range(3)]
            wide = [k.astype(F32) for k in taps]
            pair = wide[0] + wide[1]
            for s, k in enumerate(taps + [pair.astype(BF16), (pair + wide[2]).astype(BF16)]):
                base = s * 12 * C1 + b * 4 * C1
                one[base + e * C1 : base + (e + 1) * C1, 0:C1] = k
                one[base + (e + 1) * C1 : base + (e + 2) * C1, C1 : 2 * C1] = k
        for s in range(5):
            base = s * 12 * C1 + b * 4 * C1
            one[base + 3 * C1 : base + 4 * C1, 0:C1] = zero
            one[base : base + C1, C1 : 2 * C1] = zero


def weights(first):
    return pl.pallas_call(
        weights_kernel,
        out_shape=shape((5 * 12 * C1, 2 * C1), BF16),
        in_specs=[VMEM],
        out_specs=VMEM,
        compiler_params=params(8),
        cost_estimate=cost(0, 5e6),
        name="weights",
    )(first.reshape(27 * C1, C1))


def cut_kernel(features, last, first, sem):
    copies = [
        pltpu.make_async_copy(features.at[:, pl.ds(COLS - EDGE, EDGE)], last, sem.at[0]),
        pltpu.make_async_copy(features.at[:, pl.ds(0, EDGE)], first, sem.at[1]),
    ]
    for c in copies:
        c.start()
    for c in copies:
        c.wait()


def cut(features):
    edge = shape((FRAMES * ROWS, EDGE, C1), BF16)
    return pl.pallas_call(
        cut_kernel,
        out_shape=(edge, edge),
        in_specs=[HBM],
        out_specs=(VMEM,) * 2,
        scratch_shapes=[pltpu.SemaphoreType.DMA((2,))],
        compiler_params=params(4),
        cost_estimate=cost(0, 4e5),
        name="cut",
    )(features.reshape(FRAMES * ROWS, COLS, C1))


def planes_kernel(left, own, right, planes, top, bottom, line):
    _, _, first_col, last_col = position()
    left_in = 1.0 - first_col.astype(F32)
    right_in = 1.0 - last_col.astype(F32)
    for t in range(FRAMES):
        planes[t, 0] = jnp.zeros((Q, 6 * C1), BF16)
        planes[t, ROWS + 1] = jnp.zeros((Q, 6 * C1), BF16)

        def step(r, carry, t=t):
            i = t * ROWS + r
            line[i, 0:EDGE, :] = left[i].astype(F32) * left_in
            line[i, EDGE : EDGE + COLS, :] = own[i].astype(F32)
            line[i, EDGE + COLS : 2 * EDGE + COLS, :] = right[i].astype(F32) * right_in
            line[i, 2 * EDGE + COLS : LINE, :] = jnp.zeros((LINE - 2 * EDGE - COLS, C1), F32)
            for k in range(6):
                planes[t, 1 + r, :, k * C1 : (k + 1) * C1] = line[i, pl.ds(7 + k, Q, stride=4), :].astype(BF16)
            return carry

        lax.fori_loop(0, ROWS, step, 0, unroll=True)
        top[t] = planes[t, 1, :, C1 : 5 * C1]
        bottom[t] = planes[t, ROWS, :, C1 : 5 * C1]


def planes_of(left, own, right):
    lines = FRAMES * ROWS
    return pl.pallas_call(
        planes_kernel,
        out_shape=(
            shape((FRAMES, ROWS + 2, Q, 6 * C1), BF16),
            shape((FRAMES, Q, 4 * C1), BF16),
            shape((FRAMES, Q, 4 * C1), BF16),
        ),
        in_specs=[VMEM] * 3,
        out_specs=(VMEM,) * 3,
        scratch_shapes=[pltpu.VMEM((lines, LINE, C1), F32)],
        compiler_params=params(12),
        cost_estimate=cost(0, 4e6),
        name="planes",
    )(left, own.reshape(lines, COLS, C1), right)


def own_entries(rows, lanes):
    at = lax.rem(lax.broadcasted_iota(jnp.int32, (rows, lanes), 0), Q)
    return (at >= PAD) & (at < PAD + OWN)


def sums(values, mask):
    kept = jnp.where(mask, values, 0.0)
    return jnp.sum(kept, axis=0, keepdims=True), jnp.sum(kept * kept, axis=0, keepdims=True)


def frames_conv(frame, weight, store):
    store(0, mm(frame(0), weight(4)))
    store(1, mm(frame(0), weight(3)) + mm(frame(1), weight(2)))
    for t in range(2, FRAMES):
        store(t, mm(frame(t - 2), weight(0)) + mm(frame(t - 1), weight(1)) + mm(frame(t), weight(2)))


def table_of(ref, rows):
    return lambda s: ref[s * rows : (s + 1) * rows, :]


def middle_kernel(planes, table, hidden, stats):
    rows = ROWS * Q
    mask = own_entries(2 * (rows - 2 * Q), 2 * C1)
    stats[...] = jnp.zeros(stats.shape, F32)

    def frame(t):
        parts = []
        for b in range(3):
            block = planes[t, b : b + ROWS].reshape(rows, 6 * C1)
            parts.append(jnp.concatenate([block[:, : 4 * C1], block[:, 2 * C1 :]], axis=0))
        return jnp.concatenate(parts, axis=1)

    def store(t, value):
        hidden[t, :, 0:Q, :] = value[:rows].reshape(ROWS, Q, 2 * C1)
        hidden[t, :, Q : 2 * Q, :] = value[rows:].reshape(ROWS, Q, 2 * C1)
        inside = jnp.concatenate([value[Q : rows - Q], value[rows + Q : 2 * rows - Q]], axis=0)
        one, two = sums(inside, mask)
        stats[0:1, :] += one
        stats[1:2, :] += two

    frames_conv(frame, table_of(table, 12 * C1), store)


def middle(planes, table):
    return pl.pallas_call(
        middle_kernel,
        out_shape=(
            shape((FRAMES, ROWS, 2 * Q, 2 * C1), F32),
            shape((8, 2 * C1), F32),
        ),
        in_specs=[VMEM] * 2,
        out_specs=(VMEM,) * 2,
        compiler_params=params(12),
        cost_estimate=cost(6e9, 10e6),
        name="middle",
    )(planes, table)


def group_totals(values, per):
    lane = lax.broadcasted_iota(jnp.int32, (8, 128), 1)
    step = 1
    while step < per:
        other = jnp.where((lane & step) == 0, pltpu.roll(values, 128 - step, 1), pltpu.roll(values, step, 1))
        values = values + other
        step *= 2
    return values


def slots(per):
    lane = lax.broadcasted_iota(jnp.int32, (8, 128), 1)
    return (lane & (per - 1)) == lax.broadcasted_iota(jnp.int32, (8, 128), 0)


def grouped(one, two):
    channels = one.shape[1]
    per = channels // GROUPS
    lines = []
    for low in range(0, channels, 128):
        lines += [one[:, low : low + 128], two[:, low : low + 128]]
    lines += [jnp.zeros((1, 128), F32)] * (8 - len(lines))
    totals = group_totals(jnp.concatenate(lines, axis=0), per)
    return jnp.sum(jnp.where(slots(per), totals, 0.0), axis=0, keepdims=True)


def norm_terms(gathered, gain, shift, members):
    channels = gain.shape[1]
    per = channels // GROUPS
    total = jnp.broadcast_to(jnp.sum(gathered[...], axis=0, keepdims=True), (8, 128))
    lane = lax.broadcasted_iota(jnp.int32, (8, 128), 1)
    source = lane - (lane & (per - 1)) + (lax.broadcasted_iota(jnp.int32, (8, 128), 0) & (per - 1))
    lines = jnp.take_along_axis(total, source, axis=1) / members
    count = channels // 128
    mean = jnp.concatenate([lines[2 * i : 2 * i + 1] for i in range(count)], axis=1)
    square = jnp.concatenate([lines[2 * i + 1 : 2 * i + 2] for i in range(count)], axis=1)
    variance = jnp.maximum(square - mean * mean, 0.0)
    factor = gain[...] / jnp.sqrt(variance + EPSILON)
    return 0.5 * factor, 0.5 * (shift[...] - mean * factor)


def edges_kernel(above, below, table, inner, stats, hidden, share, up, down):
    mask = own_entries(2 * Q, 2 * C1)
    total = [stats[0:1, :], stats[1:2, :]]
    first_row, last_row, _, _ = position()
    for side, (ref, b, end) in enumerate(((above, 0, first_row), (below, 2, last_row))):
        inside = 1.0 - end.astype(F32)
        lines = []
        for t in range(FRAMES):
            wide = ref[t].astype(F32) * inside
            whole = wide.astype(BF16)
            first = pltpu.roll(wide[:, 3 * C1 :], 1, 0).astype(BF16)
            last = pltpu.roll(wide[:, :C1], Q - 1, 0).astype(BF16)
            even = jnp.concatenate([first, whole[:, : 3 * C1]], axis=1)
            odd = jnp.concatenate([whole[:, C1:], last], axis=1)
            lines.append(jnp.concatenate([even, odd], axis=0))

        def part(s, frames):
            base = s * 12 * C1 + b * 4 * C1
            value = mm(jnp.concatenate([lines[t] for t in frames], axis=0), table[base : base + 4 * C1, :])
            return [value[i * 2 * Q : (i + 1) * 2 * Q] for i in range(len(frames))]

        zero, one, two = part(0, (0, 1)), part(1, (1, 2)), part(2, (1, 2, 3))
        pair, all_three = part(3, (0,)), part(4, (0,))
        extra = [all_three[0], pair[0] + two[0], zero[0] + one[0] + two[1], zero[1] + one[1] + two[2]]
        for t in range(FRAMES):
            value = inner[t, side * (ROWS - 1)] + extra[t]
            hidden[t, side] = value
            if side == 0:
                up[t, 0] = value.astype(BF16)
            else:
                down[t, 1] = value.astype(BF16)
            first, second = sums(value, mask)
            total[0] += first
            total[1] += second
    for t in range(FRAMES):
        up[t, 1] = inner[t, 1].astype(BF16)
        up[t, 2] = inner[t, 2].astype(BF16)
        down[t, 0] = inner[t, ROWS - 2].astype(BF16)
    one, two = (v[:, :C1] + v[:, C1:] for v in total)
    share[...] = jnp.broadcast_to(grouped(one, two), share.shape)


def edges(above, below, table, inner, stats, devices):
    return pl.pallas_call(
        edges_kernel,
        out_shape=(
            shape((FRAMES, 2, 2 * Q, 2 * C1), F32),
            shape((devices, 128), F32),
            shape((FRAMES, 3, 2 * Q, 2 * C1), BF16),
            shape((FRAMES, 2, 2 * Q, 2 * C1), BF16),
        ),
        in_specs=[VMEM] * 5,
        out_specs=(VMEM,) * 4,
        compiler_params=params(12),
        cost_estimate=cost(2e9, 10e6),
        name="edges",
    )(above, below, table, inner, stats)


def kept(entry_out, edge):
    return 1.0 - jnp.where(entry_out, edge.astype(F32), 0.0)


def activate(values, terms):
    half = values * terms[0] + terms[1]
    return half + half * jnp.tanh(half)


def twice(terms):
    return tuple(jnp.concatenate([v, v], axis=1) for v in terms)


def raised(values):
    return pltpu.roll(values, Q - 1, 0)


def lowered(values):
    return pltpu.roll(values, 1, 0)


def second_kernel(
    inner, outer, above, below, gathered, gain, shift, reduce, second,
    hidden, share, up, down, act, lev, summed, *, members,
):
    first_row, last_row, first_col, last_col = position()
    terms = twice(norm_terms(gathered, gain, shift, members))
    entry = lax.broadcasted_iota(jnp.int32, (Q, 1), 0)
    right = kept(entry >= PAD + OWN, last_col)
    outside = right * kept(entry < PAD, first_col)
    below_in = 1.0 - last_row.astype(F32)
    above_in = 1.0 - first_row.astype(F32)

    def line(t, k, value):
        keep = right * below_in if k >= 10 else right
        a = activate(value[:Q].astype(F32), terms) * keep
        b = activate(value[Q:].astype(F32), terms) * keep
        act[t, k, 0:Q, 0 : 2 * C1] = a.astype(BF16)
        act[t, k, 0:Q, 2 * C1 :] = b[:, :C1].astype(BF16)
        act[t, k, Q:, 0 : 2 * C1] = b.astype(BF16)
        act[t, k, Q:, 2 * C1 :] = raised(a[:, :C1]).astype(BF16)

    def lines(t, carry):
        line(t, 0, above[t, 0])
        line(t, 1, above[t, 1])
        line(t, 2, outer[t, 0])
        for r in range(1, ROWS - 1):
            line(t, 2 + r, inner[t, r])
        line(t, 9, outer[t, 1])
        for r in range(3):
            line(t, 10 + r, below[t, r])
        value = None
        for b in range(3):
            left = jnp.concatenate([act[t, 2 * i + b] for i in range(6)], axis=0)
            part = mm(left, reduce[b * 3 * C1 : (b + 1) * 3 * C1, :])
            value = part if value is None else value + part
        for i in range(6):
            keep = outside
            if i == 0:
                keep = keep * above_in
            if i == 5:
                keep = keep * below_in
            even = value[i * 2 * Q : i * 2 * Q + Q] * keep
            odd = value[i * 2 * Q + Q : (i + 1) * 2 * Q] * keep
            e, o = even.astype(BF16), odd.astype(BF16)
            lev[t, i, 0:Q, 0:C2] = lowered(odd).astype(BF16)
            lev[t, i, 0:Q, C2 : 2 * C2] = e
            lev[t, i, 0:Q, 2 * C2 :] = o
            lev[t, i, Q:, 0:C2] = e
            lev[t, i, Q:, C2 : 2 * C2] = o
            lev[t, i, Q:, 2 * C2 :] = raised(even).astype(BF16)
        return carry

    lax.fori_loop(0, FRAMES, lines, 0, unroll=True)

    def add(i, carry):
        at = pl.ds(pl.multiple_of(i * C2, C2), C2)
        pair = second[0, at, :].astype(F32) + second[1, at, :].astype(F32)
        summed[0, at, :] = pair.astype(BF16)
        summed[1, at, :] = (pair + second[2, at, :].astype(F32)).astype(BF16)
        return carry

    lax.fori_loop(0, 9, add, 0, unroll=True)
    rows = 4 * 2 * Q
    mask = own_entries(rows, C2)
    total = [jnp.zeros((1, C2), F32), jnp.zeros((1, C2), F32)]

    def frame(t):
        return jnp.concatenate([lev[t, b : b + 4].reshape(rows, 3 * C2) for b in range(3)], axis=1)

    def store(t, value):
        full = value.reshape(4, 2 * Q, C2)
        hidden[t] = full
        up[t] = full[0:3].astype(BF16)
        down[t] = full[2:4].astype(BF16)
        one, two = sums(value, mask)
        total[0] += one
        total[1] += two

    frames_conv(frame, lambda s: second[s] if s < 3 else summed[s - 3], store)
    share[...] = jnp.broadcast_to(grouped(*total), share.shape)


def second_level(inner, outer, above, below, gathered, gain, shift, reduce, second, devices):
    return pl.pallas_call(
        functools.partial(second_kernel, members=float(devices * FRAMES * ROWS * COLS * (C1 // GROUPS))),
        out_shape=(
            shape((FRAMES, 4, 2 * Q, C2), F32),
            shape((devices, 128), F32),
            shape((FRAMES, 3, 2 * Q, C2), BF16),
            shape((FRAMES, 2, 2 * Q, C2), BF16),
        ),
        in_specs=[VMEM] * 9,
        out_specs=(VMEM,) * 4,
        scratch_shapes=[
            pltpu.VMEM((FRAMES, 14, 2 * Q, 3 * C1), BF16),
            pltpu.VMEM((FRAMES, 6, 2 * Q, 3 * C2), BF16),
            pltpu.VMEM((2, 9 * C2, C2), BF16),
        ],
        compiler_params=params(20),
        cost_estimate=cost(6e9, 12e6),
        name="second",
    )(
        inner, outer, above, below, gathered,
        gain.reshape(1, C1), shift.reshape(1, C1),
        reduce.reshape(9 * C1, C2), second.reshape(3, 9 * C2, C2),
    )


def third_kernel(inner, above, below, gathered, gain, shift, reduce, level, share, act, *, members):
    _, last_row, _, last_col = position()
    terms = norm_terms(gathered, gain, shift, members)
    entry = lax.broadcasted_iota(jnp.int32, (Q, 1), 0)
    right = kept(entry >= PAD + OWN, last_col)
    below_in = 1.0 - last_row.astype(F32)

    def line(t, k, value):
        keep = right * below_in if k >= 6 else right
        even = activate(value[:Q].astype(F32), terms) * keep
        odd = activate(value[Q:].astype(F32), terms) * keep
        act[t, k, :, 0:C2] = even.astype(BF16)
        act[t, k, :, C2 : 2 * C2] = odd.astype(BF16)
        act[t, k, :, 2 * C2 :] = raised(even).astype(BF16)

    def lines(t, carry):
        for r in range(2):
            line(t, r, above[t, r])
        for r in range(4):
            line(t, 2 + r, inner[t, r])
        for r in range(3):
            line(t, 6 + r, below[t, r])
        return carry

    lax.fori_loop(0, FRAMES, lines, 0, unroll=True)
    mask = own_entries(2 * Q, C3)
    total = [jnp.zeros((1, C3), F32), jnp.zeros((1, C3), F32)]
    value = None
    for b in range(3):
        left = jnp.concatenate([act[t, 2 * i + b] for t in range(FRAMES) for i in range(4)], axis=0)
        part = mm(left, reduce[b * 3 * C2 : (b + 1) * 3 * C2, :])
        value = part if value is None else value + part
    rounded = value.astype(BF16)
    level[...] = rounded.reshape(FRAMES, 4, Q, C3)
    wide = rounded.astype(F32)
    for t in range(FRAMES):
        one, two = sums(wide[(4 * t + 1) * Q : (4 * t + 3) * Q], mask)
        total[0] += one
        total[1] += two
    share[...] = jnp.broadcast_to(grouped(*total), share.shape)


def third_level(inner, above, below, gathered, gain, shift, reduce, devices):
    return pl.pallas_call(
        functools.partial(third_kernel, members=float(devices * FRAMES * 4 * 2 * OWN * (C2 // GROUPS))),
        out_shape=(shape((FRAMES, 4, Q, C3), BF16), shape((devices, 128), F32)),
        in_specs=[VMEM] * 7,
        out_specs=(VMEM,) * 2,
        scratch_shapes=[pltpu.VMEM((FRAMES, 10, Q, 3 * C2), BF16)],
        compiler_params=params(12),
        cost_estimate=cost(2e9, 8e6),
        name="third",
    )(inner, above, below, gathered, gain.reshape(1, C2), shift.reshape(1, C2), reduce.reshape(9 * C2, C3))


def last_kernel(level, gathered, gain, shift, table, result, act, *, members):
    first_row, last_row, first_col, last_col = position()
    terms = norm_terms(gathered, gain, shift, members)
    entry = lax.broadcasted_iota(jnp.int32, (Q, 1), 0)
    outside = kept(entry >= PAD + OWN, last_col) * kept(entry < PAD, first_col)
    below_in = 1.0 - last_row.astype(F32)
    above_in = 1.0 - first_row.astype(F32)
    for t in range(FRAMES):
        for i in range(4):
            keep = outside
            if i == 0:
                keep = keep * above_in
            if i == 3:
                keep = keep * below_in
            v = activate(level[t, i].astype(F32), terms) * keep
            act[t, i, :, 0:C3] = lowered(v).astype(BF16)
            act[t, i, :, C3 : 2 * C3] = v.astype(BF16)
            act[t, i, :, 2 * C3 :] = raised(v).astype(BF16)
    value = None
    for b in range(3):
        for e in range(3):
            lanes = slice(e * C3, (e + 1) * C3)
            left = jnp.concatenate([act[t, i + b, :, lanes] for t in range(FRAMES) for i in range(2)], axis=0)
            right = jnp.concatenate([table[a, 3 * b + e] for a in range(3)], axis=0)
            part = lax.dot_general(left, right, (((1,), (1,)), ((), ())), preferred_element_type=F32)
            value = part if value is None else value + part

    def tap(t, a):
        at = 2 * Q * max(t, 0)
        return value[at : at + 2 * Q, a * OUT : (a + 1) * OUT]

    side = jnp.concatenate([tap(t - 2, 0) + tap(t - 1, 1) + tap(t, 2) for t in range(FRAMES)], axis=1).T
    for t in range(FRAMES):
        for i in range(2):
            at = i * Q + PAD
            result[t, i] = side[t * OUT : (t + 1) * OUT, at : at + OWN].astype(BF16)


def last_level(level, gathered, gain, shift, table, devices):
    swapped = jnp.swapaxes(table, 3, 4).reshape(3, 9, OUT, C3)
    out = pl.pallas_call(
        functools.partial(last_kernel, members=float(devices * FRAMES * 2 * OWN * (C3 // GROUPS))),
        out_shape=shape((FRAMES, 2, OUT, OWN), BF16),
        in_specs=[VMEM] * 5,
        out_specs=VMEM,
        scratch_shapes=[pltpu.VMEM((FRAMES, 4, Q, 3 * C3), BF16)],
        compiler_params=params(10),
        cost_estimate=cost(1e9, 4e6),
        name="last",
    )(level, gathered, gain.reshape(1, C3), shift.reshape(1, C3), swapped)
    return jnp.swapaxes(out, 2, 3)


def forward(axis):
    return [(i, (i + 1) % lax.axis_size(axis)) for i in range(lax.axis_size(axis))]


def backward(axis):
    return [((i + 1) % lax.axis_size(axis), i) for i in range(lax.axis_size(axis))]


def from_both(last, first, axis):
    return lax.ppermute(last, axis, forward(axis)), lax.ppermute(first, axis, backward(axis))


def everywhere(share):
    return lax.all_to_all(share, AXES, 0, 0, tiled=True)


def shards(
    features, conv_first, first_reduce_kernel, conv_second, second_reduce_kernel, conv_last,
    gain_first, shift_first, gain_second, shift_second, gain_third, shift_third,
):
    devices = lax.axis_size("rows") * lax.axis_size("cols")
    left, right = from_both(*cut(features), "cols")
    table = weights(conv_first)
    planes, top, bottom = planes_of(left, features, right)
    above, below = from_both(bottom, top, "rows")
    inner, stats = middle(planes, table)
    outer, share, up, down = edges(above, below, table, inner, stats, devices)
    above, below = from_both(down, up, "rows")
    hidden, share, up, down = second_level(
        inner, outer, above, below, everywhere(share), gain_first, shift_first,
        first_reduce_kernel, conv_second, devices,
    )
    above, below = from_both(down, up, "rows")
    level, share = third_level(
        hidden, above, below, everywhere(share), gain_second, shift_second,
        second_reduce_kernel, devices,
    )
    return last_level(level, everywhere(share), gain_third, shift_third, conv_last, devices)


def solution(mesh):
    return jax.shard_map(
        shards,
        mesh=mesh,
        in_specs=(P(None, "rows", "cols", None),) + (P(),) * 11,
        out_specs=P(None, "rows", "cols", None),
        check_vma=False,
    )
```

```python
import functools

import jax
import jax.numpy as jnp
from jax import lax
from jax.experimental import pallas as pl
from jax.experimental.pallas import tpu as pltpu
from jax.sharding import PartitionSpec as P

GROUPS = 32
EPSILON = 1e-6
FRAMES = 4
ROWS = 8
COLS = 160
C1, C2, C3, OUT = 128, 256, 512, 32
Q = 48
PAD = 2
OWN = COLS // 4
EDGE = 16
LINE = 208
AXES = ("rows", "cols")
F32, BF16 = jnp.float32, jnp.bfloat16
VMEM = pl.BlockSpec(memory_space=pltpu.VMEM)
HBM = pl.BlockSpec(memory_space=pltpu.HBM)


def params(mib):
    return pltpu.CompilerParams(vmem_limit_bytes=mib * 1024 * 1024)


def cost(flops, read):
    return pl.CostEstimate(flops=int(flops), bytes_accessed=int(read), transcendentals=0)


def shape(dims, dtype):
    return jax.ShapeDtypeStruct(dims, dtype)


def mm(left, right):
    return jnp.dot(left, right, preferred_element_type=F32)


def position():
    row, col = lax.axis_index("rows"), lax.axis_index("cols")
    return row == 0, row == lax.axis_size("rows") - 1, col == 0, col == lax.axis_size("cols") - 1


def weights_kernel(first, one):
    zero = jnp.zeros((C1, C1), BF16)
    for b in range(3):
        for e in range(3):
            taps = [first[((a * 3 + b) * 3 + e) * C1 : ((a * 3 + b) * 3 + e + 1) * C1, :] for a in range(3)]
            wide = [k.astype(F32) for k in taps]
            pair = wide[0] + wide[1]
            for s, k in enumerate(taps + [pair.astype(BF16), (pair + wide[2]).astype(BF16)]):
                base = s * 12 * C1 + b * 4 * C1
                one[base + e * C1 : base + (e + 1) * C1, 0:C1] = k
                one[base + (e + 1) * C1 : base + (e + 2) * C1, C1 : 2 * C1] = k
        for s in range(5):
            base = s * 12 * C1 + b * 4 * C1
            one[base + 3 * C1 : base + 4 * C1, 0:C1] = zero
            one[base : base + C1, C1 : 2 * C1] = zero


def weights(first):
    return pl.pallas_call(
        weights_kernel,
        out_shape=shape((5 * 12 * C1, 2 * C1), BF16),
        in_specs=[VMEM],
        out_specs=VMEM,
        compiler_params=params(8),
        cost_estimate=cost(0, 5e6),
        name="weights",
    )(first.reshape(27 * C1, C1))


def cut_kernel(features, last, first, sem):
    copies = [
        pltpu.make_async_copy(features.at[:, pl.ds(COLS - EDGE, EDGE)], last, sem.at[0]),
        pltpu.make_async_copy(features.at[:, pl.ds(0, EDGE)], first, sem.at[1]),
    ]
    for c in copies:
        c.start()
    for c in copies:
        c.wait()


def cut(features):
    edge = shape((FRAMES * ROWS, EDGE, C1), BF16)
    return pl.pallas_call(
        cut_kernel,
        out_shape=(edge, edge),
        in_specs=[HBM],
        out_specs=(VMEM,) * 2,
        scratch_shapes=[pltpu.SemaphoreType.DMA((2,))],
        compiler_params=params(4),
        cost_estimate=cost(0, 4e5),
        name="cut",
    )(features.reshape(FRAMES * ROWS, COLS, C1))


def planes_kernel(left, own, right, planes, top, bottom, line):
    _, _, first_col, last_col = position()
    left_in = 1.0 - first_col.astype(F32)
    right_in = 1.0 - last_col.astype(F32)
    for t in range(FRAMES):

        def step(r, carry, t=t):
            i = t * ROWS + r
            line[i, 0:EDGE, :] = left[i].astype(F32) * left_in
            line[i, EDGE : EDGE + COLS, :] = own[i].astype(F32)
            line[i, EDGE + COLS : 2 * EDGE + COLS, :] = right[i].astype(F32) * right_in
            line[i, 2 * EDGE + COLS : LINE, :] = jnp.zeros((LINE - 2 * EDGE - COLS, C1), F32)
            for k in range(6):
                planes[t, r, :, k * C1 : (k + 1) * C1] = line[i, pl.ds(7 + k, Q, stride=4), :].astype(BF16)
            return carry

        lax.fori_loop(0, ROWS, step, 0, unroll=True)
        top[t] = planes[t, 0, :, C1 : 5 * C1]
        bottom[t] = planes[t, ROWS - 1, :, C1 : 5 * C1]


def planes_of(left, own, right):
    lines = FRAMES * ROWS
    return pl.pallas_call(
        planes_kernel,
        out_shape=(
            shape((FRAMES, ROWS, Q, 6 * C1), BF16),
            shape((FRAMES, Q, 4 * C1), BF16),
            shape((FRAMES, Q, 4 * C1), BF16),
        ),
        in_specs=[VMEM] * 3,
        out_specs=(VMEM,) * 3,
        scratch_shapes=[pltpu.VMEM((lines, LINE, C1), F32)],
        compiler_params=params(12),
        cost_estimate=cost(0, 4e6),
        name="planes",
    )(left, own.reshape(lines, COLS, C1), right)


def own_entries(rows, lanes):
    at = lax.rem(lax.broadcasted_iota(jnp.int32, (rows, lanes), 0), Q)
    return (at >= PAD) & (at < PAD + OWN)


def sums(values, mask):
    kept = jnp.where(mask, values, 0.0)
    return jnp.sum(kept, axis=0, keepdims=True), jnp.sum(kept * kept, axis=0, keepdims=True)


FRAME_TERMS = [[(0, 4)], [(0, 3), (1, 2)], [(0, 0), (1, 1), (2, 2)], [(1, 0), (2, 1), (3, 2)]]


def middle_kernel(planes, table, hidden, stats):
    mask = own_entries((ROWS - 2) * Q, 2 * C1)
    stats[...] = jnp.zeros(stats.shape, F32)
    for t, terms in enumerate(FRAME_TERMS):
        for odd in range(2):
            lanes = slice(2 * C1 * odd, 2 * C1 * odd + 4 * C1)

            def tap(b):
                low, high = max(b - 1, 0), ROWS + min(b - 1, 0)
                value = None
                for f, s in terms:
                    left = planes[f, low:high, :, lanes].reshape((high - low) * Q, 4 * C1)
                    base = (3 * s + b) * 4 * C1
                    part = mm(left, table[base : base + 4 * C1, :])
                    value = part if value is None else value + part
                return value

            up, here, down = tap(0), tap(1), tap(2)
            first = here[:Q] + down[:Q]
            last = here[-Q:] + up[-Q:]
            inside = here[Q:-Q] + up[:-Q] + down[Q:]
            at = slice(odd * Q, (odd + 1) * Q)
            hidden[t, 0, at, :] = first
            hidden[t, 1 : ROWS - 1, at, :] = inside.reshape(ROWS - 2, Q, 2 * C1)
            hidden[t, ROWS - 1, at, :] = last
            one, two = sums(inside, mask)
            stats[0:1, :] += one
            stats[1:2, :] += two


def middle(planes, table):
    return pl.pallas_call(
        middle_kernel,
        out_shape=(
            shape((FRAMES, ROWS, 2 * Q, 2 * C1), F32),
            shape((8, 2 * C1), F32),
        ),
        in_specs=[VMEM] * 2,
        out_specs=(VMEM,) * 2,
        compiler_params=params(12),
        cost_estimate=cost(6e9, 10e6),
        name="middle",
    )(planes, table)


def group_totals(values, per):
    lane = lax.broadcasted_iota(jnp.int32, (8, 128), 1)
    step = 1
    while step < per:
        other = jnp.where((lane & step) == 0, pltpu.roll(values, 128 - step, 1), pltpu.roll(values, step, 1))
        values = values + other
        step *= 2
    return values


def slots(per):
    lane = lax.broadcasted_iota(jnp.int32, (8, 128), 1)
    return (lane & (per - 1)) == lax.broadcasted_iota(jnp.int32, (8, 128), 0)


def grouped(one, two):
    channels = one.shape[1]
    per = channels // GROUPS
    lines = []
    for low in range(0, channels, 128):
        lines += [one[:, low : low + 128], two[:, low : low + 128]]
    lines += [jnp.zeros((1, 128), F32)] * (8 - len(lines))
    totals = group_totals(jnp.concatenate(lines, axis=0), per)
    return jnp.sum(jnp.where(slots(per), totals, 0.0), axis=0, keepdims=True)


def norm_terms(gathered, gain, shift, members):
    channels = gain.shape[1]
    per = channels // GROUPS
    total = jnp.broadcast_to(jnp.sum(gathered[...], axis=0, keepdims=True), (8, 128))
    lane = lax.broadcasted_iota(jnp.int32, (8, 128), 1)
    source = lane - (lane & (per - 1)) + (lax.broadcasted_iota(jnp.int32, (8, 128), 0) & (per - 1))
    lines = jnp.take_along_axis(total, source, axis=1) / members
    count = channels // 128
    mean = jnp.concatenate([lines[2 * i : 2 * i + 1] for i in range(count)], axis=1)
    square = jnp.concatenate([lines[2 * i + 1 : 2 * i + 2] for i in range(count)], axis=1)
    variance = jnp.maximum(square - mean * mean, 0.0)
    factor = gain[...] / jnp.sqrt(variance + EPSILON)
    return 0.5 * factor, 0.5 * (shift[...] - mean * factor)


def edges_kernel(above, below, table, inner, stats, hidden, share, up, down):
    mask = own_entries(2 * Q, 2 * C1)
    total = [stats[0:1, :], stats[1:2, :]]
    first_row, last_row, _, _ = position()
    for side, (ref, b, end) in enumerate(((above, 0, first_row), (below, 2, last_row))):
        inside = 1.0 - end.astype(F32)
        lines = []
        for t in range(FRAMES):
            wide = ref[t].astype(F32) * inside
            whole = wide.astype(BF16)
            first = pltpu.roll(wide[:, 3 * C1 :], 1, 0).astype(BF16)
            last = pltpu.roll(wide[:, :C1], Q - 1, 0).astype(BF16)
            even = jnp.concatenate([first, whole[:, : 3 * C1]], axis=1)
            odd = jnp.concatenate([whole[:, C1:], last], axis=1)
            lines.append(jnp.concatenate([even, odd], axis=0))

        def part(s, frames):
            base = s * 12 * C1 + b * 4 * C1
            value = mm(jnp.concatenate([lines[t] for t in frames], axis=0), table[base : base + 4 * C1, :])
            return [value[i * 2 * Q : (i + 1) * 2 * Q] for i in range(len(frames))]

        zero, one, two = part(0, (0, 1)), part(1, (1, 2)), part(2, (1, 2, 3))
        pair, all_three = part(3, (0,)), part(4, (0,))
        extra = [all_three[0], pair[0] + two[0], zero[0] + one[0] + two[1], zero[1] + one[1] + two[2]]
        for t in range(FRAMES):
            value = inner[t, side * (ROWS - 1)] + extra[t]
            hidden[t, side] = value
            if side == 0:
                up[t, 0] = value.astype(BF16)
            else:
                down[t, 1] = value.astype(BF16)
            first, second = sums(value, mask)
            total[0] += first
            total[1] += second
    for t in range(FRAMES):
        up[t, 1] = inner[t, 1].astype(BF16)
        up[t, 2] = inner[t, 2].astype(BF16)
        down[t, 0] = inner[t, ROWS - 2].astype(BF16)
    one, two = (v[:, :C1] + v[:, C1:] for v in total)
    share[...] = jnp.broadcast_to(grouped(one, two), share.shape)


def edges(above, below, table, inner, stats, devices):
    return pl.pallas_call(
        edges_kernel,
        out_shape=(
            shape((FRAMES, 2, 2 * Q, 2 * C1), F32),
            shape((devices, 128), F32),
            shape((FRAMES, 3, 2 * Q, 2 * C1), BF16),
            shape((FRAMES, 2, 2 * Q, 2 * C1), BF16),
        ),
        in_specs=[VMEM] * 5,
        out_specs=(VMEM,) * 4,
        compiler_params=params(12),
        cost_estimate=cost(2e9, 10e6),
        name="edges",
    )(above, below, table, inner, stats)


def kept(entry_out, edge):
    return 1.0 - jnp.where(entry_out, edge.astype(F32), 0.0)


def activate(values, terms):
    half = values * terms[0] + terms[1]
    return half + half * jnp.tanh(half)


def twice(terms):
    return tuple(jnp.concatenate([v, v], axis=1) for v in terms)


def raised(values):
    return pltpu.roll(values, Q - 1, 0)


def lowered(values):
    return pltpu.roll(values, 1, 0)


def second_kernel(
    inner, outer, above, below, gathered, gain, shift, reduce, second,
    hidden, share, up, act, lev, summed, *, members,
):
    first_row, last_row, first_col, last_col = position()
    terms = twice(norm_terms(gathered, gain, shift, members))
    entry = lax.broadcasted_iota(jnp.int32, (Q, 1), 0)
    right = kept(entry >= PAD + OWN, last_col)
    outside = right * kept(entry < PAD, first_col)
    below_in = 1.0 - last_row.astype(F32)
    above_in = 1.0 - first_row.astype(F32)

    def line(t, k, value):
        keep = right * below_in if k >= 10 else right
        a = activate(value[:Q].astype(F32), terms) * keep
        b = activate(value[Q:].astype(F32), terms) * keep
        act[t, k, 0:Q, 0 : 2 * C1] = a.astype(BF16)
        act[t, k, 0:Q, 2 * C1 :] = b[:, :C1].astype(BF16)
        act[t, k, Q:, 0 : 2 * C1] = b.astype(BF16)
        act[t, k, Q:, 2 * C1 :] = raised(a[:, :C1]).astype(BF16)

    def lines(t, carry):
        line(t, 0, above[t, 0])
        line(t, 1, above[t, 1])
        line(t, 2, outer[t, 0])
        for r in range(1, ROWS - 1):
            line(t, 2 + r, inner[t, r])
        line(t, 9, outer[t, 1])
        for r in range(3):
            line(t, 10 + r, below[t, r])
        value = None
        for b in range(3):
            left = jnp.concatenate([act[t, 2 * i + b] for i in range(6)], axis=0)
            part = mm(left, reduce[b * 3 * C1 : (b + 1) * 3 * C1, :])
            value = part if value is None else value + part
        for i in range(6):
            keep = outside
            if i == 0:
                keep = keep * above_in
            if i == 5:
                keep = keep * below_in
            even = value[i * 2 * Q : i * 2 * Q + Q] * keep
            odd = value[i * 2 * Q + Q : (i + 1) * 2 * Q] * keep
            e, o = even.astype(BF16), odd.astype(BF16)
            lev[t, i, 0:Q, 0:C2] = lowered(odd).astype(BF16)
            lev[t, i, 0:Q, C2 : 2 * C2] = e
            lev[t, i, 0:Q, 2 * C2 :] = o
            lev[t, i, Q:, 0:C2] = e
            lev[t, i, Q:, C2 : 2 * C2] = o
            lev[t, i, Q:, 2 * C2 :] = raised(even).astype(BF16)
        return carry

    lax.fori_loop(0, FRAMES, lines, 0, unroll=True)

    def add(i, carry):
        at = pl.ds(pl.multiple_of(i * C2, C2), C2)
        pair = second[0, at, :].astype(F32) + second[1, at, :].astype(F32)
        summed[0, at, :] = pair.astype(BF16)
        summed[1, at, :] = (pair + second[2, at, :].astype(F32)).astype(BF16)
        return carry

    lax.fori_loop(0, 9, add, 0, unroll=True)
    rows = 4 * 2 * Q
    mask = own_entries(rows, C2)
    total = [jnp.zeros((1, C2), F32), jnp.zeros((1, C2), F32)]

    def frame(t):
        return jnp.concatenate([lev[t, b : b + 4].reshape(rows, 3 * C2) for b in range(3)], axis=1)

    def store(t, value):
        full = value.reshape(4, 2 * Q, C2)
        hidden[t] = full
        up[t] = full[0].astype(BF16)
        one, two = sums(value, mask)
        total[0] += one
        total[1] += two

    for t, terms in enumerate(FRAME_TERMS):
        value = None
        for f, s in terms:
            part = mm(frame(f), second[s] if s < 3 else summed[s - 3])
            value = part if value is None else value + part
        store(t, value)
    share[...] = jnp.broadcast_to(grouped(*total), share.shape)


def second_level(inner, outer, above, below, gathered, gain, shift, reduce, second, devices):
    return pl.pallas_call(
        functools.partial(second_kernel, members=float(devices * FRAMES * ROWS * COLS * (C1 // GROUPS))),
        out_shape=(
            shape((FRAMES, 4, 2 * Q, C2), F32),
            shape((devices, 128), F32),
            shape((FRAMES, 2 * Q, C2), BF16),
        ),
        in_specs=[VMEM] * 9,
        out_specs=(VMEM,) * 3,
        scratch_shapes=[
            pltpu.VMEM((FRAMES, 14, 2 * Q, 3 * C1), BF16),
            pltpu.VMEM((FRAMES, 6, 2 * Q, 3 * C2), BF16),
            pltpu.VMEM((2, 9 * C2, C2), BF16),
        ],
        compiler_params=params(20),
        cost_estimate=cost(6e9, 12e6),
        name="second",
    )(
        inner, outer, above, below, gathered,
        gain.reshape(1, C1), shift.reshape(1, C1),
        reduce.reshape(9 * C1, C2), second.reshape(3, 9 * C2, C2),
    )


def third_kernel(inner, below, gathered, gain, shift, reduce, level, share, top, bottom, act, *, members):
    _, last_row, _, last_col = position()
    terms = norm_terms(gathered, gain, shift, members)
    entry = lax.broadcasted_iota(jnp.int32, (Q, 1), 0)
    right = kept(entry >= PAD + OWN, last_col)
    below_in = 1.0 - last_row.astype(F32)

    def line(t, k, value):
        keep = right * below_in if k == 4 else right
        even = activate(value[:Q].astype(F32), terms) * keep
        odd = activate(value[Q:].astype(F32), terms) * keep
        act[t, k, :, 0:C2] = even.astype(BF16)
        act[t, k, :, C2 : 2 * C2] = odd.astype(BF16)
        act[t, k, :, 2 * C2 :] = raised(even).astype(BF16)

    for t in range(FRAMES):
        for r in range(4):
            line(t, r, inner[t, r])
        line(t, 4, below[t])
    value = None
    for b in range(3):
        left = jnp.concatenate([act[t, 2 * i + b] for t in range(FRAMES) for i in range(2)], axis=0)
        part = mm(left, reduce[b * 3 * C2 : (b + 1) * 3 * C2, :])
        value = part if value is None else value + part
    rounded = value.astype(BF16)
    level[...] = rounded.reshape(FRAMES, 2, Q, C3)
    for t in range(FRAMES):
        top[t] = rounded[2 * t * Q : (2 * t + 1) * Q]
        bottom[t] = rounded[(2 * t + 1) * Q : (2 * t + 2) * Q]
    one, two = sums(rounded.astype(F32), own_entries(FRAMES * 2 * Q, C3))
    share[...] = jnp.broadcast_to(grouped(one, two), share.shape)


def third_level(inner, below, gathered, gain, shift, reduce, devices):
    return pl.pallas_call(
        functools.partial(third_kernel, members=float(devices * FRAMES * 4 * 2 * OWN * (C2 // GROUPS))),
        out_shape=(
            shape((FRAMES, 2, Q, C3), BF16),
            shape((devices, 128), F32),
            shape((FRAMES, Q, C3), BF16),
            shape((FRAMES, Q, C3), BF16),
        ),
        in_specs=[VMEM] * 6,
        out_specs=(VMEM,) * 4,
        scratch_shapes=[pltpu.VMEM((FRAMES, 5, Q, 3 * C2), BF16)],
        compiler_params=params(12),
        cost_estimate=cost(1e9, 8e6),
        name="third",
    )(inner, below, gathered, gain.reshape(1, C2), shift.reshape(1, C2), reduce.reshape(9 * C2, C3))


def last_kernel(level, above, below, gathered, gain, shift, table, result, act, *, members):
    first_row, last_row, first_col, last_col = position()
    terms = norm_terms(gathered, gain, shift, members)
    entry = lax.broadcasted_iota(jnp.int32, (Q, 1), 0)
    outside = kept(entry >= PAD + OWN, last_col) * kept(entry < PAD, first_col)
    below_in = 1.0 - last_row.astype(F32)
    above_in = 1.0 - first_row.astype(F32)
    for t in range(FRAMES):
        for i in range(4):
            keep = outside
            if i == 0:
                keep = keep * above_in
            if i == 3:
                keep = keep * below_in
            value = above[t] if i == 0 else below[t] if i == 3 else level[t, i - 1]
            v = activate(value.astype(F32), terms) * keep
            act[t, i, :, 0:C3] = lowered(v).astype(BF16)
            act[t, i, :, C3 : 2 * C3] = v.astype(BF16)
            act[t, i, :, 2 * C3 :] = raised(v).astype(BF16)
    value = None
    for b in range(3):
        for e in range(3):
            lanes = slice(e * C3, (e + 1) * C3)
            left = jnp.concatenate([act[t, i + b, :, lanes] for t in range(FRAMES) for i in range(2)], axis=0)
            right = jnp.concatenate([table[a, 3 * b + e] for a in range(3)], axis=0)
            part = lax.dot_general(left, right, (((1,), (1,)), ((), ())), preferred_element_type=F32)
            value = part if value is None else value + part

    def tap(t, a):
        at = 2 * Q * max(t, 0)
        return value[at : at + 2 * Q, a * OUT : (a + 1) * OUT]

    side = jnp.concatenate([tap(t - 2, 0) + tap(t - 1, 1) + tap(t, 2) for t in range(FRAMES)], axis=1).T
    for t in range(FRAMES):
        for i in range(2):
            at = i * Q + PAD
            result[t, i] = side[t * OUT : (t + 1) * OUT, at : at + OWN].astype(BF16)


def last_level(level, above, below, gathered, gain, shift, table, devices):
    swapped = jnp.swapaxes(table, 3, 4).reshape(3, 9, OUT, C3)
    out = pl.pallas_call(
        functools.partial(last_kernel, members=float(devices * FRAMES * 2 * OWN * (C3 // GROUPS))),
        out_shape=shape((FRAMES, 2, OUT, OWN), BF16),
        in_specs=[VMEM] * 7,
        out_specs=VMEM,
        scratch_shapes=[pltpu.VMEM((FRAMES, 4, Q, 3 * C3), BF16)],
        compiler_params=params(10),
        cost_estimate=cost(1e9, 4e6),
        name="last",
    )(level, above, below, gathered, gain.reshape(1, C3), shift.reshape(1, C3), swapped)
    return jnp.swapaxes(out, 2, 3)


def forward(axis):
    return [(i, (i + 1) % lax.axis_size(axis)) for i in range(lax.axis_size(axis))]


def backward(axis):
    return [((i + 1) % lax.axis_size(axis), i) for i in range(lax.axis_size(axis))]


def from_both(last, first, axis):
    return lax.ppermute(last, axis, forward(axis)), lax.ppermute(first, axis, backward(axis))


def everywhere(share):
    return lax.all_to_all(share, AXES, 0, 0, tiled=True)


def shards(
    features, conv_first, first_reduce_kernel, conv_second, second_reduce_kernel, conv_last,
    gain_first, shift_first, gain_second, shift_second, gain_third, shift_third,
):
    devices = lax.axis_size("rows") * lax.axis_size("cols")
    left, right = from_both(*cut(features), "cols")
    table = weights(conv_first)
    planes, top, bottom = planes_of(left, features, right)
    above, below = from_both(bottom, top, "rows")
    inner, stats = middle(planes, table)
    outer, share, up, down = edges(above, below, table, inner, stats, devices)
    above, below = from_both(down, up, "rows")
    hidden, share, up = second_level(
        inner, outer, above, below, everywhere(share), gain_first, shift_first,
        first_reduce_kernel, conv_second, devices,
    )
    below = lax.ppermute(up, "rows", backward("rows"))
    level, share, top, bottom = third_level(
        hidden, below, everywhere(share), gain_second, shift_second, second_reduce_kernel, devices
    )
    above, below = from_both(bottom, top, "rows")
    return last_level(level, above, below, everywhere(share), gain_third, shift_third, conv_last, devices)


def solution(mesh):
    return jax.shard_map(
        shards,
        mesh=mesh,
        in_specs=(P(None, "rows", "cols", None),) + (P(),) * 11,
        out_specs=P(None, "rows", "cols", None),
        check_vma=False,
    )
```

```python
import functools

import jax
import jax.numpy as jnp
from jax import lax
from jax.experimental import pallas as pl
from jax.experimental.pallas import tpu as pltpu
from jax.sharding import PartitionSpec as P

GROUPS = 32
EPSILON = 1e-6
FRAMES = 4
ROWS = 8
COLS = 160
C1, C2, C3, OUT = 128, 256, 512, 32
Q = 48
PAD = 2
OWN = COLS // 4
EDGE = 16
LINE = 208
K0, MINUS, K2, PAIR, ALL = range(5)
AXES = ("rows", "cols")
F32, BF16 = jnp.float32, jnp.bfloat16
VMEM = pl.BlockSpec(memory_space=pltpu.VMEM)
HBM = pl.BlockSpec(memory_space=pltpu.HBM)


def params(mib):
    return pltpu.CompilerParams(vmem_limit_bytes=mib * 1024 * 1024)


def cost(flops, read):
    return pl.CostEstimate(flops=int(flops), bytes_accessed=int(read), transcendentals=0)


def shape(dims, dtype):
    return jax.ShapeDtypeStruct(dims, dtype)


def mm(left, right):
    return jnp.dot(left, right, preferred_element_type=F32)


def position():
    row, col = lax.axis_index("rows"), lax.axis_index("cols")
    return row == 0, row == lax.axis_size("rows") - 1, col == 0, col == lax.axis_size("cols") - 1


def weights_kernel(first, one):
    zero = jnp.zeros((C1, C1), BF16)
    for b in range(3):
        for e in range(3):
            taps = [first[((a * 3 + b) * 3 + e) * C1 : ((a * 3 + b) * 3 + e + 1) * C1, :] for a in range(3)]
            wide = [k.astype(F32) for k in taps]
            pair, ends = wide[0] + wide[1], wide[0] + wide[2]
            made = [v.astype(BF16) for v in (ends - wide[1], pair, pair + wide[2])]
            for s, k in enumerate([taps[0], made[0], taps[2], made[1], made[2]]):
                base = s * 12 * C1 + b * 4 * C1
                one[base + e * C1 : base + (e + 1) * C1, 0:C1] = k
                one[base + (e + 1) * C1 : base + (e + 2) * C1, C1 : 2 * C1] = k
        for s in range(5):
            base = s * 12 * C1 + b * 4 * C1
            one[base + 3 * C1 : base + 4 * C1, 0:C1] = zero
            one[base : base + C1, C1 : 2 * C1] = zero


def weights(first):
    return pl.pallas_call(
        weights_kernel,
        out_shape=shape((5 * 12 * C1, 2 * C1), BF16),
        in_specs=[VMEM],
        out_specs=VMEM,
        compiler_params=params(8),
        cost_estimate=cost(0, 5e6),
        name="weights",
    )(first.reshape(27 * C1, C1))


def cut_kernel(features, last, first, sem):
    copies = [
        pltpu.make_async_copy(features.at[:, pl.ds(COLS - EDGE, EDGE)], last, sem.at[0]),
        pltpu.make_async_copy(features.at[:, pl.ds(0, EDGE)], first, sem.at[1]),
    ]
    for c in copies:
        c.start()
    for c in copies:
        c.wait()


def cut(features):
    edge = shape((FRAMES * ROWS, EDGE, C1), BF16)
    return pl.pallas_call(
        cut_kernel,
        out_shape=(edge, edge),
        in_specs=[HBM],
        out_specs=(VMEM,) * 2,
        scratch_shapes=[pltpu.SemaphoreType.DMA((2,))],
        compiler_params=params(4),
        cost_estimate=cost(0, 4e5),
        name="cut",
    )(features.reshape(FRAMES * ROWS, COLS, C1))


def planes_kernel(left, own, right, planes, top, bottom, line):
    _, _, first_col, last_col = position()
    left_in = 1.0 - first_col.astype(F32)
    right_in = 1.0 - last_col.astype(F32)
    for t in range(FRAMES):

        def step(r, carry, t=t):
            i = t * ROWS + r
            line[i, 0:EDGE, :] = left[i].astype(F32) * left_in
            line[i, EDGE : EDGE + COLS, :] = own[i].astype(F32)
            line[i, EDGE + COLS : 2 * EDGE + COLS, :] = right[i].astype(F32) * right_in
            line[i, 2 * EDGE + COLS : LINE, :] = jnp.zeros((LINE - 2 * EDGE - COLS, C1), F32)
            for k in range(6):
                planes[t, r, :, k * C1 : (k + 1) * C1] = line[i, pl.ds(7 + k, Q, stride=4), :].astype(BF16)
            return carry

        lax.fori_loop(0, ROWS, step, 0, unroll=True)
        top[t] = planes[t, 0, :, C1 : 5 * C1]
        bottom[t] = planes[t, ROWS - 1, :, C1 : 5 * C1]


def planes_of(left, own, right):
    lines = FRAMES * ROWS
    return pl.pallas_call(
        planes_kernel,
        out_shape=(
            shape((FRAMES, ROWS, Q, 6 * C1), BF16),
            shape((FRAMES, Q, 4 * C1), BF16),
            shape((FRAMES, Q, 4 * C1), BF16),
        ),
        in_specs=[VMEM] * 3,
        out_specs=(VMEM,) * 3,
        scratch_shapes=[pltpu.VMEM((lines, LINE, C1), F32)],
        compiler_params=params(12),
        cost_estimate=cost(0, 4e6),
        name="planes",
    )(left, own.reshape(lines, COLS, C1), right)


def own_entries(rows, lanes):
    at = lax.rem(lax.broadcasted_iota(jnp.int32, (rows, lanes), 0), Q)
    return (at >= PAD) & (at < PAD + OWN)


def sums(values, mask):
    kept = jnp.where(mask, values, 0.0)
    return jnp.sum(kept, axis=0, keepdims=True), jnp.sum(kept * kept, axis=0, keepdims=True)


def mixed(one):
    return one[0] - one[2], one[1] + one[2], one[2] - one[1], one[1] - one[3]


def causal(product, frames, mix):
    yield product(frames[0], ALL)
    yield product(frames[0], PAIR) + product(frames[1], K2)
    plus, minus = product(mix[1], ALL), product(mix[2], MINUS)
    yield product(mix[0], K0) + 0.5 * (plus + minus)
    yield 0.5 * (plus - minus) - product(mix[3], K2)


def middle_kernel(planes, table, hidden, stats, mix):
    mask = own_entries((ROWS - 2) * Q, 2 * C1)
    stats[...] = jnp.zeros(stats.shape, F32)
    for i, value in enumerate(mixed([planes[t] for t in range(FRAMES)])):
        mix[i] = value
    for odd in range(2):
        lanes = slice(2 * C1 * odd, 2 * C1 * odd + 4 * C1)
        at = slice(odd * Q, (odd + 1) * Q)

        def product(v, s):
            def tap(b):
                low, high = max(b - 1, 0), ROWS + min(b - 1, 0)
                left = v[0][v[1], low:high, :, lanes].reshape((high - low) * Q, 4 * C1)
                base = (3 * s + b) * 4 * C1
                return mm(left, table[base : base + 4 * C1, :])

            up, here, down = tap(0), tap(1), tap(2)
            return jnp.concatenate([here[:Q] + down[:Q], here[Q:-Q] + up[:-Q] + down[Q:], here[-Q:] + up[-Q:]], axis=0)

        for t, value in enumerate(causal(product, [(planes, t) for t in range(FRAMES)], [(mix, i) for i in range(4)])):
            hidden[t, :, at, :] = value.reshape(ROWS, Q, 2 * C1)
            one, two = sums(value[Q:-Q], mask)
            stats[0:1, :] += one
            stats[1:2, :] += two


def middle(planes, table):
    return pl.pallas_call(
        middle_kernel,
        out_shape=(
            shape((FRAMES, ROWS, 2 * Q, 2 * C1), F32),
            shape((8, 2 * C1), F32),
        ),
        in_specs=[VMEM] * 2,
        out_specs=(VMEM,) * 2,
        scratch_shapes=[pltpu.VMEM((4, ROWS, Q, 6 * C1), BF16)],
        compiler_params=params(12),
        cost_estimate=cost(6e9, 10e6),
        name="middle",
    )(planes, table)


def group_totals(values, per):
    lane = lax.broadcasted_iota(jnp.int32, (8, 128), 1)
    step = 1
    while step < per:
        other = jnp.where((lane & step) == 0, pltpu.roll(values, 128 - step, 1), pltpu.roll(values, step, 1))
        values = values + other
        step *= 2
    return values


def slots(per):
    lane = lax.broadcasted_iota(jnp.int32, (8, 128), 1)
    return (lane & (per - 1)) == lax.broadcasted_iota(jnp.int32, (8, 128), 0)


def grouped(one, two):
    channels = one.shape[1]
    per = channels // GROUPS
    lines = []
    for low in range(0, channels, 128):
        lines += [one[:, low : low + 128], two[:, low : low + 128]]
    lines += [jnp.zeros((1, 128), F32)] * (8 - len(lines))
    totals = group_totals(jnp.concatenate(lines, axis=0), per)
    return jnp.sum(jnp.where(slots(per), totals, 0.0), axis=0, keepdims=True)


def norm_terms(gathered, gain, shift, members):
    channels = gain.shape[1]
    per = channels // GROUPS
    total = jnp.broadcast_to(jnp.sum(gathered[...], axis=0, keepdims=True), (8, 128))
    lane = lax.broadcasted_iota(jnp.int32, (8, 128), 1)
    source = lane - (lane & (per - 1)) + (lax.broadcasted_iota(jnp.int32, (8, 128), 0) & (per - 1))
    lines = jnp.take_along_axis(total, source, axis=1) / members
    count = channels // 128
    mean = jnp.concatenate([lines[2 * i : 2 * i + 1] for i in range(count)], axis=1)
    square = jnp.concatenate([lines[2 * i + 1 : 2 * i + 2] for i in range(count)], axis=1)
    variance = jnp.maximum(square - mean * mean, 0.0)
    factor = gain[...] / jnp.sqrt(variance + EPSILON)
    return 0.5 * factor, 0.5 * (shift[...] - mean * factor)


def edges_kernel(above, below, table, inner, stats, hidden, share, up, down):
    mask = own_entries(2 * Q, 2 * C1)
    total = [stats[0:1, :], stats[1:2, :]]
    first_row, last_row, _, _ = position()
    for side, (ref, b, end) in enumerate(((above, 0, first_row), (below, 2, last_row))):
        inside = 1.0 - end.astype(F32)
        lines = []
        for t in range(FRAMES):
            wide = ref[t].astype(F32) * inside
            whole = wide.astype(BF16)
            first = pltpu.roll(wide[:, 3 * C1 :], 1, 0).astype(BF16)
            last = pltpu.roll(wide[:, :C1], Q - 1, 0).astype(BF16)
            even = jnp.concatenate([first, whole[:, : 3 * C1]], axis=1)
            odd = jnp.concatenate([whole[:, C1:], last], axis=1)
            lines.append(jnp.concatenate([even, odd], axis=0))

        def product(v, s):
            base = s * 12 * C1 + b * 4 * C1
            return mm(v, table[base : base + 4 * C1, :])

        extra = list(causal(product, lines, mixed(lines)))
        for t in range(FRAMES):
            value = inner[t, side * (ROWS - 1)] + extra[t]
            hidden[t, side] = value
            if side == 0:
                up[t, 0] = value.astype(BF16)
            else:
                down[t, 1] = value.astype(BF16)
            first, second = sums(value, mask)
            total[0] += first
            total[1] += second
    for t in range(FRAMES):
        up[t, 1] = inner[t, 1].astype(BF16)
        up[t, 2] = inner[t, 2].astype(BF16)
        down[t, 0] = inner[t, ROWS - 2].astype(BF16)
    one, two = (v[:, :C1] + v[:, C1:] for v in total)
    share[...] = jnp.broadcast_to(grouped(one, two), share.shape)


def edges(above, below, table, inner, stats, devices):
    return pl.pallas_call(
        edges_kernel,
        out_shape=(
            shape((FRAMES, 2, 2 * Q, 2 * C1), F32),
            shape((devices, 128), F32),
            shape((FRAMES, 3, 2 * Q, 2 * C1), BF16),
            shape((FRAMES, 2, 2 * Q, 2 * C1), BF16),
        ),
        in_specs=[VMEM] * 5,
        out_specs=(VMEM,) * 4,
        compiler_params=params(12),
        cost_estimate=cost(2e9, 10e6),
        name="edges",
    )(above, below, table, inner, stats)


def kept(entry_out, edge):
    return 1.0 - jnp.where(entry_out, edge.astype(F32), 0.0)


def activate(values, terms):
    half = values * terms[0] + terms[1]
    return half + half * jnp.tanh(half)


def twice(terms):
    return tuple(jnp.concatenate([v, v], axis=1) for v in terms)


def raised(values):
    return pltpu.roll(values, Q - 1, 0)


def lowered(values):
    return pltpu.roll(values, 1, 0)


def second_kernel(
    inner, outer, above, below, gathered, gain, shift, reduce, second,
    hidden, share, up, down, act, lev, mix, made, *, members,
):
    first_row, last_row, first_col, last_col = position()
    terms = twice(norm_terms(gathered, gain, shift, members))
    entry = lax.broadcasted_iota(jnp.int32, (Q, 1), 0)
    right = kept(entry >= PAD + OWN, last_col)
    outside = right * kept(entry < PAD, first_col)
    below_in = 1.0 - last_row.astype(F32)
    above_in = 1.0 - first_row.astype(F32)

    def line(t, k, value):
        keep = right * below_in if k >= 10 else right
        a = activate(value[:Q].astype(F32), terms) * keep
        b = activate(value[Q:].astype(F32), terms) * keep
        act[t, k, 0:Q, 0 : 2 * C1] = a.astype(BF16)
        act[t, k, 0:Q, 2 * C1 :] = b[:, :C1].astype(BF16)
        act[t, k, Q:, 0 : 2 * C1] = b.astype(BF16)
        act[t, k, Q:, 2 * C1 :] = raised(a[:, :C1]).astype(BF16)

    def lines(t, carry):
        line(t, 0, above[t, 0])
        line(t, 1, above[t, 1])
        line(t, 2, outer[t, 0])
        for r in range(1, ROWS - 1):
            line(t, 2 + r, inner[t, r])
        line(t, 9, outer[t, 1])
        for r in range(3):
            line(t, 10 + r, below[t, r])
        value = None
        for b in range(3):
            left = jnp.concatenate([act[t, 2 * i + b] for i in range(6)], axis=0)
            part = mm(left, reduce[b * 3 * C1 : (b + 1) * 3 * C1, :])
            value = part if value is None else value + part
        for i in range(6):
            keep = outside
            if i == 0:
                keep = keep * above_in
            if i == 5:
                keep = keep * below_in
            even = value[i * 2 * Q : i * 2 * Q + Q] * keep
            odd = value[i * 2 * Q + Q : (i + 1) * 2 * Q] * keep
            e, o = even.astype(BF16), odd.astype(BF16)
            lev[t, i, 0:Q, 0:C2] = lowered(odd).astype(BF16)
            lev[t, i, 0:Q, C2 : 2 * C2] = e
            lev[t, i, 0:Q, 2 * C2 :] = o
            lev[t, i, Q:, 0:C2] = e
            lev[t, i, Q:, C2 : 2 * C2] = o
            lev[t, i, Q:, 2 * C2 :] = raised(even).astype(BF16)
        return carry

    lax.fori_loop(0, FRAMES, lines, 0, unroll=True)

    def add(i, carry):
        at = pl.ds(pl.multiple_of(i * C2, C2), C2)
        k0, k1, k2 = (second[a, at, :].astype(F32) for a in range(3))
        made[0, at, :] = (k0 - k1 + k2).astype(BF16)
        made[1, at, :] = (k0 + k1).astype(BF16)
        made[2, at, :] = (k0 + k1 + k2).astype(BF16)
        return carry

    lax.fori_loop(0, 9, add, 0, unroll=True)
    rows = 4 * 2 * Q
    mask = own_entries(rows, C2)
    total = [jnp.zeros((1, C2), F32), jnp.zeros((1, C2), F32)]

    for i, value in enumerate(mixed([lev[t] for t in range(FRAMES)])):
        mix[i] = value
    tables = {K0: second.at[0], MINUS: made.at[0], K2: second.at[2], PAIR: made.at[1], ALL: made.at[2]}

    def product(v, s):
        left = jnp.concatenate([v[0][v[1], b : b + 4].reshape(rows, 3 * C2) for b in range(3)], axis=1)
        return mm(left, tables[s][...])

    def store(t, value):
        full = value.reshape(4, 2 * Q, C2)
        hidden[t] = full
        up[t] = full[0:3].astype(BF16)
        down[t] = full[2:4].astype(BF16)
        one, two = sums(value, mask)
        total[0] += one
        total[1] += two

    for t, value in enumerate(causal(product, [(lev, t) for t in range(FRAMES)], [(mix, i) for i in range(4)])):
        store(t, value)
    share[...] = jnp.broadcast_to(grouped(*total), share.shape)


def second_level(inner, outer, above, below, gathered, gain, shift, reduce, second, devices):
    return pl.pallas_call(
        functools.partial(second_kernel, members=float(devices * FRAMES * ROWS * COLS * (C1 // GROUPS))),
        out_shape=(
            shape((FRAMES, 4, 2 * Q, C2), F32),
            shape((devices, 128), F32),
            shape((FRAMES, 3, 2 * Q, C2), BF16),
            shape((FRAMES, 2, 2 * Q, C2), BF16),
        ),
        in_specs=[VMEM] * 9,
        out_specs=(VMEM,) * 4,
        scratch_shapes=[
            pltpu.VMEM((FRAMES, 14, 2 * Q, 3 * C1), BF16),
            pltpu.VMEM((FRAMES, 6, 2 * Q, 3 * C2), BF16),
            pltpu.VMEM((4, 6, 2 * Q, 3 * C2), BF16),
            pltpu.VMEM((3, 9 * C2, C2), BF16),
        ],
        compiler_params=params(24),
        cost_estimate=cost(6e9, 12e6),
        name="second",
    )(
        inner, outer, above, below, gathered,
        gain.reshape(1, C1), shift.reshape(1, C1),
        reduce.reshape(9 * C1, C2), second.reshape(3, 9 * C2, C2),
    )


def third_kernel(inner, above, below, gathered, gain, shift, reduce, level, share, act, *, members):
    _, last_row, _, last_col = position()
    terms = norm_terms(gathered, gain, shift, members)
    entry = lax.broadcasted_iota(jnp.int32, (Q, 1), 0)
    right = kept(entry >= PAD + OWN, last_col)
    below_in = 1.0 - last_row.astype(F32)

    def line(t, k, value):
        keep = right * below_in if k >= 6 else right
        even = activate(value[:Q].astype(F32), terms) * keep
        odd = activate(value[Q:].astype(F32), terms) * keep
        act[t, k, :, 0:C2] = even.astype(BF16)
        act[t, k, :, C2 : 2 * C2] = odd.astype(BF16)
        act[t, k, :, 2 * C2 :] = raised(even).astype(BF16)

    def lines(t, carry):
        for r in range(2):
            line(t, r, above[t, r])
        for r in range(4):
            line(t, 2 + r, inner[t, r])
        for r in range(3):
            line(t, 6 + r, below[t, r])
        return carry

    lax.fori_loop(0, FRAMES, lines, 0, unroll=True)
    mask = own_entries(2 * Q, C3)
    total = [jnp.zeros((1, C3), F32), jnp.zeros((1, C3), F32)]
    value = None
    for b in range(3):
        left = jnp.concatenate([act[t, 2 * i + b] for t in range(FRAMES) for i in range(4)], axis=0)
        part = mm(left, reduce[b * 3 * C2 : (b + 1) * 3 * C2, :])
        value = part if value is None else value + part
    rounded = value.astype(BF16)
    level[...] = rounded.reshape(FRAMES, 4, Q, C3)
    wide = rounded.astype(F32)
    for t in range(FRAMES):
        one, two = sums(wide[(4 * t + 1) * Q : (4 * t + 3) * Q], mask)
        total[0] += one
        total[1] += two
    share[...] = jnp.broadcast_to(grouped(*total), share.shape)


def third_level(inner, above, below, gathered, gain, shift, reduce, devices):
    return pl.pallas_call(
        functools.partial(third_kernel, members=float(devices * FRAMES * 4 * 2 * OWN * (C2 // GROUPS))),
        out_shape=(shape((FRAMES, 4, Q, C3), BF16), shape((devices, 128), F32)),
        in_specs=[VMEM] * 7,
        out_specs=(VMEM,) * 2,
        scratch_shapes=[pltpu.VMEM((FRAMES, 10, Q, 3 * C2), BF16)],
        compiler_params=params(12),
        cost_estimate=cost(2e9, 8e6),
        name="third",
    )(inner, above, below, gathered, gain.reshape(1, C2), shift.reshape(1, C2), reduce.reshape(9 * C2, C3))


def last_kernel(level, gathered, gain, shift, table, result, act, *, members):
    first_row, last_row, first_col, last_col = position()
    terms = norm_terms(gathered, gain, shift, members)
    entry = lax.broadcasted_iota(jnp.int32, (Q, 1), 0)
    outside = kept(entry >= PAD + OWN, last_col) * kept(entry < PAD, first_col)
    below_in = 1.0 - last_row.astype(F32)
    above_in = 1.0 - first_row.astype(F32)
    for t in range(FRAMES):
        for i in range(4):
            keep = outside
            if i == 0:
                keep = keep * above_in
            if i == 3:
                keep = keep * below_in
            v = activate(level[t, i].astype(F32), terms) * keep
            act[t, i, :, 0:C3] = lowered(v).astype(BF16)
            act[t, i, :, C3 : 2 * C3] = v.astype(BF16)
            act[t, i, :, 2 * C3 :] = raised(v).astype(BF16)
    value = None
    for b in range(3):
        for e in range(3):
            lanes = slice(e * C3, (e + 1) * C3)
            left = jnp.concatenate([act[t, i + b, :, lanes] for t in range(FRAMES) for i in range(2)], axis=0)
            right = jnp.concatenate([table[a, 3 * b + e] for a in range(3)], axis=0)
            part = lax.dot_general(left, right, (((1,), (1,)), ((), ())), preferred_element_type=F32)
            value = part if value is None else value + part

    def tap(t, a):
        at = 2 * Q * max(t, 0)
        return value[at : at + 2 * Q, a * OUT : (a + 1) * OUT]

    side = jnp.concatenate([tap(t - 2, 0) + tap(t - 1, 1) + tap(t, 2) for t in range(FRAMES)], axis=1).T
    for t in range(FRAMES):
        for i in range(2):
            at = i * Q + PAD
            result[t, i] = side[t * OUT : (t + 1) * OUT, at : at + OWN].astype(BF16)


def last_level(level, gathered, gain, shift, table, devices):
    swapped = jnp.swapaxes(table, 3, 4).reshape(3, 9, OUT, C3)
    out = pl.pallas_call(
        functools.partial(last_kernel, members=float(devices * FRAMES * 2 * OWN * (C3 // GROUPS))),
        out_shape=shape((FRAMES, 2, OUT, OWN), BF16),
        in_specs=[VMEM] * 5,
        out_specs=VMEM,
        scratch_shapes=[pltpu.VMEM((FRAMES, 4, Q, 3 * C3), BF16)],
        compiler_params=params(10),
        cost_estimate=cost(1e9, 4e6),
        name="last",
    )(level, gathered, gain.reshape(1, C3), shift.reshape(1, C3), swapped)
    return jnp.swapaxes(out, 2, 3)


def forward(axis):
    return [(i, (i + 1) % lax.axis_size(axis)) for i in range(lax.axis_size(axis))]


def backward(axis):
    return [((i + 1) % lax.axis_size(axis), i) for i in range(lax.axis_size(axis))]


def from_both(last, first, axis):
    return lax.ppermute(last, axis, forward(axis)), lax.ppermute(first, axis, backward(axis))


def everywhere(share):
    return lax.all_to_all(share, AXES, 0, 0, tiled=True)


def shards(
    features, conv_first, first_reduce_kernel, conv_second, second_reduce_kernel, conv_last,
    gain_first, shift_first, gain_second, shift_second, gain_third, shift_third,
):
    devices = lax.axis_size("rows") * lax.axis_size("cols")
    left, right = from_both(*cut(features), "cols")
    table = weights(conv_first)
    planes, top, bottom = planes_of(left, features, right)
    above, below = from_both(bottom, top, "rows")
    inner, stats = middle(planes, table)
    outer, share, up, down = edges(above, below, table, inner, stats, devices)
    above, below = from_both(down, up, "rows")
    hidden, share, up, down = second_level(
        inner, outer, above, below, everywhere(share), gain_first, shift_first,
        first_reduce_kernel, conv_second, devices,
    )
    above, below = from_both(down, up, "rows")
    level, share = third_level(
        hidden, above, below, everywhere(share), gain_second, shift_second,
        second_reduce_kernel, devices,
    )
    return last_level(level, everywhere(share), gain_third, shift_third, conv_last, devices)


def solution(mesh):
    return jax.shard_map(
        shards,
        mesh=mesh,
        in_specs=(P(None, "rows", "cols", None),) + (P(),) * 11,
        out_specs=P(None, "rows", "cols", None),
        check_vma=False,
    )
```

```python
import functools

import jax
import jax.numpy as jnp
from jax import lax
from jax.experimental import pallas as pl
from jax.experimental.pallas import tpu as pltpu
from jax.sharding import PartitionSpec as P

GROUPS = 32
EPSILON = 1e-6
FRAMES = 4
ROWS = 8
COLS = 160
C1, C2, C3, OUT = 128, 256, 512, 32
Q = 48
PAD = 2
OWN = COLS // 4
EDGE = 16
LINE = 208
K0, MINUS, K2, PAIR, ALL = range(5)
AXES = ("rows", "cols")
F32, BF16 = jnp.float32, jnp.bfloat16
VMEM = pl.BlockSpec(memory_space=pltpu.VMEM)
HBM = pl.BlockSpec(memory_space=pltpu.HBM)


def params(mib):
    return pltpu.CompilerParams(vmem_limit_bytes=mib * 1024 * 1024)


def cost(flops, read):
    return pl.CostEstimate(flops=int(flops), bytes_accessed=int(read), transcendentals=0)


def shape(dims, dtype):
    return jax.ShapeDtypeStruct(dims, dtype)


def mm(left, right):
    return jnp.dot(left, right, preferred_element_type=F32)


def position():
    row, col = lax.axis_index("rows"), lax.axis_index("cols")
    return row == 0, row == lax.axis_size("rows") - 1, col == 0, col == lax.axis_size("cols") - 1


def weights_kernel(first, one):
    zero = jnp.zeros((C1, C1), BF16)
    for b in range(3):
        for e in range(3):
            taps = [first[((a * 3 + b) * 3 + e) * C1 : ((a * 3 + b) * 3 + e + 1) * C1, :] for a in range(3)]
            wide = [k.astype(F32) for k in taps]
            pair, ends = wide[0] + wide[1], wide[0] + wide[2]
            made = [v.astype(BF16) for v in (ends - wide[1], pair, pair + wide[2])]
            for s, k in enumerate([taps[0], made[0], taps[2], made[1], made[2]]):
                base = s * 12 * C1 + b * 4 * C1
                one[base + e * C1 : base + (e + 1) * C1, 0:C1] = k
                one[base + (e + 1) * C1 : base + (e + 2) * C1, C1 : 2 * C1] = k
        for s in range(5):
            base = s * 12 * C1 + b * 4 * C1
            one[base + 3 * C1 : base + 4 * C1, 0:C1] = zero
            one[base : base + C1, C1 : 2 * C1] = zero


def weights(first):
    return pl.pallas_call(
        weights_kernel,
        out_shape=shape((5 * 12 * C1, 2 * C1), BF16),
        in_specs=[VMEM],
        out_specs=VMEM,
        compiler_params=params(8),
        cost_estimate=cost(0, 5e6),
        name="weights",
    )(first.reshape(27 * C1, C1))


def cut_kernel(features, last, first, bottom, top, sem):
    def copy(i, source, target):
        return pltpu.make_async_copy(source, target, sem.at[i])

    copies = [
        copy(0, features.at[:, :, pl.ds(COLS - EDGE, EDGE)], last),
        copy(1, features.at[:, :, pl.ds(0, EDGE)], first),
        copy(2, features.at[:, ROWS - 1], bottom),
        copy(3, features.at[:, 0], top),
    ]
    for c in copies:
        c.start()
    for c in copies:
        c.wait()


def cut(features):
    edge, line = shape((FRAMES, ROWS, EDGE, C1), BF16), shape((FRAMES, COLS, C1), BF16)
    return pl.pallas_call(
        cut_kernel,
        out_shape=(edge, edge, line, line),
        in_specs=[HBM],
        out_specs=(VMEM,) * 4,
        scratch_shapes=[pltpu.SemaphoreType.DMA((4,))],
        compiler_params=params(4),
        cost_estimate=cost(0, 4e5),
        name="cut",
    )(features)


def lay(line, left, own, right):
    line[0:EDGE, :] = left
    line[EDGE : EDGE + COLS, :] = own
    line[EDGE + COLS : 2 * EDGE + COLS, :] = right
    line[2 * EDGE + COLS : LINE, :] = jnp.zeros((LINE - 2 * EDGE - COLS, C1), F32)


def plane(line, k):
    return line[pl.ds(7 + k, Q, stride=4), :].astype(BF16)


def planes_kernel(left, own, right, planes, top, bottom, line):
    _, _, first_col, last_col = position()
    left_in = 1.0 - first_col.astype(F32)
    right_in = 1.0 - last_col.astype(F32)
    for t in range(FRAMES):
        for r in range(ROWS):
            before = left[t, r].astype(F32) * left_in
            after = right[t, r].astype(F32) * right_in
            at = line.at[t * ROWS + r]
            lay(at, before, own[t, r].astype(F32), after)
            for k in range(6):
                planes[t, r, :, k * C1 : (k + 1) * C1] = plane(at, k)
            if r in (0, ROWS - 1):
                corner = top if r == 0 else bottom
                corner[t, 0] = before.astype(BF16)
                corner[t, 1] = after.astype(BF16)


def planes_of(left, own, right):
    corner = shape((FRAMES, 2, EDGE, C1), BF16)
    return pl.pallas_call(
        planes_kernel,
        out_shape=(shape((FRAMES, ROWS, Q, 6 * C1), BF16), corner, corner),
        in_specs=[VMEM] * 3,
        out_specs=(VMEM,) * 3,
        scratch_shapes=[pltpu.VMEM((FRAMES * ROWS, LINE, C1), F32)],
        compiler_params=params(12),
        cost_estimate=cost(0, 4e6),
        name="planes",
    )(left, own, right)


def own_entries(rows, lanes):
    at = lax.rem(lax.broadcasted_iota(jnp.int32, (rows, lanes), 0), Q)
    return (at >= PAD) & (at < PAD + OWN)


def sums(values, mask):
    kept = jnp.where(mask, values, 0.0)
    return jnp.sum(kept, axis=0, keepdims=True), jnp.sum(kept * kept, axis=0, keepdims=True)


def mixed(one):
    return one[0] - one[2], one[1] + one[2], one[2] - one[1], one[1] - one[3]


def causal(product, frames, mix):
    yield product(frames[0], ALL)
    yield product(frames[0], PAIR) + product(frames[1], K2)
    plus, minus = product(mix[1], ALL), product(mix[2], MINUS)
    yield product(mix[0], K0) + 0.5 * (plus + minus)
    yield 0.5 * (plus - minus) - product(mix[3], K2)


def middle_kernel(planes, table, hidden, stats, mix):
    mask = own_entries((ROWS - 2) * Q, 2 * C1)
    stats[...] = jnp.zeros(stats.shape, F32)
    for i, value in enumerate(mixed([planes[t] for t in range(FRAMES)])):
        mix[i] = value
    for odd in range(2):
        lanes = slice(2 * C1 * odd, 2 * C1 * odd + 4 * C1)
        at = slice(odd * Q, (odd + 1) * Q)

        def product(v, s):
            def tap(b):
                low, high = max(b - 1, 0), ROWS + min(b - 1, 0)
                left = v[0][v[1], low:high, :, lanes].reshape((high - low) * Q, 4 * C1)
                base = (3 * s + b) * 4 * C1
                return mm(left, table[base : base + 4 * C1, :])

            up, here, down = tap(0), tap(1), tap(2)
            return jnp.concatenate([here[:Q] + down[:Q], here[Q:-Q] + up[:-Q] + down[Q:], here[-Q:] + up[-Q:]], axis=0)

        for t, value in enumerate(causal(product, [(planes, t) for t in range(FRAMES)], [(mix, i) for i in range(4)])):
            hidden[t, :, at, :] = value.reshape(ROWS, Q, 2 * C1)
            one, two = sums(value[Q:-Q], mask)
            stats[0:1, :] += one
            stats[1:2, :] += two


def middle(planes, table):
    return pl.pallas_call(
        middle_kernel,
        out_shape=(
            shape((FRAMES, ROWS, 2 * Q, 2 * C1), F32),
            shape((8, 2 * C1), F32),
        ),
        in_specs=[VMEM] * 2,
        out_specs=(VMEM,) * 2,
        scratch_shapes=[pltpu.VMEM((4, ROWS, Q, 6 * C1), BF16)],
        compiler_params=params(12),
        cost_estimate=cost(6e9, 10e6),
        name="middle",
    )(planes, table)


def group_totals(values, per):
    lane = lax.broadcasted_iota(jnp.int32, (8, 128), 1)
    step = 1
    while step < per:
        other = jnp.where((lane & step) == 0, pltpu.roll(values, 128 - step, 1), pltpu.roll(values, step, 1))
        values = values + other
        step *= 2
    return values


def slots(per):
    lane = lax.broadcasted_iota(jnp.int32, (8, 128), 1)
    return (lane & (per - 1)) == lax.broadcasted_iota(jnp.int32, (8, 128), 0)


def grouped(one, two):
    channels = one.shape[1]
    per = channels // GROUPS
    lines = []
    for low in range(0, channels, 128):
        lines += [one[:, low : low + 128], two[:, low : low + 128]]
    lines += [jnp.zeros((1, 128), F32)] * (8 - len(lines))
    totals = group_totals(jnp.concatenate(lines, axis=0), per)
    return jnp.sum(jnp.where(slots(per), totals, 0.0), axis=0, keepdims=True)


def norm_terms(gathered, gain, shift, members):
    channels = gain.shape[1]
    per = channels // GROUPS
    total = jnp.broadcast_to(jnp.sum(gathered[...], axis=0, keepdims=True), (8, 128))
    lane = lax.broadcasted_iota(jnp.int32, (8, 128), 1)
    source = lane - (lane & (per - 1)) + (lax.broadcasted_iota(jnp.int32, (8, 128), 0) & (per - 1))
    lines = jnp.take_along_axis(total, source, axis=1) / members
    count = channels // 128
    mean = jnp.concatenate([lines[2 * i : 2 * i + 1] for i in range(count)], axis=1)
    square = jnp.concatenate([lines[2 * i + 1 : 2 * i + 2] for i in range(count)], axis=1)
    variance = jnp.maximum(square - mean * mean, 0.0)
    factor = gain[...] / jnp.sqrt(variance + EPSILON)
    return 0.5 * factor, 0.5 * (shift[...] - mean * factor)


def edges_kernel(
    above, below, corners_above, corners_below, table, inner, stats, hidden, share, up, down, line
):
    mask = own_entries(2 * Q, 2 * C1)
    total = [stats[0:1, :], stats[1:2, :]]
    first_row, last_row, _, _ = position()
    sides = ((above, corners_above, 0, first_row), (below, corners_below, 2, last_row))
    for side, (ref, corner, b, end) in enumerate(sides):
        inside = 1.0 - end.astype(F32)
        lines = []
        for t in range(FRAMES):
            at = line.at[side * FRAMES + t]
            lay(at, *(v.astype(F32) * inside for v in (corner[t, 0], ref[t], corner[t, 1])))
            parts = [plane(at, k) for k in range(6)]
            even = jnp.concatenate(parts[:4], axis=1)
            odd = jnp.concatenate(parts[2:], axis=1)
            lines.append(jnp.concatenate([even, odd], axis=0))

        def product(v, s):
            base = s * 12 * C1 + b * 4 * C1
            return mm(v, table[base : base + 4 * C1, :])

        extra = list(causal(product, lines, mixed(lines)))
        for t in range(FRAMES):
            value = inner[t, side * (ROWS - 1)] + extra[t]
            hidden[t, side] = value
            if side == 0:
                up[t, 0] = value.astype(BF16)
            else:
                down[t, 1] = value.astype(BF16)
            first, second = sums(value, mask)
            total[0] += first
            total[1] += second
    for t in range(FRAMES):
        up[t, 1] = inner[t, 1].astype(BF16)
        up[t, 2] = inner[t, 2].astype(BF16)
        down[t, 0] = inner[t, ROWS - 2].astype(BF16)
    one, two = (v[:, :C1] + v[:, C1:] for v in total)
    share[...] = jnp.broadcast_to(grouped(one, two), share.shape)


def edges(above, below, corners_above, corners_below, table, inner, stats, devices):
    return pl.pallas_call(
        edges_kernel,
        out_shape=(
            shape((FRAMES, 2, 2 * Q, 2 * C1), F32),
            shape((devices, 128), F32),
            shape((FRAMES, 3, 2 * Q, 2 * C1), BF16),
            shape((FRAMES, 2, 2 * Q, 2 * C1), BF16),
        ),
        in_specs=[VMEM] * 7,
        out_specs=(VMEM,) * 4,
        scratch_shapes=[pltpu.VMEM((2 * FRAMES, LINE, C1), F32)],
        compiler_params=params(12),
        cost_estimate=cost(2e9, 10e6),
        name="edges",
    )(above, below, corners_above, corners_below, table, inner, stats)


def kept(entry_out, edge):
    return 1.0 - jnp.where(entry_out, edge.astype(F32), 0.0)


def activate(values, terms):
    half = values * terms[0] + terms[1]
    return half + half * jnp.tanh(half)


def twice(terms):
    return tuple(jnp.concatenate([v, v], axis=1) for v in terms)


def raised(values):
    return pltpu.roll(values, Q - 1, 0)


def lowered(values):
    return pltpu.roll(values, 1, 0)


def second_kernel(
    inner, outer, above, below, gathered, gain, shift, reduce, second,
    hidden, share, up, down, act, lev, mix, made, *, members,
):
    first_row, last_row, first_col, last_col = position()
    terms = twice(norm_terms(gathered, gain, shift, members))
    entry = lax.broadcasted_iota(jnp.int32, (Q, 1), 0)
    right = kept(entry >= PAD + OWN, last_col)
    outside = right * kept(entry < PAD, first_col)
    below_in = 1.0 - last_row.astype(F32)
    above_in = 1.0 - first_row.astype(F32)

    def line(t, k, value):
        keep = right * below_in if k >= 10 else right
        a = activate(value[:Q].astype(F32), terms) * keep
        b = activate(value[Q:].astype(F32), terms) * keep
        act[t, k, 0:Q, 0 : 2 * C1] = a.astype(BF16)
        act[t, k, 0:Q, 2 * C1 :] = b[:, :C1].astype(BF16)
        act[t, k, Q:, 0 : 2 * C1] = b.astype(BF16)
        act[t, k, Q:, 2 * C1 :] = raised(a[:, :C1]).astype(BF16)

    def lines(t, carry):
        line(t, 0, above[t, 0])
        line(t, 1, above[t, 1])
        line(t, 2, outer[t, 0])
        for r in range(1, ROWS - 1):
            line(t, 2 + r, inner[t, r])
        line(t, 9, outer[t, 1])
        for r in range(3):
            line(t, 10 + r, below[t, r])
        value = None
        for b in range(3):
            left = jnp.concatenate([act[t, 2 * i + b] for i in range(6)], axis=0)
            part = mm(left, reduce[b * 3 * C1 : (b + 1) * 3 * C1, :])
            value = part if value is None else value + part
        for i in range(6):
            keep = outside
            if i == 0:
                keep = keep * above_in
            if i == 5:
                keep = keep * below_in
            even = value[i * 2 * Q : i * 2 * Q + Q] * keep
            odd = value[i * 2 * Q + Q : (i + 1) * 2 * Q] * keep
            e, o = even.astype(BF16), odd.astype(BF16)
            lev[t, i, 0:Q, 0:C2] = lowered(odd).astype(BF16)
            lev[t, i, 0:Q, C2 : 2 * C2] = e
            lev[t, i, 0:Q, 2 * C2 :] = o
            lev[t, i, Q:, 0:C2] = e
            lev[t, i, Q:, C2 : 2 * C2] = o
            lev[t, i, Q:, 2 * C2 :] = raised(even).astype(BF16)
        return carry

    lax.fori_loop(0, FRAMES, lines, 0, unroll=True)

    def add(i, carry):
        at = pl.ds(pl.multiple_of(i * C2, C2), C2)
        k0, k1, k2 = (second[a, at, :].astype(F32) for a in range(3))
        made[0, at, :] = (k0 - k1 + k2).astype(BF16)
        made[1, at, :] = (k0 + k1).astype(BF16)
        made[2, at, :] = (k0 + k1 + k2).astype(BF16)
        return carry

    lax.fori_loop(0, 9, add, 0, unroll=True)
    rows = 4 * 2 * Q
    mask = own_entries(rows, C2)
    total = [jnp.zeros((1, C2), F32), jnp.zeros((1, C2), F32)]

    for i, value in enumerate(mixed([lev[t] for t in range(FRAMES)])):
        mix[i] = value
    tables = {K0: second.at[0], MINUS: made.at[0], K2: second.at[2], PAIR: made.at[1], ALL: made.at[2]}

    def product(v, s):
        left = jnp.concatenate([v[0][v[1], b : b + 4].reshape(rows, 3 * C2) for b in range(3)], axis=1)
        return mm(left, tables[s][...])

    def store(t, value):
        full = value.reshape(4, 2 * Q, C2)
        hidden[t] = full
        up[t] = full[0:3].astype(BF16)
        down[t] = full[2:4].astype(BF16)
        one, two = sums(value, mask)
        total[0] += one
        total[1] += two

    for t, value in enumerate(causal(product, [(lev, t) for t in range(FRAMES)], [(mix, i) for i in range(4)])):
        store(t, value)
    share[...] = jnp.broadcast_to(grouped(*total), share.shape)


def second_level(inner, outer, above, below, gathered, gain, shift, reduce, second, devices):
    return pl.pallas_call(
        functools.partial(second_kernel, members=float(devices * FRAMES * ROWS * COLS * (C1 // GROUPS))),
        out_shape=(
            shape((FRAMES, 4, 2 * Q, C2), F32),
            shape((devices, 128), F32),
            shape((FRAMES, 3, 2 * Q, C2), BF16),
            shape((FRAMES, 2, 2 * Q, C2), BF16),
        ),
        in_specs=[VMEM] * 9,
        out_specs=(VMEM,) * 4,
        scratch_shapes=[
            pltpu.VMEM((FRAMES, 14, 2 * Q, 3 * C1), BF16),
            pltpu.VMEM((FRAMES, 6, 2 * Q, 3 * C2), BF16),
            pltpu.VMEM((4, 6, 2 * Q, 3 * C2), BF16),
            pltpu.VMEM((3, 9 * C2, C2), BF16),
        ],
        compiler_params=params(24),
        cost_estimate=cost(6e9, 12e6),
        name="second",
    )(
        inner, outer, above, below, gathered,
        gain.reshape(1, C1), shift.reshape(1, C1),
        reduce.reshape(9 * C1, C2), second.reshape(3, 9 * C2, C2),
    )


def third_kernel(inner, above, below, gathered, gain, shift, reduce, level, share, act, *, members):
    _, last_row, _, last_col = position()
    terms = norm_terms(gathered, gain, shift, members)
    entry = lax.broadcasted_iota(jnp.int32, (Q, 1), 0)
    right = kept(entry >= PAD + OWN, last_col)
    below_in = 1.0 - last_row.astype(F32)

    def line(t, k, value):
        keep = right * below_in if k >= 6 else right
        even = activate(value[:Q].astype(F32), terms) * keep
        odd = activate(value[Q:].astype(F32), terms) * keep
        act[t, k, :, 0:C2] = even.astype(BF16)
        act[t, k, :, C2 : 2 * C2] = odd.astype(BF16)
        act[t, k, :, 2 * C2 :] = raised(even).astype(BF16)

    def lines(t, carry):
        for r in range(2):
            line(t, r, above[t, r])
        for r in range(4):
            line(t, 2 + r, inner[t, r])
        for r in range(3):
            line(t, 6 + r, below[t, r])
        return carry

    lax.fori_loop(0, FRAMES, lines, 0, unroll=True)
    mask = own_entries(2 * Q, C3)
    total = [jnp.zeros((1, C3), F32), jnp.zeros((1, C3), F32)]
    value = None
    for b in range(3):
        left = jnp.concatenate([act[t, 2 * i + b] for t in range(FRAMES) for i in range(4)], axis=0)
        part = mm(left, reduce[b * 3 * C2 : (b + 1) * 3 * C2, :])
        value = part if value is None else value + part
    rounded = value.astype(BF16)
    level[...] = rounded.reshape(FRAMES, 4, Q, C3)
    wide = rounded.astype(F32)
    for t in range(FRAMES):
        one, two = sums(wide[(4 * t + 1) * Q : (4 * t + 3) * Q], mask)
        total[0] += one
        total[1] += two
    share[...] = jnp.broadcast_to(grouped(*total), share.shape)


def third_level(inner, above, below, gathered, gain, shift, reduce, devices):
    return pl.pallas_call(
        functools.partial(third_kernel, members=float(devices * FRAMES * 4 * 2 * OWN * (C2 // GROUPS))),
        out_shape=(shape((FRAMES, 4, Q, C3), BF16), shape((devices, 128), F32)),
        in_specs=[VMEM] * 7,
        out_specs=(VMEM,) * 2,
        scratch_shapes=[pltpu.VMEM((FRAMES, 10, Q, 3 * C2), BF16)],
        compiler_params=params(12),
        cost_estimate=cost(2e9, 8e6),
        name="third",
    )(inner, above, below, gathered, gain.reshape(1, C2), shift.reshape(1, C2), reduce.reshape(9 * C2, C3))


def last_kernel(level, gathered, gain, shift, table, result, act, *, members):
    first_row, last_row, first_col, last_col = position()
    terms = norm_terms(gathered, gain, shift, members)
    entry = lax.broadcasted_iota(jnp.int32, (Q, 1), 0)
    outside = kept(entry >= PAD + OWN, last_col) * kept(entry < PAD, first_col)
    below_in = 1.0 - last_row.astype(F32)
    above_in = 1.0 - first_row.astype(F32)
    for t in range(FRAMES):
        for i in range(4):
            keep = outside
            if i == 0:
                keep = keep * above_in
            if i == 3:
                keep = keep * below_in
            v = activate(level[t, i].astype(F32), terms) * keep
            act[t, i, :, 0:C3] = lowered(v).astype(BF16)
            act[t, i, :, C3 : 2 * C3] = v.astype(BF16)
            act[t, i, :, 2 * C3 :] = raised(v).astype(BF16)
    value = None
    for b in range(3):
        for e in range(3):
            lanes = slice(e * C3, (e + 1) * C3)
            left = jnp.concatenate([act[t, i + b, :, lanes] for t in range(FRAMES) for i in range(2)], axis=0)
            right = jnp.concatenate([table[a, 3 * b + e] for a in range(3)], axis=0)
            part = lax.dot_general(left, right, (((1,), (1,)), ((), ())), preferred_element_type=F32)
            value = part if value is None else value + part

    def tap(t, a):
        at = 2 * Q * max(t, 0)
        return value[at : at + 2 * Q, a * OUT : (a + 1) * OUT]

    side = jnp.concatenate([tap(t - 2, 0) + tap(t - 1, 1) + tap(t, 2) for t in range(FRAMES)], axis=1).T
    for t in range(FRAMES):
        for i in range(2):
            at = i * Q + PAD
            result[t, i] = side[t * OUT : (t + 1) * OUT, at : at + OWN].astype(BF16)


def last_level(level, gathered, gain, shift, table, devices):
    swapped = jnp.swapaxes(table, 3, 4).reshape(3, 9, OUT, C3)
    out = pl.pallas_call(
        functools.partial(last_kernel, members=float(devices * FRAMES * 2 * OWN * (C3 // GROUPS))),
        out_shape=shape((FRAMES, 2, OUT, OWN), BF16),
        in_specs=[VMEM] * 5,
        out_specs=VMEM,
        scratch_shapes=[pltpu.VMEM((FRAMES, 4, Q, 3 * C3), BF16)],
        compiler_params=params(10),
        cost_estimate=cost(1e9, 4e6),
        name="last",
    )(level, gathered, gain.reshape(1, C3), shift.reshape(1, C3), swapped)
    return jnp.swapaxes(out, 2, 3)


def forward(axis):
    return [(i, (i + 1) % lax.axis_size(axis)) for i in range(lax.axis_size(axis))]


def backward(axis):
    return [((i + 1) % lax.axis_size(axis), i) for i in range(lax.axis_size(axis))]


def from_both(last, first, axis):
    return lax.ppermute(last, axis, forward(axis)), lax.ppermute(first, axis, backward(axis))


def everywhere(share):
    return lax.all_to_all(share, AXES, 0, 0, tiled=True)


def shards(
    features, conv_first, first_reduce_kernel, conv_second, second_reduce_kernel, conv_last,
    gain_first, shift_first, gain_second, shift_second, gain_third, shift_third,
):
    devices = lax.axis_size("rows") * lax.axis_size("cols")
    last, first, bottom, top = cut(features)
    left, right = from_both(last, first, "cols")
    above, below = from_both(bottom, top, "rows")
    table = weights(conv_first)
    planes, top, bottom = planes_of(left, features, right)
    corners_above, corners_below = from_both(bottom, top, "rows")
    inner, stats = middle(planes, table)
    outer, share, up, down = edges(above, below, corners_above, corners_below, table, inner, stats, devices)
    above, below = from_both(down, up, "rows")
    hidden, share, up, down = second_level(
        inner, outer, above, below, everywhere(share), gain_first, shift_first,
        first_reduce_kernel, conv_second, devices,
    )
    above, below = from_both(down, up, "rows")
    level, share = third_level(
        hidden, above, below, everywhere(share), gain_second, shift_second,
        second_reduce_kernel, devices,
    )
    return last_level(level, everywhere(share), gain_third, shift_third, conv_last, devices)


def solution(mesh):
    return jax.shard_map(
        shards,
        mesh=mesh,
        in_specs=(P(None, "rows", "cols", None),) + (P(),) * 11,
        out_specs=P(None, "rows", "cols", None),
        check_vma=False,
    )
```

```python
import functools

import jax
import jax.numpy as jnp
from jax import lax
from jax.experimental import pallas as pl
from jax.experimental.pallas import tpu as pltpu
from jax.sharding import PartitionSpec as P

GROUPS = 32
EPSILON = 1e-6
FRAMES = 4
ROWS = 8
COLS = 160
C1, C2, C3, OUT = 128, 256, 512, 32
Q = 48
PAD = 2
OWN = COLS // 4
EDGE = 16
LINE = 208
K0, MINUS, K2, PAIR, ALL = range(5)
AXES = ("rows", "cols")
F32, BF16 = jnp.float32, jnp.bfloat16
VMEM = pl.BlockSpec(memory_space=pltpu.VMEM)
HBM = pl.BlockSpec(memory_space=pltpu.HBM)


def params(mib):
    return pltpu.CompilerParams(vmem_limit_bytes=mib * 1024 * 1024)


def cost(flops, read):
    return pl.CostEstimate(flops=int(flops), bytes_accessed=int(read), transcendentals=0)


def shape(dims, dtype):
    return jax.ShapeDtypeStruct(dims, dtype)


def mm(left, right):
    return jnp.dot(left, right, preferred_element_type=F32)


def position():
    row, col = lax.axis_index("rows"), lax.axis_index("cols")
    return row == 0, row == lax.axis_size("rows") - 1, col == 0, col == lax.axis_size("cols") - 1


def weights_kernel(first, one):
    zero = jnp.zeros((C1, C1), BF16)
    for b in range(3):
        for e in range(3):
            taps = [first[((a * 3 + b) * 3 + e) * C1 : ((a * 3 + b) * 3 + e + 1) * C1, :] for a in range(3)]
            wide = [k.astype(F32) for k in taps]
            pair, ends = wide[0] + wide[1], wide[0] + wide[2]
            made = [v.astype(BF16) for v in (ends - wide[1], pair, pair + wide[2])]
            for s, k in enumerate([taps[0], made[0], taps[2], made[1], made[2]]):
                base = s * 12 * C1 + b * 4 * C1
                one[base + e * C1 : base + (e + 1) * C1, 0:C1] = k
                one[base + (e + 1) * C1 : base + (e + 2) * C1, C1 : 2 * C1] = k
        for s in range(5):
            base = s * 12 * C1 + b * 4 * C1
            one[base + 3 * C1 : base + 4 * C1, 0:C1] = zero
            one[base : base + C1, C1 : 2 * C1] = zero


def weights(first):
    return pl.pallas_call(
        weights_kernel,
        out_shape=shape((5 * 12 * C1, 2 * C1), BF16),
        in_specs=[VMEM],
        out_specs=VMEM,
        compiler_params=params(8),
        cost_estimate=cost(0, 5e6),
        name="weights",
    )(first.reshape(27 * C1, C1))


def cut_kernel(features, last, first, sem):
    copies = [
        pltpu.make_async_copy(features.at[:, pl.ds(COLS - EDGE, EDGE)], last, sem.at[0]),
        pltpu.make_async_copy(features.at[:, pl.ds(0, EDGE)], first, sem.at[1]),
    ]
    for c in copies:
        c.start()
    for c in copies:
        c.wait()


def cut(features):
    edge = shape((FRAMES * ROWS, EDGE, C1), BF16)
    return pl.pallas_call(
        cut_kernel,
        out_shape=(edge, edge),
        in_specs=[HBM],
        out_specs=(VMEM,) * 2,
        scratch_shapes=[pltpu.SemaphoreType.DMA((2,))],
        compiler_params=params(4),
        cost_estimate=cost(0, 4e5),
        name="cut",
    )(features.reshape(FRAMES * ROWS, COLS, C1))


def planes_kernel(left, own, right, planes, top, bottom, line):
    _, _, first_col, last_col = position()
    left_in = 1.0 - first_col.astype(F32)
    right_in = 1.0 - last_col.astype(F32)
    for t in range(FRAMES):

        def step(r, carry, t=t):
            i = t * ROWS + r
            line[i, 0:EDGE, :] = left[i].astype(F32) * left_in
            line[i, EDGE : EDGE + COLS, :] = own[i].astype(F32)
            line[i, EDGE + COLS : 2 * EDGE + COLS, :] = right[i].astype(F32) * right_in
            line[i, 2 * EDGE + COLS : LINE, :] = jnp.zeros((LINE - 2 * EDGE - COLS, C1), F32)
            for k in range(6):
                planes[t, r, :, k * C1 : (k + 1) * C1] = line[i, pl.ds(7 + k, Q, stride=4), :].astype(BF16)
            return carry

        lax.fori_loop(0, ROWS, step, 0, unroll=True)
        top[t] = planes[t, 0, :, C1 : 5 * C1]
        bottom[t] = planes[t, ROWS - 1, :, C1 : 5 * C1]


def planes_of(left, own, right):
    lines = FRAMES * ROWS
    return pl.pallas_call(
        planes_kernel,
        out_shape=(
            shape((FRAMES, ROWS, Q, 6 * C1), BF16),
            shape((FRAMES, Q, 4 * C1), BF16),
            shape((FRAMES, Q, 4 * C1), BF16),
        ),
        in_specs=[VMEM] * 3,
        out_specs=(VMEM,) * 3,
        scratch_shapes=[pltpu.VMEM((lines, LINE, C1), F32)],
        compiler_params=params(12),
        cost_estimate=cost(0, 4e6),
        name="planes",
    )(left, own.reshape(lines, COLS, C1), right)


def own_entries(rows, lanes):
    at = lax.rem(lax.broadcasted_iota(jnp.int32, (rows, lanes), 0), Q)
    return (at >= PAD) & (at < PAD + OWN)


def sums(values, mask):
    kept = jnp.where(mask, values, 0.0)
    return jnp.sum(kept, axis=0, keepdims=True), jnp.sum(kept * kept, axis=0, keepdims=True)


def mixed(one):
    return one[0] - one[2], one[1] + one[2], one[2] - one[1], one[1] - one[3]


def causal(product, frames, mix):
    yield product(frames[0], ALL)
    yield product(frames[0], PAIR) + product(frames[1], K2)
    plus, minus = product(mix[1], ALL), product(mix[2], MINUS)
    yield product(mix[0], K0) + 0.5 * (plus + minus)
    yield 0.5 * (plus - minus) - product(mix[3], K2)


def middle_kernel(planes, table, hidden, stats, mix):
    mask = own_entries((ROWS - 2) * Q, 2 * C1)
    stats[...] = jnp.zeros(stats.shape, F32)
    for i, value in enumerate(mixed([planes[t] for t in range(FRAMES)])):
        mix[i] = value
    for odd in range(2):
        lanes = slice(2 * C1 * odd, 2 * C1 * odd + 4 * C1)
        at = slice(odd * Q, (odd + 1) * Q)

        def product(v, s):
            def tap(b):
                low, high = max(b - 1, 0), ROWS + min(b - 1, 0)
                left = v[0][v[1], low:high, :, lanes].reshape((high - low) * Q, 4 * C1)
                base = (3 * s + b) * 4 * C1
                return mm(left, table[base : base + 4 * C1, :])

            up, here, down = tap(0), tap(1), tap(2)
            return jnp.concatenate([here[:Q] + down[:Q], here[Q:-Q] + up[:-Q] + down[Q:], here[-Q:] + up[-Q:]], axis=0)

        for t, value in enumerate(causal(product, [(planes, t) for t in range(FRAMES)], [(mix, i) for i in range(4)])):
            hidden[t, :, at, :] = value.reshape(ROWS, Q, 2 * C1)
            one, two = sums(value[Q:-Q], mask)
            stats[0:1, :] += one
            stats[1:2, :] += two


def middle(planes, table):
    return pl.pallas_call(
        middle_kernel,
        out_shape=(
            shape((FRAMES, ROWS, 2 * Q, 2 * C1), F32),
            shape((8, 2 * C1), F32),
        ),
        in_specs=[VMEM] * 2,
        out_specs=(VMEM,) * 2,
        scratch_shapes=[pltpu.VMEM((4, ROWS, Q, 6 * C1), BF16)],
        compiler_params=params(12),
        cost_estimate=cost(6e9, 10e6),
        name="middle",
    )(planes, table)


def group_totals(values, per):
    lane = lax.broadcasted_iota(jnp.int32, (8, 128), 1)
    step = 1
    while step < per:
        other = jnp.where((lane & step) == 0, pltpu.roll(values, 128 - step, 1), pltpu.roll(values, step, 1))
        values = values + other
        step *= 2
    return values


def slots(per):
    lane = lax.broadcasted_iota(jnp.int32, (8, 128), 1)
    return (lane & (per - 1)) == lax.broadcasted_iota(jnp.int32, (8, 128), 0)


def grouped(one, two):
    channels = one.shape[1]
    per = channels // GROUPS
    lines = []
    for low in range(0, channels, 128):
        lines += [one[:, low : low + 128], two[:, low : low + 128]]
    lines += [jnp.zeros((1, 128), F32)] * (8 - len(lines))
    totals = group_totals(jnp.concatenate(lines, axis=0), per)
    return jnp.sum(jnp.where(slots(per), totals, 0.0), axis=0, keepdims=True)


def norm_terms(gathered, gain, shift, members):
    channels = gain.shape[1]
    per = channels // GROUPS
    total = jnp.broadcast_to(jnp.sum(gathered[...], axis=0, keepdims=True), (8, 128))
    lane = lax.broadcasted_iota(jnp.int32, (8, 128), 1)
    source = lane - (lane & (per - 1)) + (lax.broadcasted_iota(jnp.int32, (8, 128), 0) & (per - 1))
    lines = jnp.take_along_axis(total, source, axis=1) / members
    count = channels // 128
    mean = jnp.concatenate([lines[2 * i : 2 * i + 1] for i in range(count)], axis=1)
    square = jnp.concatenate([lines[2 * i + 1 : 2 * i + 2] for i in range(count)], axis=1)
    variance = jnp.maximum(square - mean * mean, 0.0)
    factor = gain[...] / jnp.sqrt(variance + EPSILON)
    return 0.5 * factor, 0.5 * (shift[...] - mean * factor)


def edges_kernel(above, below, table, inner, stats, hidden, share, up, down):
    mask = own_entries(2 * Q, 2 * C1)
    total = [stats[0:1, :], stats[1:2, :]]
    first_row, last_row, _, _ = position()
    for side, (ref, b, end) in enumerate(((above, 0, first_row), (below, 2, last_row))):
        inside = 1.0 - end.astype(F32)
        lines = []
        for t in range(FRAMES):
            wide = ref[t].astype(F32) * inside
            whole = wide.astype(BF16)
            first = pltpu.roll(wide[:, 3 * C1 :], 1, 0).astype(BF16)
            last = pltpu.roll(wide[:, :C1], Q - 1, 0).astype(BF16)
            even = jnp.concatenate([first, whole[:, : 3 * C1]], axis=1)
            odd = jnp.concatenate([whole[:, C1:], last], axis=1)
            lines.append(jnp.concatenate([even, odd], axis=0))

        def product(v, s):
            base = s * 12 * C1 + b * 4 * C1
            return mm(v, table[base : base + 4 * C1, :])

        extra = list(causal(product, lines, mixed(lines)))
        for t in range(FRAMES):
            value = inner[t, side * (ROWS - 1)] + extra[t]
            hidden[t, side] = value
            if side == 0:
                up[t, 0] = value.astype(BF16)
            else:
                down[t, 1] = value.astype(BF16)
            first, second = sums(value, mask)
            total[0] += first
            total[1] += second
    for t in range(FRAMES):
        up[t, 1] = inner[t, 1].astype(BF16)
        up[t, 2] = inner[t, 2].astype(BF16)
        down[t, 0] = inner[t, ROWS - 2].astype(BF16)
    one, two = (v[:, :C1] + v[:, C1:] for v in total)
    share[...] = jnp.broadcast_to(grouped(one, two), share.shape)


def edges(above, below, table, inner, stats, devices):
    return pl.pallas_call(
        edges_kernel,
        out_shape=(
            shape((FRAMES, 2, 2 * Q, 2 * C1), F32),
            shape((devices, 128), F32),
            shape((FRAMES, 3, 2 * Q, 2 * C1), BF16),
            shape((FRAMES, 2, 2 * Q, 2 * C1), BF16),
        ),
        in_specs=[VMEM] * 5,
        out_specs=(VMEM,) * 4,
        compiler_params=params(12),
        cost_estimate=cost(2e9, 10e6),
        name="edges",
    )(above, below, table, inner, stats)


def kept(entry_out, edge):
    return 1.0 - jnp.where(entry_out, edge.astype(F32), 0.0)


def activate(values, terms):
    half = values * terms[0] + terms[1]
    return half + half * jnp.tanh(half)


def twice(terms):
    return tuple(jnp.concatenate([v, v], axis=1) for v in terms)


def raised(values):
    return pltpu.roll(values, Q - 1, 0)


def lowered(values):
    return pltpu.roll(values, 1, 0)


def second_kernel(
    inner, outer, above, below, gathered, gain, shift, reduce, second,
    hidden, share, up, down, act, lev, mix, made, *, members,
):
    first_row, last_row, first_col, last_col = position()
    terms = twice(norm_terms(gathered, gain, shift, members))
    entry = lax.broadcasted_iota(jnp.int32, (Q, 1), 0)
    right = kept(entry >= PAD + OWN, last_col)
    outside = right * kept(entry < PAD, first_col)
    below_in = 1.0 - last_row.astype(F32)
    above_in = 1.0 - first_row.astype(F32)

    def line(t, k, value):
        keep = right * below_in if k >= 10 else right
        a = activate(value[:Q].astype(F32), terms) * keep
        b = activate(value[Q:].astype(F32), terms) * keep
        act[t, k, :, 0 : 2 * C1] = a.astype(BF16)
        act[t, k, :, 2 * C1 : 4 * C1] = b.astype(BF16)
        act[t, k, :, 4 * C1 :] = raised(a[:, :C1]).astype(BF16)

    def lines(t, carry):
        line(t, 0, above[t, 0])
        line(t, 1, above[t, 1])
        line(t, 2, outer[t, 0])
        for r in range(1, ROWS - 1):
            line(t, 2 + r, inner[t, r])
        line(t, 9, outer[t, 1])
        for r in range(3):
            line(t, 10 + r, below[t, r])
        parts = []
        for b in range(3):
            whole = [act[t, 2 * i + b, :, low : low + 3 * C1] for i in range(6) for low in (0, 2 * C1)]
            parts.append(jnp.concatenate(whole, axis=0))
        value = mm(jnp.concatenate(parts, axis=1), reduce[...])
        for i in range(6):
            keep = outside
            if i == 0:
                keep = keep * above_in
            if i == 5:
                keep = keep * below_in
            even = value[i * 2 * Q : i * 2 * Q + Q] * keep
            odd = value[i * 2 * Q + Q : (i + 1) * 2 * Q] * keep
            lev[t, i, :, 0:C2] = lowered(odd).astype(BF16)
            lev[t, i, :, C2 : 2 * C2] = even.astype(BF16)
            lev[t, i, :, 2 * C2 : 3 * C2] = odd.astype(BF16)
            lev[t, i, :, 3 * C2 :] = raised(even).astype(BF16)
        return carry

    lax.fori_loop(0, FRAMES, lines, 0, unroll=True)

    def add(i, carry):
        at = pl.ds(pl.multiple_of(i * C2, C2), C2)
        k0, k1, k2 = (second[a, at, :].astype(F32) for a in range(3))
        made[0, at, :] = (k0 - k1 + k2).astype(BF16)
        made[1, at, :] = (k0 + k1).astype(BF16)
        made[2, at, :] = (k0 + k1 + k2).astype(BF16)
        return carry

    lax.fori_loop(0, 9, add, 0, unroll=True)
    rows = 4 * 2 * Q
    mask = own_entries(rows, C2)
    total = [jnp.zeros((1, C2), F32), jnp.zeros((1, C2), F32)]

    for i, value in enumerate(mixed([lev[t] for t in range(FRAMES)])):
        mix[i] = value
    tables = {K0: second.at[0], MINUS: made.at[0], K2: second.at[2], PAIR: made.at[1], ALL: made.at[2]}

    def product(v, s):
        parts = []
        for b in range(3):
            lines = [v[0][v[1], b + i, :, low : low + 3 * C2] for i in range(4) for low in (0, C2)]
            parts.append(jnp.concatenate(lines, axis=0))
        return mm(jnp.concatenate(parts, axis=1), tables[s][...])

    def store(t, value):
        full = value.reshape(4, 2 * Q, C2)
        hidden[t] = full
        up[t] = full[0:3].astype(BF16)
        down[t] = full[2:4].astype(BF16)
        one, two = sums(value, mask)
        total[0] += one
        total[1] += two

    for t, value in enumerate(causal(product, [(lev, t) for t in range(FRAMES)], [(mix, i) for i in range(4)])):
        store(t, value)
    share[...] = jnp.broadcast_to(grouped(*total), share.shape)


def second_level(inner, outer, above, below, gathered, gain, shift, reduce, second, devices):
    return pl.pallas_call(
        functools.partial(second_kernel, members=float(devices * FRAMES * ROWS * COLS * (C1 // GROUPS))),
        out_shape=(
            shape((FRAMES, 4, 2 * Q, C2), F32),
            shape((devices, 128), F32),
            shape((FRAMES, 3, 2 * Q, C2), BF16),
            shape((FRAMES, 2, 2 * Q, C2), BF16),
        ),
        in_specs=[VMEM] * 9,
        out_specs=(VMEM,) * 4,
        scratch_shapes=[
            pltpu.VMEM((FRAMES, 14, Q, 5 * C1), BF16),
            pltpu.VMEM((FRAMES, 6, Q, 4 * C2), BF16),
            pltpu.VMEM((4, 6, Q, 4 * C2), BF16),
            pltpu.VMEM((3, 9 * C2, C2), BF16),
        ],
        compiler_params=params(24),
        cost_estimate=cost(6e9, 12e6),
        name="second",
    )(
        inner, outer, above, below, gathered,
        gain.reshape(1, C1), shift.reshape(1, C1),
        reduce.reshape(9 * C1, C2), second.reshape(3, 9 * C2, C2),
    )


def third_kernel(inner, above, below, gathered, gain, shift, reduce, level, share, act, *, members):
    _, last_row, _, last_col = position()
    terms = norm_terms(gathered, gain, shift, members)
    entry = lax.broadcasted_iota(jnp.int32, (Q, 1), 0)
    right = kept(entry >= PAD + OWN, last_col)
    below_in = 1.0 - last_row.astype(F32)

    def line(t, k, value):
        keep = right * below_in if k >= 6 else right
        even = activate(value[:Q].astype(F32), terms) * keep
        odd = activate(value[Q:].astype(F32), terms) * keep
        act[t, k, :, 0:C2] = even.astype(BF16)
        act[t, k, :, C2 : 2 * C2] = odd.astype(BF16)
        act[t, k, :, 2 * C2 :] = raised(even).astype(BF16)

    def lines(t, carry):
        for r in range(2):
            line(t, r, above[t, r])
        for r in range(4):
            line(t, 2 + r, inner[t, r])
        for r in range(3):
            line(t, 6 + r, below[t, r])
        return carry

    lax.fori_loop(0, FRAMES, lines, 0, unroll=True)
    mask = own_entries(2 * Q, C3)
    total = [jnp.zeros((1, C3), F32), jnp.zeros((1, C3), F32)]
    value = None
    for b in range(3):
        left = jnp.concatenate([act[t, 2 * i + b] for t in range(FRAMES) for i in range(4)], axis=0)
        part = mm(left, reduce[b * 3 * C2 : (b + 1) * 3 * C2, :])
        value = part if value is None else value + part
    rounded = value.astype(BF16)
    level[...] = rounded.reshape(FRAMES, 4, Q, C3)
    wide = rounded.astype(F32)
    for t in range(FRAMES):
        one, two = sums(wide[(4 * t + 1) * Q : (4 * t + 3) * Q], mask)
        total[0] += one
        total[1] += two
    share[...] = jnp.broadcast_to(grouped(*total), share.shape)


def third_level(inner, above, below, gathered, gain, shift, reduce, devices):
    return pl.pallas_call(
        functools.partial(third_kernel, members=float(devices * FRAMES * 4 * 2 * OWN * (C2 // GROUPS))),
        out_shape=(shape((FRAMES, 4, Q, C3), BF16), shape((devices, 128), F32)),
        in_specs=[VMEM] * 7,
        out_specs=(VMEM,) * 2,
        scratch_shapes=[pltpu.VMEM((FRAMES, 10, Q, 3 * C2), BF16)],
        compiler_params=params(12),
        cost_estimate=cost(2e9, 8e6),
        name="third",
    )(inner, above, below, gathered, gain.reshape(1, C2), shift.reshape(1, C2), reduce.reshape(9 * C2, C3))


def last_kernel(level, gathered, gain, shift, table, result, act, *, members):
    first_row, last_row, first_col, last_col = position()
    terms = norm_terms(gathered, gain, shift, members)
    entry = lax.broadcasted_iota(jnp.int32, (Q, 1), 0)
    outside = kept(entry >= PAD + OWN, last_col) * kept(entry < PAD, first_col)
    below_in = 1.0 - last_row.astype(F32)
    above_in = 1.0 - first_row.astype(F32)
    for t in range(FRAMES):
        for i in range(4):
            keep = outside
            if i == 0:
                keep = keep * above_in
            if i == 3:
                keep = keep * below_in
            v = activate(level[t, i].astype(F32), terms) * keep
            act[t, i, :, 0:C3] = lowered(v).astype(BF16)
            act[t, i, :, C3 : 2 * C3] = v.astype(BF16)
            act[t, i, :, 2 * C3 :] = raised(v).astype(BF16)
    value = None
    for b in range(3):
        for e in range(3):
            lanes = slice(e * C3, (e + 1) * C3)
            left = jnp.concatenate([act[t, i + b, :, lanes] for t in range(FRAMES) for i in range(2)], axis=0)
            right = jnp.concatenate([table[a, 3 * b + e] for a in range(3)], axis=0)
            part = lax.dot_general(left, right, (((1,), (1,)), ((), ())), preferred_element_type=F32)
            value = part if value is None else value + part

    def tap(t, a):
        at = 2 * Q * max(t, 0)
        return value[at : at + 2 * Q, a * OUT : (a + 1) * OUT]

    side = jnp.concatenate([tap(t - 2, 0) + tap(t - 1, 1) + tap(t, 2) for t in range(FRAMES)], axis=1).T
    for t in range(FRAMES):
        for i in range(2):
            at = i * Q + PAD
            result[t, i] = side[t * OUT : (t + 1) * OUT, at : at + OWN].astype(BF16)


def last_level(level, gathered, gain, shift, table, devices):
    swapped = jnp.swapaxes(table, 3, 4).reshape(3, 9, OUT, C3)
    out = pl.pallas_call(
        functools.partial(last_kernel, members=float(devices * FRAMES * 2 * OWN * (C3 // GROUPS))),
        out_shape=shape((FRAMES, 2, OUT, OWN), BF16),
        in_specs=[VMEM] * 5,
        out_specs=VMEM,
        scratch_shapes=[pltpu.VMEM((FRAMES, 4, Q, 3 * C3), BF16)],
        compiler_params=params(10),
        cost_estimate=cost(1e9, 4e6),
        name="last",
    )(level, gathered, gain.reshape(1, C3), shift.reshape(1, C3), swapped)
    return jnp.swapaxes(out, 2, 3)


def forward(axis):
    return [(i, (i + 1) % lax.axis_size(axis)) for i in range(lax.axis_size(axis))]


def backward(axis):
    return [((i + 1) % lax.axis_size(axis), i) for i in range(lax.axis_size(axis))]


def from_both(last, first, axis):
    return lax.ppermute(last, axis, forward(axis)), lax.ppermute(first, axis, backward(axis))


def everywhere(share):
    return lax.all_to_all(share, AXES, 0, 0, tiled=True)


def shards(
    features, conv_first, first_reduce_kernel, conv_second, second_reduce_kernel, conv_last,
    gain_first, shift_first, gain_second, shift_second, gain_third, shift_third,
):
    devices = lax.axis_size("rows") * lax.axis_size("cols")
    left, right = from_both(*cut(features), "cols")
    table = weights(conv_first)
    planes, top, bottom = planes_of(left, features, right)
    above, below = from_both(bottom, top, "rows")
    inner, stats = middle(planes, table)
    outer, share, up, down = edges(above, below, table, inner, stats, devices)
    above, below = from_both(down, up, "rows")
    hidden, share, up, down = second_level(
        inner, outer, above, below, everywhere(share), gain_first, shift_first,
        first_reduce_kernel, conv_second, devices,
    )
    above, below = from_both(down, up, "rows")
    level, share = third_level(
        hidden, above, below, everywhere(share), gain_second, shift_second,
        second_reduce_kernel, devices,
    )
    return last_level(level, everywhere(share), gain_third, shift_third, conv_last, devices)


def solution(mesh):
    return jax.shard_map(
        shards,
        mesh=mesh,
        in_specs=(P(None, "rows", "cols", None),) + (P(),) * 11,
        out_specs=P(None, "rows", "cols", None),
        check_vma=False,
    )
```

```python
import functools

import jax
import jax.numpy as jnp
from jax import lax
from jax.experimental import pallas as pl
from jax.experimental.pallas import tpu as pltpu
from jax.sharding import PartitionSpec as P

GROUPS = 32
EPSILON = 1e-6
FRAMES = 4
ROWS = 8
COLS = 160
C1, C2, C3, OUT = 128, 256, 512, 32
Q = 48
PAD = 2
OWN = COLS // 4
EDGE = 16
LINE = 208
K0, MINUS, K2, PAIR, ALL = range(5)
AXES = ("rows", "cols")
F32, BF16 = jnp.float32, jnp.bfloat16
VMEM = pl.BlockSpec(memory_space=pltpu.VMEM)
HBM = pl.BlockSpec(memory_space=pltpu.HBM)


def params(mib):
    return pltpu.CompilerParams(vmem_limit_bytes=mib * 1024 * 1024)


def cost(flops, read):
    return pl.CostEstimate(flops=int(flops), bytes_accessed=int(read), transcendentals=0)


def shape(dims, dtype):
    return jax.ShapeDtypeStruct(dims, dtype)


def mm(left, right):
    return jnp.dot(left, right, preferred_element_type=F32)


def position():
    row, col = lax.axis_index("rows"), lax.axis_index("cols")
    return row == 0, row == lax.axis_size("rows") - 1, col == 0, col == lax.axis_size("cols") - 1


def weights_kernel(first, one):
    zero = jnp.zeros((C1, C1), BF16)
    for b in range(3):
        for e in range(3):
            taps = [first[((a * 3 + b) * 3 + e) * C1 : ((a * 3 + b) * 3 + e + 1) * C1, :] for a in range(3)]
            wide = [k.astype(F32) for k in taps]
            pair, ends = wide[0] + wide[1], wide[0] + wide[2]
            made = [v.astype(BF16) for v in (ends - wide[1], pair, pair + wide[2])]
            for s, k in enumerate([taps[0], made[0], taps[2], made[1], made[2]]):
                base = s * 12 * C1 + b * 4 * C1
                one[base + e * C1 : base + (e + 1) * C1, 0:C1] = k
                one[base + (e + 1) * C1 : base + (e + 2) * C1, C1 : 2 * C1] = k
        for s in range(5):
            base = s * 12 * C1 + b * 4 * C1
            one[base + 3 * C1 : base + 4 * C1, 0:C1] = zero
            one[base : base + C1, C1 : 2 * C1] = zero


def weights(first):
    return pl.pallas_call(
        weights_kernel,
        out_shape=shape((5 * 12 * C1, 2 * C1), BF16),
        in_specs=[VMEM],
        out_specs=VMEM,
        compiler_params=params(8),
        cost_estimate=cost(0, 5e6),
        name="weights",
    )(first.reshape(27 * C1, C1))


def cut_kernel(features, last, first, sem):
    copies = [
        pltpu.make_async_copy(features.at[:, pl.ds(COLS - EDGE, EDGE)], last, sem.at[0]),
        pltpu.make_async_copy(features.at[:, pl.ds(0, EDGE)], first, sem.at[1]),
    ]
    for c in copies:
        c.start()
    for c in copies:
        c.wait()


def cut(features):
    edge = shape((FRAMES * ROWS, EDGE, C1), BF16)
    return pl.pallas_call(
        cut_kernel,
        out_shape=(edge, edge),
        in_specs=[HBM],
        out_specs=(VMEM,) * 2,
        scratch_shapes=[pltpu.SemaphoreType.DMA((2,))],
        compiler_params=params(4),
        cost_estimate=cost(0, 4e5),
        name="cut",
    )(pltpu.with_memory_space_constraint(features.reshape(FRAMES * ROWS, COLS, C1), pltpu.HBM))


def planes_kernel(left, own, right, planes, top, bottom, line):
    _, _, first_col, last_col = position()
    left_in = 1.0 - first_col.astype(F32)
    right_in = 1.0 - last_col.astype(F32)
    for t in range(FRAMES):

        def step(r, carry, t=t):
            i = t * ROWS + r
            line[i, 0:EDGE, :] = left[i].astype(F32) * left_in
            line[i, EDGE : EDGE + COLS, :] = own[i].astype(F32)
            line[i, EDGE + COLS : 2 * EDGE + COLS, :] = right[i].astype(F32) * right_in
            line[i, 2 * EDGE + COLS : LINE, :] = jnp.zeros((LINE - 2 * EDGE - COLS, C1), F32)
            for k in range(6):
                planes[t, r, :, k * C1 : (k + 1) * C1] = line[i, pl.ds(7 + k, Q, stride=4), :].astype(BF16)
            return carry

        lax.fori_loop(0, ROWS, step, 0, unroll=True)
        top[t] = planes[t, 0, :, C1 : 5 * C1]
        bottom[t] = planes[t, ROWS - 1, :, C1 : 5 * C1]


def planes_of(left, own, right):
    lines = FRAMES * ROWS
    return pl.pallas_call(
        planes_kernel,
        out_shape=(
            shape((FRAMES, ROWS, Q, 6 * C1), BF16),
            shape((FRAMES, Q, 4 * C1), BF16),
            shape((FRAMES, Q, 4 * C1), BF16),
        ),
        in_specs=[VMEM] * 3,
        out_specs=(VMEM,) * 3,
        scratch_shapes=[pltpu.VMEM((lines, LINE, C1), F32)],
        compiler_params=params(12),
        cost_estimate=cost(0, 4e6),
        name="planes",
    )(left, own.reshape(lines, COLS, C1), right)


def own_entries(rows, lanes):
    at = lax.rem(lax.broadcasted_iota(jnp.int32, (rows, lanes), 0), Q)
    return (at >= PAD) & (at < PAD + OWN)


def sums(values, mask):
    kept = jnp.where(mask, values, 0.0)
    return jnp.sum(kept, axis=0, keepdims=True), jnp.sum(kept * kept, axis=0, keepdims=True)


def mixed(one):
    return one[0] - one[2], one[1] + one[2], one[2] - one[1], one[1] - one[3]


def causal(product, frames, mix):
    yield product(frames[0], ALL)
    yield product(frames[0], PAIR) + product(frames[1], K2)
    plus, minus = product(mix[1], ALL), product(mix[2], MINUS)
    yield product(mix[0], K0) + 0.5 * (plus + minus)
    yield 0.5 * (plus - minus) - product(mix[3], K2)


def middle_kernel(planes, table, hidden, stats, mix):
    mask = own_entries((ROWS - 2) * Q, 2 * C1)
    stats[...] = jnp.zeros(stats.shape, F32)
    for i, value in enumerate(mixed([planes[t] for t in range(FRAMES)])):
        mix[i] = value
    for odd in range(2):
        lanes = slice(2 * C1 * odd, 2 * C1 * odd + 4 * C1)
        at = slice(odd * Q, (odd + 1) * Q)

        def product(v, s):
            def tap(b):
                low, high = max(b - 1, 0), ROWS + min(b - 1, 0)
                left = v[0][v[1], low:high, :, lanes].reshape((high - low) * Q, 4 * C1)
                base = (3 * s + b) * 4 * C1
                return mm(left, table[base : base + 4 * C1, :])

            up, here, down = tap(0), tap(1), tap(2)
            return jnp.concatenate([here[:Q] + down[:Q], here[Q:-Q] + up[:-Q] + down[Q:], here[-Q:] + up[-Q:]], axis=0)

        for t, value in enumerate(causal(product, [(planes, t) for t in range(FRAMES)], [(mix, i) for i in range(4)])):
            hidden[t, :, at, :] = value.reshape(ROWS, Q, 2 * C1)
            one, two = sums(value[Q:-Q], mask)
            stats[0:1, :] += one
            stats[1:2, :] += two


def middle(planes, table):
    return pl.pallas_call(
        middle_kernel,
        out_shape=(
            shape((FRAMES, ROWS, 2 * Q, 2 * C1), F32),
            shape((8, 2 * C1), F32),
        ),
        in_specs=[VMEM] * 2,
        out_specs=(VMEM,) * 2,
        scratch_shapes=[pltpu.VMEM((4, ROWS, Q, 6 * C1), BF16)],
        compiler_params=params(12),
        cost_estimate=cost(6e9, 10e6),
        name="middle",
    )(planes, table)


def group_totals(values, per):
    lane = lax.broadcasted_iota(jnp.int32, (8, 128), 1)
    step = 1
    while step < per:
        other = jnp.where((lane & step) == 0, pltpu.roll(values, 128 - step, 1), pltpu.roll(values, step, 1))
        values = values + other
        step *= 2
    return values


def slots(per):
    lane = lax.broadcasted_iota(jnp.int32, (8, 128), 1)
    return (lane & (per - 1)) == lax.broadcasted_iota(jnp.int32, (8, 128), 0)


def grouped(one, two):
    channels = one.shape[1]
    per = channels // GROUPS
    lines = []
    for low in range(0, channels, 128):
        lines += [one[:, low : low + 128], two[:, low : low + 128]]
    lines += [jnp.zeros((1, 128), F32)] * (8 - len(lines))
    totals = group_totals(jnp.concatenate(lines, axis=0), per)
    return jnp.sum(jnp.where(slots(per), totals, 0.0), axis=0, keepdims=True)


def norm_terms(gathered, gain, shift, members):
    channels = gain.shape[1]
    per = channels // GROUPS
    total = jnp.broadcast_to(jnp.sum(gathered[...], axis=0, keepdims=True), (8, 128))
    lane = lax.broadcasted_iota(jnp.int32, (8, 128), 1)
    source = lane - (lane & (per - 1)) + (lax.broadcasted_iota(jnp.int32, (8, 128), 0) & (per - 1))
    lines = jnp.take_along_axis(total, source, axis=1) / members
    count = channels // 128
    mean = jnp.concatenate([lines[2 * i : 2 * i + 1] for i in range(count)], axis=1)
    square = jnp.concatenate([lines[2 * i + 1 : 2 * i + 2] for i in range(count)], axis=1)
    variance = jnp.maximum(square - mean * mean, 0.0)
    factor = gain[...] / jnp.sqrt(variance + EPSILON)
    return 0.5 * factor, 0.5 * (shift[...] - mean * factor)


def edges_kernel(above, below, table, inner, stats, hidden, share, up, down):
    mask = own_entries(2 * Q, 2 * C1)
    total = [stats[0:1, :], stats[1:2, :]]
    first_row, last_row, _, _ = position()
    for side, (ref, b, end) in enumerate(((above, 0, first_row), (below, 2, last_row))):
        inside = 1.0 - end.astype(F32)
        lines = []
        for t in range(FRAMES):
            wide = ref[t].astype(F32) * inside
            whole = wide.astype(BF16)
            first = pltpu.roll(wide[:, 3 * C1 :], 1, 0).astype(BF16)
            last = pltpu.roll(wide[:, :C1], Q - 1, 0).astype(BF16)
            even = jnp.concatenate([first, whole[:, : 3 * C1]], axis=1)
            odd = jnp.concatenate([whole[:, C1:], last], axis=1)
            lines.append(jnp.concatenate([even, odd], axis=0))

        def product(v, s):
            base = s * 12 * C1 + b * 4 * C1
            return mm(v, table[base : base + 4 * C1, :])

        extra = list(causal(product, lines, mixed(lines)))
        for t in range(FRAMES):
            value = inner[t, side * (ROWS - 1)] + extra[t]
            hidden[t, side] = value
            if side == 0:
                up[t, 0] = value.astype(BF16)
            else:
                down[t, 1] = value.astype(BF16)
            first, second = sums(value, mask)
            total[0] += first
            total[1] += second
    for t in range(FRAMES):
        up[t, 1] = inner[t, 1].astype(BF16)
        up[t, 2] = inner[t, 2].astype(BF16)
        down[t, 0] = inner[t, ROWS - 2].astype(BF16)
    one, two = (v[:, :C1] + v[:, C1:] for v in total)
    share[...] = jnp.broadcast_to(grouped(one, two), share.shape)


def edges(above, below, table, inner, stats, devices):
    return pl.pallas_call(
        edges_kernel,
        out_shape=(
            shape((FRAMES, 2, 2 * Q, 2 * C1), F32),
            shape((devices, 128), F32),
            shape((FRAMES, 3, 2 * Q, 2 * C1), BF16),
            shape((FRAMES, 2, 2 * Q, 2 * C1), BF16),
        ),
        in_specs=[VMEM] * 5,
        out_specs=(VMEM,) * 4,
        compiler_params=params(12),
        cost_estimate=cost(2e9, 10e6),
        name="edges",
    )(above, below, table, inner, stats)


def kept(entry_out, edge):
    return 1.0 - jnp.where(entry_out, edge.astype(F32), 0.0)


def activate(values, terms):
    half = values * terms[0] + terms[1]
    return half + half * jnp.tanh(half)


def twice(terms):
    return tuple(jnp.concatenate([v, v], axis=1) for v in terms)


def raised(values):
    return pltpu.roll(values, Q - 1, 0)


def lowered(values):
    return pltpu.roll(values, 1, 0)


def second_kernel(
    inner, outer, above, below, gathered, gain, shift, reduce, second,
    hidden, share, up, down, act, lev, mix, made, *, members,
):
    first_row, last_row, first_col, last_col = position()
    terms = twice(norm_terms(gathered, gain, shift, members))
    entry = lax.broadcasted_iota(jnp.int32, (Q, 1), 0)
    right = kept(entry >= PAD + OWN, last_col)
    outside = right * kept(entry < PAD, first_col)
    below_in = 1.0 - last_row.astype(F32)
    above_in = 1.0 - first_row.astype(F32)

    def line(t, k, value):
        keep = right * below_in if k >= 10 else right
        a = activate(value[:Q].astype(F32), terms) * keep
        b = activate(value[Q:].astype(F32), terms) * keep
        act[t, k, :, 0 : 2 * C1] = a.astype(BF16)
        act[t, k, :, 2 * C1 : 4 * C1] = b.astype(BF16)
        act[t, k, :, 4 * C1 :] = raised(a[:, :C1]).astype(BF16)

    def lines(t, carry):
        line(t, 0, above[t, 0])
        line(t, 1, above[t, 1])
        line(t, 2, outer[t, 0])
        for r in range(1, ROWS - 1):
            line(t, 2 + r, inner[t, r])
        line(t, 9, outer[t, 1])
        for r in range(3):
            line(t, 10 + r, below[t, r])
        parts = []
        for b in range(3):
            whole = [act[t, 2 * i + b, :, low : low + 3 * C1] for i in range(6) for low in (0, 2 * C1)]
            parts.append(jnp.concatenate(whole, axis=0))
        value = mm(jnp.concatenate(parts, axis=1), reduce[...])
        for i in range(6):
            keep = outside
            if i == 0:
                keep = keep * above_in
            if i == 5:
                keep = keep * below_in
            even = value[i * 2 * Q : i * 2 * Q + Q] * keep
            odd = value[i * 2 * Q + Q : (i + 1) * 2 * Q] * keep
            lev[t, i, :, 0:C2] = lowered(odd).astype(BF16)
            lev[t, i, :, C2 : 2 * C2] = even.astype(BF16)
            lev[t, i, :, 2 * C2 : 3 * C2] = odd.astype(BF16)
            lev[t, i, :, 3 * C2 :] = raised(even).astype(BF16)
        return carry

    lax.fori_loop(0, FRAMES, lines, 0, unroll=True)

    def add(i, carry):
        at = pl.ds(pl.multiple_of(i * C2, C2), C2)
        k0, k1, k2 = (second[a, at, :].astype(F32) for a in range(3))
        made[0, at, :] = (k0 - k1 + k2).astype(BF16)
        made[1, at, :] = (k0 + k1).astype(BF16)
        made[2, at, :] = (k0 + k1 + k2).astype(BF16)
        return carry

    lax.fori_loop(0, 9, add, 0, unroll=True)
    rows = 4 * 2 * Q
    mask = own_entries(rows, C2)
    total = [jnp.zeros((1, C2), F32), jnp.zeros((1, C2), F32)]

    for i, value in enumerate(mixed([lev[t] for t in range(FRAMES)])):
        mix[i] = value
    tables = {K0: second.at[0], MINUS: made.at[0], K2: second.at[2], PAIR: made.at[1], ALL: made.at[2]}

    def product(v, s):
        parts = []
        for b in range(3):
            lines = [v[0][v[1], b + i, :, low : low + 3 * C2] for i in range(4) for low in (0, C2)]
            parts.append(jnp.concatenate(lines, axis=0))
        return mm(jnp.concatenate(parts, axis=1), tables[s][...])

    def store(t, value):
        full = value.reshape(4, 2 * Q, C2)
        hidden[t] = full
        up[t] = full[0:3].astype(BF16)
        down[t] = full[2:4].astype(BF16)
        one, two = sums(value, mask)
        total[0] += one
        total[1] += two

    for t, value in enumerate(causal(product, [(lev, t) for t in range(FRAMES)], [(mix, i) for i in range(4)])):
        store(t, value)
    share[...] = jnp.broadcast_to(grouped(*total), share.shape)


def second_level(inner, outer, above, below, gathered, gain, shift, reduce, second, devices):
    return pl.pallas_call(
        functools.partial(second_kernel, members=float(devices * FRAMES * ROWS * COLS * (C1 // GROUPS))),
        out_shape=(
            shape((FRAMES, 4, 2 * Q, C2), F32),
            shape((devices, 128), F32),
            shape((FRAMES, 3, 2 * Q, C2), BF16),
            shape((FRAMES, 2, 2 * Q, C2), BF16),
        ),
        in_specs=[VMEM] * 9,
        out_specs=(VMEM,) * 4,
        scratch_shapes=[
            pltpu.VMEM((FRAMES, 14, Q, 5 * C1), BF16),
            pltpu.VMEM((FRAMES, 6, Q, 4 * C2), BF16),
            pltpu.VMEM((4, 6, Q, 4 * C2), BF16),
            pltpu.VMEM((3, 9 * C2, C2), BF16),
        ],
        compiler_params=params(24),
        cost_estimate=cost(6e9, 12e6),
        name="second",
    )(
        inner, outer, above, below, gathered,
        gain.reshape(1, C1), shift.reshape(1, C1),
        reduce.reshape(9 * C1, C2), second.reshape(3, 9 * C2, C2),
    )


def third_kernel(inner, above, below, gathered, gain, shift, reduce, level, share, act, *, members):
    _, last_row, _, last_col = position()
    terms = norm_terms(gathered, gain, shift, members)
    entry = lax.broadcasted_iota(jnp.int32, (Q, 1), 0)
    right = kept(entry >= PAD + OWN, last_col)
    below_in = 1.0 - last_row.astype(F32)

    def line(t, k, value):
        keep = right * below_in if k >= 6 else right
        even = activate(value[:Q].astype(F32), terms) * keep
        odd = activate(value[Q:].astype(F32), terms) * keep
        act[t, k, :, 0:C2] = even.astype(BF16)
        act[t, k, :, C2 : 2 * C2] = odd.astype(BF16)
        act[t, k, :, 2 * C2 :] = raised(even).astype(BF16)

    def lines(t, carry):
        for r in range(2):
            line(t, r, above[t, r])
        for r in range(4):
            line(t, 2 + r, inner[t, r])
        for r in range(3):
            line(t, 6 + r, below[t, r])
        return carry

    lax.fori_loop(0, FRAMES, lines, 0, unroll=True)
    mask = own_entries(2 * Q, C3)
    total = [jnp.zeros((1, C3), F32), jnp.zeros((1, C3), F32)]
    value = None
    for b in range(3):
        left = jnp.concatenate([act[t, 2 * i + b] for t in range(FRAMES) for i in range(4)], axis=0)
        part = mm(left, reduce[b * 3 * C2 : (b + 1) * 3 * C2, :])
        value = part if value is None else value + part
    rounded = value.astype(BF16)
    level[...] = rounded.reshape(FRAMES, 4, Q, C3)
    wide = rounded.astype(F32)
    for t in range(FRAMES):
        one, two = sums(wide[(4 * t + 1) * Q : (4 * t + 3) * Q], mask)
        total[0] += one
        total[1] += two
    share[...] = jnp.broadcast_to(grouped(*total), share.shape)


def third_level(inner, above, below, gathered, gain, shift, reduce, devices):
    return pl.pallas_call(
        functools.partial(third_kernel, members=float(devices * FRAMES * 4 * 2 * OWN * (C2 // GROUPS))),
        out_shape=(shape((FRAMES, 4, Q, C3), BF16), shape((devices, 128), F32)),
        in_specs=[VMEM] * 7,
        out_specs=(VMEM,) * 2,
        scratch_shapes=[pltpu.VMEM((FRAMES, 10, Q, 3 * C2), BF16)],
        compiler_params=params(12),
        cost_estimate=cost(2e9, 8e6),
        name="third",
    )(inner, above, below, gathered, gain.reshape(1, C2), shift.reshape(1, C2), reduce.reshape(9 * C2, C3))


def last_kernel(level, gathered, gain, shift, table, result, act, *, members):
    first_row, last_row, first_col, last_col = position()
    terms = norm_terms(gathered, gain, shift, members)
    entry = lax.broadcasted_iota(jnp.int32, (Q, 1), 0)
    outside = kept(entry >= PAD + OWN, last_col) * kept(entry < PAD, first_col)
    below_in = 1.0 - last_row.astype(F32)
    above_in = 1.0 - first_row.astype(F32)
    for t in range(FRAMES):
        for i in range(4):
            keep = outside
            if i == 0:
                keep = keep * above_in
            if i == 3:
                keep = keep * below_in
            v = activate(level[t, i].astype(F32), terms) * keep
            act[t, i, :, 0:C3] = lowered(v).astype(BF16)
            act[t, i, :, C3 : 2 * C3] = v.astype(BF16)
            act[t, i, :, 2 * C3 :] = raised(v).astype(BF16)
    value = None
    for b in range(3):
        for e in range(3):
            lanes = slice(e * C3, (e + 1) * C3)
            left = jnp.concatenate([act[t, i + b, :, lanes] for t in range(FRAMES) for i in range(2)], axis=0)
            right = jnp.concatenate([table[a, 3 * b + e] for a in range(3)], axis=0)
            part = lax.dot_general(left, right, (((1,), (1,)), ((), ())), preferred_element_type=F32)
            value = part if value is None else value + part

    def tap(t, a):
        at = 2 * Q * max(t, 0)
        return value[at : at + 2 * Q, a * OUT : (a + 1) * OUT]

    side = jnp.concatenate([tap(t - 2, 0) + tap(t - 1, 1) + tap(t, 2) for t in range(FRAMES)], axis=1).T
    for t in range(FRAMES):
        for i in range(2):
            at = i * Q + PAD
            result[t, i] = side[t * OUT : (t + 1) * OUT, at : at + OWN].astype(BF16)


def last_level(level, gathered, gain, shift, table, devices):
    swapped = jnp.swapaxes(table, 3, 4).reshape(3, 9, OUT, C3)
    out = pl.pallas_call(
        functools.partial(last_kernel, members=float(devices * FRAMES * 2 * OWN * (C3 // GROUPS))),
        out_shape=shape((FRAMES, 2, OUT, OWN), BF16),
        in_specs=[VMEM] * 5,
        out_specs=VMEM,
        scratch_shapes=[pltpu.VMEM((FRAMES, 4, Q, 3 * C3), BF16)],
        compiler_params=params(10),
        cost_estimate=cost(1e9, 4e6),
        name="last",
    )(level, gathered, gain.reshape(1, C3), shift.reshape(1, C3), swapped)
    return jnp.swapaxes(out, 2, 3)


def forward(axis):
    return [(i, (i + 1) % lax.axis_size(axis)) for i in range(lax.axis_size(axis))]


def backward(axis):
    return [((i + 1) % lax.axis_size(axis), i) for i in range(lax.axis_size(axis))]


def from_both(last, first, axis):
    return lax.ppermute(last, axis, forward(axis)), lax.ppermute(first, axis, backward(axis))


def everywhere(share):
    return lax.all_to_all(share, AXES, 0, 0, tiled=True)


def shards(
    features, conv_first, first_reduce_kernel, conv_second, second_reduce_kernel, conv_last,
    gain_first, shift_first, gain_second, shift_second, gain_third, shift_third,
):
    devices = lax.axis_size("rows") * lax.axis_size("cols")
    left, right = from_both(*cut(features), "cols")
    table = weights(conv_first)
    planes, top, bottom = planes_of(left, features, right)
    above, below = from_both(bottom, top, "rows")
    inner, stats = middle(planes, table)
    outer, share, up, down = edges(above, below, table, inner, stats, devices)
    above, below = from_both(down, up, "rows")
    hidden, share, up, down = second_level(
        inner, outer, above, below, everywhere(share), gain_first, shift_first,
        first_reduce_kernel, conv_second, devices,
    )
    above, below = from_both(down, up, "rows")
    level, share = third_level(
        hidden, above, below, everywhere(share), gain_second, shift_second,
        second_reduce_kernel, devices,
    )
    return last_level(level, everywhere(share), gain_third, shift_third, conv_last, devices)


def solution(mesh):
    return jax.shard_map(
        shards,
        mesh=mesh,
        in_specs=(P(None, "rows", "cols", None),) + (P(),) * 11,
        out_specs=P(None, "rows", "cols", None),
        check_vma=False,
    )
```
